32 devices in a mesh: section: 2 (over core), dp: 4 (over z), ctx: 4 (over y, x).
Axes of the slice: x: 2, y: 2, z: 4, core: 2. Of those that a mesh axis runs over, the one named last changes fastest.
Arguments:
- token_ids: int32 [2, 4, 1024], P(None, None, 'ctx'), may hold values from 0 to 49151
- doc_lengths: int32 [2, 4, 4], P(None, 'dp'), may hold values from 1 to 896, 1024 in all within a row
- picks: int32 [2, 4, 64], P(None, 'dp', 'ctx'), may hold values from -1 to 255, as said below
- targets: int32 [2, 4, 64], P(None, None, 'ctx'), may hold values from -1 to 49151, as said below
- table: float32 [49152, 768], P('dp')
- table_rows: float32 [49152], P('dp'), may hold values from 0.0020833334 to 0.008333334
- table_cols: float32 [768], replicated, may hold values from 0.0020833334 to 0.008333334
- attention_in: float32 [2, 768, 896], P('section', ('dp', 'ctx')), may hold values from -0.21875 to 0.21875
- attention_in_rows: float32 [2, 768], P('section', ('dp', 'ctx')), may hold values from 0.01536 to 0.06144
- attention_in_cols: float32 [2, 896], P('section'), may hold values from 0.01536 to 0.06144
- attention_out: float32 [2, 768, 768], P('section', ('dp', 'ctx')), may hold values from -0.875 to 0.875
- attention_out_rows: float32 [2, 768], P('section', ('dp', 'ctx')), may hold values from 0.01536 to 0.06144
- attention_out_cols: float32 [2, 768], P('section'), may hold values from 0.01536 to 0.06144
- hidden_in: float32 [2, 768, 3072], P('section', ('dp', 'ctx')), may hold values from -0.21875 to 0.21875
- hidden_in_rows: float32 [2, 768], P('section', ('dp', 'ctx')), may hold values from 0.01536 to 0.06144
- hidden_in_cols: float32 [2, 3072], P('section'), may hold values from 0.01536 to 0.06144
- hidden_out: float32 [2, 3072, 768], P('section', ('dp', 'ctx')), may hold values from -0.109375 to 0.109375
- hidden_out_rows: float32 [2, 3072], P('section', ('dp', 'ctx')), may hold values from 0.01536 to 0.06144
- hidden_out_cols: float32 [2, 768], P('section'), may hold values from 0.01536 to 0.06144
- gains: float32 [2, 4, 768], P('section', None, ('dp', 'ctx'))
- gains_stat: float32 [2, 4, 768], P('section', None, ('dp', 'ctx')), may hold values from 0.2048 to 0.8192
Outputs:
- loss_sum: float32 [], replicated
- loss_count: float32 [], replicated
- table_grad: float32 [49152, 768], P('dp')
- table_rows_new: float32 [49152], P('dp')
- table_cols_new: float32 [768], replicated
- table_new: float32 [49152, 768], P('dp')
- attention_in_grad: float32 [2, 768, 896], P('section', ('dp', 'ctx'))
- attention_in_rows_new: float32 [2, 768], P('section', ('dp', 'ctx'))
- attention_in_cols_new: float32 [2, 896], P('section')
- attention_in_new: float32 [2, 768, 896], P('section', ('dp', 'ctx'))
- attention_out_grad: float32 [2, 768, 768], P('section', ('dp', 'ctx'))
- attention_out_rows_new: float32 [2, 768], P('section', ('dp', 'ctx'))
- attention_out_cols_new: float32 [2, 768], P('section')
- attention_out_new: float32 [2, 768, 768], P('section', ('dp', 'ctx'))
- hidden_in_grad: float32 [2, 768, 3072], P('section', ('dp', 'ctx'))
- hidden_in_rows_new: float32 [2, 768], P('section', ('dp', 'ctx'))
- hidden_in_cols_new: float32 [2, 3072], P('section')
- hidden_in_new: float32 [2, 768, 3072], P('section', ('dp', 'ctx'))
- hidden_out_grad: float32 [2, 3072, 768], P('section', ('dp', 'ctx'))
- hidden_out_rows_new: float32 [2, 3072], P('section', ('dp', 'ctx'))
- hidden_out_cols_new: float32 [2, 768], P('section')
- hidden_out_new: float32 [2, 3072, 768], P('section', ('dp', 'ctx'))
- gains_grad: float32 [2, 4, 768], P('section', None, ('dp', 'ctx'))
- gains_stat_new: float32 [2, 4, 768], P('section', None, ('dp', 'ctx'))
- gains_new: float32 [2, 4, 768], P('section', None, ('dp', 'ctx'))
The draws below stay inside these ranges and needn't reach their ends.
Inputs may be any that keep to these rules, and one draw needn't show every extreme that they name: `picks`: within each block of 16 slots (one sequence's positions on one device) the live slots come first, there is at least one, and their positions are distinct positions of that block; in every micro-batch the block of the last sequence on the last ctx device is full. `targets`: -1 exactly where picks is -1.
All inputs are finite; a program needn't handle non-finite values.
Results may differ from the reference program's by a relative error of at most 0.017.
The reference program's roundings to bfloat16 on the way count: a program that leaves them out, or rounds other values in their place, can miss the bound.
Values may be sent and summed in bfloat16 or wider, within the bound.
No kernel may reach another device: no remote copies, remote signals or barrier semaphores. Data moves between devices by JAX's collectives and lax.ppermute only.
A program may use at most 384 MiB of HBM per device.

```python
import math
import jax
import jax.numpy as jnp
import numpy as np
from jax import lax

D = 768
HEADS = 12
HD = 64
FF = 3072
VOCAB = 49152
CTX_TOK = 256
PICK = 16
WINDOW = 512
MICRO = 2
DOCS = 4
STEP = 10
SEQ = 1024
SEQS = 4
LAYERS = 2
BLOCK = 512
N_CTX = 4


def completion(key):
    key = jax.random.fold_in(key, 5)
    key_jitter, key_places, key_tokens = jax.random.split(key, 3)
    blocks = SEQS * N_CTX
    ranking = jnp.arange(blocks, dtype=jnp.int32)
    rising = PICK // 3 + (PICK - PICK // 3) * (ranking + 1) // blocks
    jitter = jax.random.randint(key_jitter, (MICRO, blocks), 0, 2)
    counts = jnp.where(ranking[None, :] == blocks - 1, PICK, jnp.maximum(rising[None, :] - jitter, 1))
    place_keys = jax.random.split(key_places, MICRO * blocks)

    def choose(single):
        return jax.random.permutation(single, CTX_TOK)[:PICK]
    places = jax.vmap(choose)(place_keys).reshape(MICRO, blocks, PICK).astype(jnp.int32)
    slots = jnp.arange(PICK, dtype=jnp.int32)
    live = slots[None, None, :] < counts[:, :, None]
    chosen = jnp.where(live, places, -1)
    tokens = jax.random.randint(key_tokens, (MICRO, blocks, PICK), 0, VOCAB)
    wanted = jnp.where(live, tokens, -1)
    return (chosen.reshape(MICRO, SEQS, N_CTX * PICK), wanted.reshape(MICRO, SEQS, N_CTX * PICK))


def draw_picks(key, part):
    return completion(key)[0]


def draw_targets(key, part):
    return completion(key)[1]


def draw_table(key, part):
    key = jax.random.fold_in(key, 11)
    ranking = jnp.arange(VOCAB, dtype=jnp.float32)[:, None] / VOCAB
    base = jax.random.normal(key, (VOCAB, D), jnp.float32)
    rising = 1.0 + 2.0 * ranking
    return 0.025 * base * rising


def draw_gains(key, part):
    key = jax.random.fold_in(key, 12)
    key_gain, key_shift = jax.random.split(key)
    along = jnp.arange(D, dtype=jnp.float32)[None, None, :] / D
    kinds = jnp.arange(4, dtype=jnp.int32)[None, :, None] % 2
    shape = (LAYERS, 4, D)
    factor = jax.random.uniform(key_gain, shape, jnp.float32, 0.8, 1.2)
    shift = 0.2 * jax.random.normal(key_shift, shape, jnp.float32)
    return jnp.where(kinds == 0, (0.5 + along) * factor, shift)


def touch_ends(array, rng, smallest, largest):
    longest = array.shape.index(max(array.shape))
    spots = []
    for shift in (0, 1):
        where = [jax.random.randint(jax.random.fold_in(rng, axis), (), 0, length) for axis, length in enumerate(array.shape)]
        where[longest] = (where[longest] + shift) % array.shape[longest]
        spots.append(tuple(where))
    return array.at[spots[0]].set(smallest).at[spots[1]].set(largest)


def block_levels(rng, dims, pieces, smallest, top_value):
    level = 1.0
    for axis_at, blocks in pieces:
        draws = jax.random.uniform(jax.random.fold_in(jax.random.fold_in(rng, 6), axis_at), (blocks,), jnp.float32, smallest / len(pieces), top_value / len(pieces))
        level = level * jnp.repeat(jnp.exp(draws), dims[axis_at] // blocks).reshape((-1,) + (1,) * (len(dims) - 1 - axis_at))
    return level


def rank_bounds(count, lean):
    weights = [(1 << 20) // math.isqrt(standing ** lean) + 1 for standing in range(1, count + 1)]
    scale = 1 + sum(weights) // (1 << 30)
    return np.cumsum(np.array([max(1, weight // scale) for weight in weights]))


def ranked(rng, dims, number_of, skew):
    table = rank_bounds(number_of, skew)
    pick = jax.random.randint(jax.random.fold_in(rng, 1), dims, 0, int(table[number_of - 1]))
    standing = jnp.searchsorted(jnp.asarray(table, jnp.int32), pick, side="right")
    return jax.random.permutation(jax.random.fold_in(rng, 2), number_of)[standing].astype(jnp.int32)


def profile(count, total, limit, lean):
    weights = [(1 << 20) // math.isqrt(rank ** lean) + 1 for rank in range(2, count + 1)]
    rest, given = total - limit - (count - 1), [1] * (count - 1)
    while rest > 0:
        movable = [i for i in range(count - 1) if given[i] < limit]
        mass, left = sum([weights[i] for i in movable]), rest
        for i in movable:
            extra = min(limit - given[i], max(1, left * weights[i] // mass), rest)
            given[i] = given[i] + extra
            rest = rest - extra
    return np.array([limit] + given)


def uneven(own_key, amount, total, bound, lean):
    if amount == 2:
        one = jax.random.randint(own_key, (), max(1, total - bound), min(bound, total - 1) + 1)
        return jnp.stack([one, total - one])
    sizes = jnp.asarray(profile(amount, total, bound, lean), jnp.int32)
    twos = (amount - 1) // 2
    giver, sink = sizes[1:1 + 2 * twos:2], sizes[2:2 + 2 * twos:2]
    room = jnp.minimum(giver - 1, bound - sink)
    shifted = jax.random.randint(jax.random.fold_in(own_key, 1), (twos,), 0, 1 << 20) % (room + 1)
    sizes = sizes.at[1:1 + 2 * twos:2].set(giver - shifted).at[2:2 + 2 * twos:2].set(sink + shifted)
    return sizes[jax.random.permutation(jax.random.fold_in(own_key, 2), amount)]


def bell_draw(rng, shape, width, most, pieces=(), held_as=jnp.bfloat16):
    values = jax.random.normal(rng, shape, jnp.float32) * width
    if len(pieces) > 0:
        values = block_levels(rng, shape, pieces, -0.22, 0.18) * values
    return jnp.clip(values, min=-most, max=most).astype(held_as)


def setup_inputs(seed: int = 0) -> dict:
    arg_keys = jax.random.split(jax.random.key(seed), 22)
    token_ids = touch_ends(ranked(arg_keys[0], (MICRO, SEQS, SEQ), VOCAB, 2), jax.random.fold_in(arg_keys[0], 3), 0, VOCAB - 1).astype(jnp.int32)
    doc_lengths = jax.vmap(lambda own: uneven(own, DOCS, CTX_TOK * N_CTX, CTX_TOK * N_CTX - CTX_TOK * N_CTX // 8, 2))(jax.random.split(arg_keys[1], MICRO * SEQS)).reshape((MICRO, SEQS, DOCS)).astype(jnp.int32)
    picks = draw_picks(jax.random.fold_in(arg_keys[21], 71), 0)
    targets = draw_targets(jax.random.fold_in(arg_keys[21], 71), 0)
    table = draw_table(jax.random.fold_in(arg_keys[21], 71), 0)
    table_rows = jnp.clip(jnp.exp(math.log(0.008333334) - 1.3862944 * jax.random.uniform(arg_keys[5], (VOCAB,), jnp.float32) ** block_levels(arg_keys[5], (VOCAB,), ((0, 4),), -0.2, 0.2)), 0.0020833334, 0.008333334)
    table_cols = jnp.clip(jnp.exp(jax.random.uniform(arg_keys[6], (D,), jnp.float32, math.log(0.0020833334), math.log(0.008333334))), 0.0020833334, 0.008333334)
    attention_in = bell_draw(arg_keys[7], (LAYERS, D, D + 2 * HD), D ** -0.5, 0.21875, ((0, 2), (1, 16)), jnp.float32)
    attention_in_rows = jnp.clip(jnp.exp(math.log(0.06144) - 1.3862944 * jax.random.uniform(arg_keys[8], (LAYERS, D), jnp.float32) ** block_levels(arg_keys[8], (LAYERS, D), ((0, 2), (1, 16)), -0.2, 0.2)), 0.01536, 0.06144)
    attention_in_cols = jnp.clip(jnp.exp(math.log(0.06144) - 1.3862944 * jax.random.uniform(arg_keys[9], (LAYERS, D + 2 * HD), jnp.float32) ** block_levels(arg_keys[9], (LAYERS, D + 2 * HD), ((0, 2),), -0.2, 0.2)), 0.01536, 0.06144)
    attention_out = bell_draw(arg_keys[10], (LAYERS, D, D), (D // 16) ** -0.5, 0.875, ((0, 2), (1, 16)), jnp.float32)
    attention_out_rows = jnp.clip(jnp.exp(math.log(0.06144) - 1.3862944 * jax.random.uniform(arg_keys[11], (LAYERS, D), jnp.float32) ** block_levels(arg_keys[11], (LAYERS, D), ((0, 2), (1, 16)), -0.2, 0.2)), 0.01536, 0.06144)
    attention_out_cols = jnp.clip(jnp.exp(math.log(0.06144) - 1.3862944 * jax.random.uniform(arg_keys[12], (LAYERS, D), jnp.float32) ** block_levels(arg_keys[12], (LAYERS, D), ((0, 2),), -0.2, 0.2)), 0.01536, 0.06144)
    hidden_in = bell_draw(arg_keys[13], (LAYERS, D, FF), D ** -0.5, 0.21875, ((0, 2), (1, 16)), jnp.float32)
    hidden_in_rows = jnp.clip(jnp.exp(math.log(0.06144) - 1.3862944 * jax.random.uniform(arg_keys[14], (LAYERS, D), jnp.float32) ** block_levels(arg_keys[14], (LAYERS, D), ((0, 2), (1, 16)), -0.2, 0.2)), 0.01536, 0.06144)
    hidden_in_cols = jnp.clip(jnp.exp(math.log(0.06144) - 1.3862944 * jax.random.uniform(arg_keys[15], (LAYERS, FF), jnp.float32) ** block_levels(arg_keys[15], (LAYERS, FF), ((0, 2),), -0.2, 0.2)), 0.01536, 0.06144)
    hidden_out = bell_draw(arg_keys[16], (LAYERS, FF, D), FF ** -0.5, 0.109375, ((0, 2), (1, 16)), jnp.float32)
    hidden_out_rows = jnp.clip(jnp.exp(math.log(0.06144) - 1.3862944 * jax.random.uniform(arg_keys[17], (LAYERS, FF), jnp.float32) ** block_levels(arg_keys[17], (LAYERS, FF), ((0, 2), (1, 16)), -0.2, 0.2)), 0.01536, 0.06144)
    hidden_out_cols = jnp.clip(jnp.exp(math.log(0.06144) - 1.3862944 * jax.random.uniform(arg_keys[18], (LAYERS, D), jnp.float32) ** block_levels(arg_keys[18], (LAYERS, D), ((0, 2),), -0.2, 0.2)), 0.01536, 0.06144)
    gains = draw_gains(jax.random.fold_in(arg_keys[21], 71), 0)
    gains_stat = jnp.clip(jnp.exp(math.log(0.8192) - 1.3862944 * jax.random.uniform(arg_keys[20], (LAYERS, 4, D), jnp.float32) ** block_levels(arg_keys[20], (LAYERS, 4, D), ((0, 2), (2, 16)), -0.2, 0.2)), 0.2048, 0.8192)
    return {"token_ids": token_ids, "doc_lengths": doc_lengths, "picks": picks, "targets": targets, "table": table, "table_rows": table_rows, "table_cols": table_cols, "attention_in": attention_in, "attention_in_rows": attention_in_rows, "attention_in_cols": attention_in_cols, "attention_out": attention_out, "attention_out_rows": attention_out_rows, "attention_out_cols": attention_out_cols, "hidden_in": hidden_in, "hidden_in_rows": hidden_in_rows, "hidden_in_cols": hidden_in_cols, "hidden_out": hidden_out, "hidden_out_rows": hidden_out_rows, "hidden_out_cols": hidden_out_cols, "gains": gains, "gains_stat": gains_stat}


@jax.custom_vjp
def low(v):
    return lax.optimization_barrier(v.astype(jnp.bfloat16)).astype(jnp.float32)

@jax.custom_vjp
def low_back(v):
    return v

def low_keep(v):
    return (low(v), None)

def low_pass(kept, grad):
    return (grad,)

def back_keep(v):
    return (v, None)

def back_low(kept, grad):
    return (low(grad),)
low.defvjp(low_keep, low_pass)
low_back.defvjp(back_keep, back_low)
HIGHEST = lax.Precision.HIGHEST
NORM_EPS = 1e-05
SQUARE_EPS = 1e-30
SCALE_FLOOR = 0.001
RELATIVE_RATE = 0.5
MASKED = -1e+30

def matmul(left, right):
    return jnp.dot(left, right, precision=HIGHEST, preferred_element_type=jnp.float32)

def layer_norm(values, gain, shift):
    center = values - lax.optimization_barrier(jnp.mean(values, -1, keepdims=True))
    spread = lax.optimization_barrier(jnp.mean(center * center, -1, keepdims=True))
    return center * lax.rsqrt(spread + NORM_EPS) * gain + shift

def doc_numbers(lengths):
    bounds = jnp.cumsum(lengths)
    places = jnp.arange(SEQ, dtype=jnp.int32)
    return lax.optimization_barrier(jnp.sum((places[:, None] >= bounds[None, :]).astype(jnp.int32), -1))

def attention(hidden, weight_in, weight_out, doc_ids):
    mixed = matmul(hidden, weight_in)
    query = low(low_back(mixed[:, :D] * HD ** (-0.5)))
    keyval = low(low_back(mixed[:, D:]))
    key_rows, value_rows = (keyval[:, :HD], keyval[:, HD:])
    stacked = query.reshape(SEQ, HEADS, HD).transpose(1, 0, 2)
    places = jnp.arange(SEQ, dtype=jnp.int32)

    def one_block(offset):
        query_rows = lax.dynamic_slice_in_dim(stacked, offset, BLOCK, 1)
        spots = offset + jnp.arange(BLOCK, dtype=jnp.int32)
        owners = lax.dynamic_slice_in_dim(doc_ids, offset, BLOCK)
        allowed = (places[None, :] <= spots[:, None]) & (places[None, :] > spots[:, None] - WINDOW) & (doc_ids[None, :] == owners[:, None])
        scores = low_back(jnp.einsum('hbd,kd->hbk', query_rows, key_rows, precision=HIGHEST))
        scores = jnp.where(allowed[None], scores, MASKED)
        probs = low(jax.nn.softmax(scores, -1))
        return low(low_back(jnp.einsum('hbk,kd->hbd', probs, value_rows, precision=HIGHEST)))
    offsets = (jnp.arange(SEQ // BLOCK, dtype=jnp.int32) * BLOCK).astype(jnp.int32)
    outputs = lax.map(jax.checkpoint(one_block), offsets)
    outputs = outputs.transpose(0, 2, 1, 3).reshape(SEQ, D)
    return low_back(matmul(outputs, weight_out))

def layer(values, weight_in, weight_out, weight_up, weight_down, gain_rows, doc_ids):
    normed = low(layer_norm(values, gain_rows[0], gain_rows[1]))
    mixed = values + attention(normed, weight_in, weight_out, doc_ids)
    normed_two = low(layer_norm(mixed, gain_rows[2], gain_rows[3]))
    upper = low_back(matmul(normed_two, weight_up))
    active = low(jax.nn.gelu(upper, approximate=True))
    return mixed + low_back(matmul(active, weight_down))

def sequence_loss(lowered, items):
    table_low, weight_in, weight_out, weight_up, weight_down, gain_all = lowered
    token_row, length_row, pick_row, target_row = items
    doc_ids = doc_numbers(length_row)
    state = low_back(table_low[token_row])
    for depth in range(LAYERS):
        if depth > 0:
            state = low(low_back(state))
        state = layer(state, weight_in[depth], weight_out[depth], weight_up[depth], weight_down[depth], gain_all[depth], doc_ids)
    rounded = low(state)
    slots = jnp.arange(N_CTX * PICK, dtype=jnp.int32)
    live = target_row >= 0
    spots = slots // PICK * CTX_TOK + jnp.maximum(pick_row, 0)
    chosen = rounded[spots]
    logits = low_back(matmul(chosen, table_low.T))
    logsum = jax.nn.logsumexp(logits, -1)
    target_logit = jnp.take_along_axis(logits, jnp.maximum(target_row, 0)[:, None], 1)[:, 0]
    return jnp.sum(jnp.where(live, logsum - target_logit, 0.0))

def total_loss(params, data):
    lowered = tuple((low(item) for item in params))

    def one_sequence(carry, items):
        return (carry + jax.checkpoint(sequence_loss)(lowered, items), None)
    result, _ = lax.scan(one_sequence, jnp.zeros((), jnp.float32), data)
    return result

def factored(weight, gradient, row_stat, col_stat):
    decay = 1.0 - STEP ** (-0.8)
    square = gradient * gradient + SQUARE_EPS
    rows_new = decay * row_stat + (1.0 - decay) * lax.optimization_barrier(jnp.mean(square, -1))
    cols_new = decay * col_stat + (1.0 - decay) * lax.optimization_barrier(jnp.mean(square, -2))
    scaled = rows_new[..., :, None] * cols_new[..., None, :] / lax.optimization_barrier(jnp.mean(rows_new, -1))[..., None, None]
    update = gradient * lax.rsqrt(scaled)
    update = update / jnp.maximum(1.0, jnp.sqrt(lax.optimization_barrier(jnp.mean(update * update, (-2, -1)))))[..., None, None]
    size = jnp.maximum(SCALE_FLOOR, jnp.sqrt(lax.optimization_barrier(jnp.mean(weight * weight, (-2, -1)))))
    return (rows_new, cols_new, weight - RELATIVE_RATE * size[..., None, None] * update)

def unfactored(weight, gradient, stat):
    decay = 1.0 - STEP ** (-0.8)
    stat_new = decay * stat + (1.0 - decay) * (gradient * gradient + SQUARE_EPS)
    update = gradient * lax.rsqrt(stat_new)
    update = update / jnp.maximum(1.0, jnp.sqrt(lax.optimization_barrier(jnp.mean(update * update, -1))))[..., None]
    size = jnp.maximum(SCALE_FLOOR, jnp.sqrt(lax.optimization_barrier(jnp.mean(weight * weight, -1))))
    return (stat_new, weight - RELATIVE_RATE * size[..., None] * update)

def reference(token_ids, doc_lengths, picks, targets, table, table_rows, table_cols, attention_in, attention_in_rows, attention_in_cols, attention_out, attention_out_rows, attention_out_cols, hidden_in, hidden_in_rows, hidden_in_cols, hidden_out, hidden_out_rows, hidden_out_cols, gains, gains_stat):
    data = (token_ids.reshape(-1, SEQ), doc_lengths.reshape(-1, DOCS), picks.reshape(-1, N_CTX * PICK), targets.reshape(-1, N_CTX * PICK))
    params = (table, attention_in, attention_out, hidden_in, hidden_out, gains)

    def loss_of(weights):
        return total_loss(weights, data)
    loss_sum, pullback = jax.vjp(loss_of, params)
    grads = pullback(jnp.ones((), jnp.float32))[0]
    loss_count = jnp.sum((targets >= 0).astype(jnp.float32))
    table_grad, in_grad, out_grad, up_grad, down_grad, gains_grad = grads
    table_rows_new, table_cols_new, table_new = factored(table, table_grad, table_rows, table_cols)
    in_rows, in_cols, in_new = factored(attention_in, in_grad, attention_in_rows, attention_in_cols)
    out_rows, out_cols, out_new = factored(attention_out, out_grad, attention_out_rows, attention_out_cols)
    up_rows, up_cols, up_new = factored(hidden_in, up_grad, hidden_in_rows, hidden_in_cols)
    down_rows, down_cols, down_new = factored(hidden_out, down_grad, hidden_out_rows, hidden_out_cols)
    gains_stat_new, gains_new = unfactored(gains, gains_grad, gains_stat)
    return (loss_sum, loss_count, table_grad, table_rows_new, table_cols_new, table_new, in_grad, in_rows, in_cols, in_new, out_grad, out_rows, out_cols, out_new, up_grad, up_rows, up_cols, up_new, down_grad, down_rows, down_cols, down_new, gains_grad, gains_stat_new, gains_new)
```

```python
import jax
import jax.numpy as jnp
from jax import lax
from jax.sharding import PartitionSpec as P

HD = 64
WINDOW = 512
STEP = 10
NORM_EPS = 1e-05
SQUARE_EPS = 1e-30
SCALE_FLOOR = 0.001
RELATIVE_RATE = 0.5
MASKED = -1e30
DECAY = 1.0 - STEP ** (-0.8)
BLOCKS = ("dp", "ctx")


def bfloat(values):
    return values.astype(jnp.bfloat16)


def single(values):
    return values.astype(jnp.float32)


def matmul(left, right):
    return jnp.dot(left, right, preferred_element_type=jnp.float32)


def matmul_left(left, right):
    return lax.dot_general(
        left, right, (((0,), (0,)), ((), ())), preferred_element_type=jnp.float32
    )


def matmul_right(left, right):
    return lax.dot_general(
        left, right, (((1,), (1,)), ((), ())), preferred_element_type=jnp.float32
    )


def layer_norm(values, gain, shift):
    center = values - jnp.mean(values, -1, keepdims=True)
    spread = jnp.mean(center * center, -1, keepdims=True)
    return center * lax.rsqrt(spread + NORM_EPS) * gain + shift


def gelu_tanh(values):
    return jax.nn.gelu(values, approximate=True)


def at(values, index, axis):
    return lax.dynamic_index_in_dim(values, index, axis, keepdims=False)


def swap(values):
    return lax.ppermute(values, "section", [(0, 1), (1, 0)])


def cross(values, axis, bits):
    return lax.ppermute(values, axis, [(i, i ^ bits) for i in range(lax.axis_size(axis))])


def shifted(values, axis, distance):
    devices = range(lax.axis_size(axis))
    return lax.ppermute(
        values, axis, [(i, i + distance) for i in devices if i + distance in devices]
    )


def by_fours():
    return lax.axis_size("dp") == 4 and lax.axis_size("ctx") == 4


def mine_first(mine, theirs):
    first = lax.axis_index("section") == 0
    return jnp.where(first, mine, theirs), jnp.where(first, theirs, mine)


def gather_blocks(part):
    if not by_fours():
        return lax.all_gather(part, BLOCKS, axis=0)
    z, c = lax.axis_index("dp"), lax.axis_index("ctx")
    pieces = [part] + [cross(part, "dp", k) for k in (1, 2, 3)]
    column = jnp.stack(
        [lax.select_n(z, *[pieces[place ^ k] for k in range(4)]) for place in range(4)]
    )
    beside = cross(column, "ctx", 1)
    above = cross(column, "ctx", 2)
    far = jnp.concatenate([cross(above[:2], "ctx", 1), cross(beside[2:], "ctx", 2)])
    whole = jnp.zeros((4, 4) + part.shape, part.dtype)
    for k, piece in enumerate((column, beside, above, far)):
        whole = lax.dynamic_update_slice_in_dim(whole, piece[:, None], c ^ k, 1)
    return whole.reshape((16,) + part.shape)


def scatter_blocks(parts):
    if not by_fours():
        total = lax.psum_scatter(bfloat(parts), BLOCKS, scatter_dimension=0)
        return single(total)
    z, c = lax.axis_index("dp"), lax.axis_index("ctx")
    x, y = c & 1, c >> 1
    grid = parts.reshape((4, 2, 2) + parts.shape[1:])

    def halve(values, axis, bits, index):
        sent = cross(bfloat(at(values, 1 - index, axis)), "ctx", bits)
        return single(at(values, index, axis)) + single(sent)

    near, far = grid[:2], grid[2:]
    near, far = halve(near, 2, 1, x), halve(far, 1, 2, y)
    near, far = halve(near, 1, 2, y), halve(far, 1, 1, x)
    column = jnp.concatenate([near, far])
    low = bfloat(column)
    total = at(column, z, 0)
    for k in (1, 2, 3):
        total = total + single(cross(at(low, z ^ k, 0), "dp", k))
    return total


def scatter_rows(parts):
    if not by_fours():
        return single(lax.psum_scatter(bfloat(parts), "dp", scatter_dimension=0))
    z = lax.axis_index("dp")
    low = bfloat(parts)
    total = single(at(parts, z, 0))
    for k in (1, 2, 3):
        total = total + single(cross(at(low, z ^ k, 0), "dp", k))
    return total


def summed(values, axes):
    if not by_fours():
        return lax.psum(values, axes)
    for axis in axes:
        one, two, three = (cross(values, axis, k) for k in (1, 2, 3))
        values = (values + one) + (two + three)
    return values


def doc_numbers(lengths, places):
    bounds = jnp.cumsum(lengths)
    return jnp.sum((places[:, None] >= bounds[None, :]).astype(jnp.int32), -1)


def allowed_pairs(lengths, query_places, key_places):
    query_docs = doc_numbers(lengths, query_places)
    key_docs = doc_numbers(lengths, key_places)
    return (
        (key_places[None, :] <= query_places[:, None])
        & (key_places[None, :] > query_places[:, None] - WINDOW)
        & (key_places[None, :] >= 0)
        & (key_docs[None, :] == query_docs[:, None])
    )


def earlier_count(local_len):
    return min(lax.axis_size("ctx") - 1, -(-(WINDOW - 1) // local_len))


def key_rows(keyval):
    reach = earlier_count(keyval.shape[0])
    return jnp.concatenate(
        [shifted(keyval, "ctx", k) for k in range(reach, 0, -1)] + [keyval]
    )


def key_rows_back(grads, local_len):
    reach = earlier_count(local_len)
    total = grads[reach * local_len :]
    for k in range(1, reach + 1):
        start = (reach - k) * local_len
        total = total + shifted(grads[start : start + local_len], "ctx", -k)
    return total


def attend(query, keyval, allowed):
    rows, columns = query.shape
    heads = query.reshape(rows, columns // HD, HD)
    keys, values = keyval[:, :HD], keyval[:, HD:]
    scores = jnp.einsum("qhd,kd->hqk", heads, keys, preferred_element_type=jnp.float32)
    scores = jnp.where(allowed[None], scores, MASKED)
    highest = jnp.max(scores, -1, keepdims=True)
    exponents = jnp.exp(scores - highest)
    totals = jnp.sum(exponents, -1, keepdims=True)
    output = jnp.einsum(
        "hqk,kd->qhd", bfloat(exponents / totals), values, preferred_element_type=jnp.float32
    )
    return bfloat(output).reshape(rows, columns), highest + jnp.log(totals)


def attend_back(query, keyval, allowed, logsum, grad_out):
    rows, columns = query.shape
    heads = query.reshape(rows, columns // HD, HD)
    grads = bfloat(grad_out).reshape(rows, columns // HD, HD)
    keys, values = keyval[:, :HD], keyval[:, HD:]
    scores = jnp.einsum("qhd,kd->hqk", heads, keys, preferred_element_type=jnp.float32)
    probs = jnp.exp(jnp.where(allowed[None], scores, MASKED) - logsum)
    grad_probs = jnp.einsum("qhd,kd->hqk", grads, values, preferred_element_type=jnp.float32)
    grad_scores = bfloat(probs * (grad_probs - jnp.sum(probs * grad_probs, -1, keepdims=True)))
    grad_query = jnp.einsum("hqk,kd->qhd", grad_scores, keys, preferred_element_type=jnp.float32)
    grad_keys = jnp.einsum("hqk,qhd->kd", grad_scores, heads, preferred_element_type=jnp.float32)
    grad_values = jnp.einsum(
        "hqk,qhd->kd", bfloat(probs), grads, preferred_element_type=jnp.float32
    )
    grad_query = bfloat(single(bfloat(grad_query.reshape(rows, columns))) * HD ** (-0.5))
    return grad_query, jnp.concatenate([grad_keys, grad_values], 1)


def feed_forward(mixed, weights):
    gains, hidden_in, hidden_out = weights
    rows = mixed.shape[0]
    normed = bfloat(layer_norm(mixed, gains[2], gains[3]))
    both = jnp.concatenate([normed, swap(normed)])
    upper = matmul(both, hidden_in)
    active = bfloat(gelu_tanh(upper))
    partial = matmul(active, hidden_out)
    result = mixed + (partial[:rows] + swap(partial[rows:]))
    return result, (both, upper, active)


def feed_forward_back(grad_result, mixed, kept, weights):
    gains, hidden_in, hidden_out = weights
    both, upper, active = kept
    rows = mixed.shape[0]
    low = bfloat(grad_result)
    grad_both = jnp.concatenate([low, swap(low)])
    grad_hidden_out = matmul_left(active, grad_both)
    _, pull = jax.vjp(gelu_tanh, upper)
    grad_upper = bfloat(pull(matmul_right(grad_both, hidden_out))[0])
    grad_hidden_in = matmul_left(both, grad_upper)
    partial = matmul_right(grad_upper, hidden_in)
    _, pull = jax.vjp(layer_norm, mixed, gains[2], gains[3])
    grad_mixed, grad_gain, grad_shift = pull(partial[:rows] + swap(partial[rows:]))
    return grad_mixed + grad_result, grad_hidden_in, grad_hidden_out, grad_gain, grad_shift


def factored_sums(weight, gradient, row_stat):
    square = gradient * gradient + SQUARE_EPS
    rows_new = DECAY * row_stat + (1.0 - DECAY) * jnp.mean(square, -1)
    columns = jnp.sum(square, 0)
    scaled = jnp.sum(gradient * gradient / rows_new[:, None], 0)
    return rows_new, columns, scaled, jnp.sum(rows_new), jnp.sum(weight * weight)


def factored_new(weight, gradient, rows_new, col_stat, sums, row_count):
    columns, scaled, rows_sum, weight_sum = sums
    entries = row_count * weight.shape[1]
    cols_new = DECAY * col_stat + (1.0 - DECAY) * columns / row_count
    mean_rows = rows_sum / row_count
    update_sum = mean_rows * jnp.sum(scaled / cols_new)
    clipping = jnp.maximum(1.0, jnp.sqrt(update_sum / entries))
    size = jnp.maximum(SCALE_FLOOR, jnp.sqrt(weight_sum / entries))
    update = gradient * lax.rsqrt(rows_new[:, None] * cols_new[None, :] / mean_rows)
    return cols_new, weight - RELATIVE_RATE * size * (update / clipping)


def body(
    token_ids,
    doc_lengths,
    picks,
    targets,
    table,
    table_rows,
    table_cols,
    attention_in,
    attention_in_rows,
    attention_in_cols,
    attention_out,
    attention_out_rows,
    attention_out_cols,
    hidden_in,
    hidden_in_rows,
    hidden_in_cols,
    hidden_out,
    hidden_out_rows,
    hidden_out_cols,
    gains,
    gains_stat,
):
    section = lax.axis_index("section")
    first = section == 0
    z, c = lax.axis_index("dp"), lax.axis_index("ctx")
    z_count, c_count = lax.axis_size("dp"), lax.axis_size("ctx")
    blocks = z_count * c_count
    model = table.shape[1]
    part = attention_in.shape[1]
    units = hidden_in.shape[2]
    half = units // (2 * blocks)
    wide = attention_in.shape[2]
    local_len = token_ids.shape[2]
    slots = picks.shape[2]
    vocab_here = table.shape[0]
    vocab_base = z * vocab_here

    low_in = bfloat(attention_in[0])
    low_out = jnp.concatenate(
        [bfloat(attention_out[0]), bfloat(gains[0]).T, jnp.zeros((part, wide - model - 4), jnp.bfloat16)], 1
    )
    attention_parts = mine_first(
        jnp.where(first, low_in, low_out), swap(jnp.where(first, low_out, low_in))
    )
    low_up = bfloat(hidden_in[0]).reshape(part, blocks, 2, half)
    low_down = bfloat(hidden_out[0])

    def unit_half(index):
        up = at(low_up, index, 2).reshape(part, -1, model)
        down = lax.dynamic_slice_in_dim(low_down, index * half, half, 0)
        return jnp.concatenate([up[:, k] for k in range(up.shape[1])] + [down])

    hidden_parts = mine_first(unit_half(section), swap(unit_half(1 - section)))

    def layer_weights(layer):
        mine = gather_blocks(attention_parts[layer]).reshape(model, wide)
        weight_in, weight_out = mine_first(mine, swap(mine))
        gain_rows = single(weight_out[:, model : model + 4]).T
        hidden = gather_blocks(hidden_parts[layer])
        ups = units // 2 // model
        up = jnp.concatenate(
            [hidden[:, k * part : (k + 1) * part].reshape(model, model) for k in range(ups)], 1
        )
        down = hidden[:, ups * part :].reshape(units // 2, model)
        return weight_in, weight_out[:, :model], gain_rows, up, down

    my_ids = at(token_ids, section, 0) - vocab_base
    inside = (my_ids >= 0) & (my_ids < vocab_here)
    looked = jnp.take(table, jnp.clip(my_ids, 0, vocab_here - 1), axis=0)
    start = scatter_rows(jnp.where(inside[..., None], bfloat(looked), 0))

    all_targets = lax.all_gather(targets, "ctx").transpose(1, 2, 0, 3).reshape(-1)
    all_ids = lax.all_gather(token_ids, "ctx").transpose(1, 2, 0, 3).reshape(-1)
    lengths = at(doc_lengths, section, 0)[0]
    my_picks = at(picks, section, 0)[0]

    places = c * local_len + jnp.arange(local_len, dtype=jnp.int32)
    reach = earlier_count(local_len)
    key_places = (c - reach) * local_len + jnp.arange((reach + 1) * local_len, dtype=jnp.int32)
    allowed = allowed_pairs(lengths, places, key_places)
    pick_allowed = allowed_pairs(lengths, c * local_len + jnp.maximum(my_picks, 0), key_places)
    onehot = (my_picks[:, None] == jnp.arange(local_len, dtype=jnp.int32)[None, :]).astype(
        jnp.bfloat16
    )

    in0, out0, gains0, up0, down0 = layer_weights(0)
    normed0 = bfloat(layer_norm(start, gains0[0], gains0[1]))
    mixed_in = matmul(normed0, in0)
    query0 = bfloat(mixed_in[:, :model] * HD ** (-0.5))
    keyval0 = key_rows(bfloat(mixed_in[:, model:]))
    attended0, logsum0 = attend(query0, keyval0, allowed)
    mixed0 = start + matmul(attended0, out0)
    result0, hidden0 = feed_forward(mixed0, (gains0, up0, down0))

    in1, out1, gains1, up1, down1 = layer_weights(1)
    inputs1_low = bfloat(result0)
    inputs1 = single(inputs1_low)
    normed1 = bfloat(layer_norm(inputs1, gains1[0], gains1[1]))
    keyval1 = key_rows(bfloat(matmul(normed1, in1[:, model:])))
    picked_normed = bfloat(matmul(onehot, normed1))
    picked = matmul(onehot, inputs1_low)
    query1 = bfloat(matmul(picked_normed, in1[:, :model]) * HD ** (-0.5))
    attended1, logsum1 = attend(query1, keyval1, pick_allowed)
    mixed1 = picked + matmul(attended1, out1)
    result1, hidden1 = feed_forward(mixed1, (gains1, up1, down1))

    chosen_mine = gather_blocks(bfloat(result1)).reshape(-1, model)
    chosen = jnp.concatenate(mine_first(chosen_mine, swap(chosen_mine)))
    table_low = bfloat(table)
    logits = matmul_right(chosen, table_low)
    local_target = all_targets - vocab_base
    matches = local_target[:, None] == jnp.arange(vocab_here, dtype=jnp.int32)[None, :]
    highest = jnp.max(logits, -1)
    totals = jnp.sum(jnp.exp(logits - highest[:, None]), -1)
    target_logit = jnp.sum(jnp.where(matches, logits, 0.0), -1)
    stats = jnp.stack([highest, totals, target_logit])

    def combine(one, two):
        top = jnp.maximum(one[0], two[0])
        both = one[1] * jnp.exp(one[0] - top) + two[1] * jnp.exp(two[0] - top)
        return jnp.stack([top, both, one[2] + two[2]])

    if by_fours():
        one, two, three = (cross(stats, "dp", k) for k in (1, 2, 3))
        stats = combine(combine(stats, one), combine(two, three))
    else:
        stats = lax.scan(
            lambda total, share: (combine(total, share), None),
            jnp.stack([jnp.full_like(highest, MASKED), 0 * highest, 0 * highest]),
            lax.all_gather(stats, "dp"),
        )[0]
    logsum = stats[0] + jnp.log(stats[1])
    live = all_targets >= 0
    loss_sum = jnp.sum(jnp.where(live, logsum - stats[2], 0.0))
    loss_count = jnp.sum(single(live))
    grad_logits = bfloat(
        jnp.where(live[:, None], jnp.exp(logits - logsum[:, None]) - single(matches), 0.0)
    )
    grad_head = matmul_left(grad_logits, chosen)
    mine_logits = at(
        at(grad_logits.reshape(2, z_count, c_count, slots, vocab_here), section, 0), c, 1
    )
    grad_chosen = matmul(mine_logits.reshape(-1, vocab_here), table_low)
    grad_result1 = scatter_rows(grad_chosen.reshape(z_count, slots, model))

    grad_mixed1, grad_up1, grad_down1, grad_gain2, grad_shift2 = feed_forward_back(
        grad_result1, mixed1, hidden1, (gains1, up1, down1)
    )
    grad_low = bfloat(grad_mixed1)
    grad_out1 = matmul_left(attended1, grad_low)
    grad_query, grad_keyval = attend_back(
        query1, keyval1, pick_allowed, logsum1, matmul_right(grad_low, out1)
    )
    grad_keyval = bfloat(key_rows_back(grad_keyval, local_len))
    grad_in1 = jnp.concatenate(
        [matmul_left(picked_normed, grad_query), matmul_left(normed1, grad_keyval)], 1
    )
    spread = jnp.dot(
        single(onehot).T,
        jnp.concatenate([matmul_right(grad_query, in1[:, :model]), grad_mixed1], 1),
        precision=lax.Precision.HIGHEST,
    )
    grad_normed = matmul_right(grad_keyval, in1[:, model:]) + spread[:, :model]
    _, pull = jax.vjp(layer_norm, inputs1, gains1[0], gains1[1])
    grad_inputs1, grad_gain1, grad_shift1 = pull(grad_normed)
    grad_result0 = single(bfloat(grad_inputs1 + spread[:, model:]))
    grad_gains1 = jnp.stack([grad_gain1, grad_shift1, grad_gain2, grad_shift2])

    grad_mixed0, grad_up0, grad_down0, grad_gain2, grad_shift2 = feed_forward_back(
        grad_result0, mixed0, hidden0, (gains0, up0, down0)
    )
    grad_low = bfloat(grad_mixed0)
    grad_out0 = matmul_left(attended0, grad_low)
    grad_query, grad_keyval = attend_back(
        query0, keyval0, allowed, logsum0, matmul_right(grad_low, out0)
    )
    grad_keyval = bfloat(key_rows_back(grad_keyval, local_len))
    grad_mixed_in = jnp.concatenate([grad_query, grad_keyval], 1)
    grad_in0 = matmul_left(normed0, grad_mixed_in)
    _, pull = jax.vjp(layer_norm, start, gains0[0], gains0[1])
    grad_start, grad_gain1, grad_shift1 = pull(matmul_right(grad_mixed_in, in0))
    grad_start = bfloat(grad_start + grad_mixed0)
    grad_gains0 = jnp.stack([grad_gain1, grad_shift1, grad_gain2, grad_shift2])

    if 2 * blocks * local_len <= 2 * vocab_here:
        mine = gather_blocks(grad_start).reshape(-1, model)
        looked_grads = jnp.concatenate(mine_first(mine, swap(mine)))
        local = all_ids - vocab_base
        local = jnp.where((local >= 0) & (local < vocab_here), local, vocab_here)
        lookup_grad = jax.ops.segment_sum(single(looked_grads), local, num_segments=vocab_here)
    else:
        column = lax.all_gather(grad_start, "dp").reshape(-1, model)
        local = jnp.where(inside, my_ids, vocab_here).reshape(-1)
        lookup_grad = jax.ops.segment_sum(single(column), local, num_segments=vocab_here)
        lookup_grad = single(lax.psum(bfloat(lookup_grad), ("section", "ctx")))
    grad_table = grad_head + lookup_grad

    def weight_grads(grad_in, grad_out, grad_gains, grad_up, grad_down):
        grad_out = jnp.concatenate(
            [grad_out, grad_gains.T, jnp.zeros((model, wide - model - 4), jnp.float32)], 1
        )
        kept = jnp.where(first, grad_in, grad_out)
        sent = swap(bfloat(jnp.where(first, grad_out, grad_in)))
        attention = scatter_blocks((kept + single(sent)).reshape(blocks, part, wide))
        ups = grad_up.shape[1] // model
        packed = jnp.concatenate(
            [grad_up[:, k * model : (k + 1) * model].reshape(blocks, part, model) for k in range(ups)]
            + [grad_down.reshape(blocks, half, model)],
            1,
        )
        return attention, scatter_blocks(packed)

    grads1 = weight_grads(grad_in1, grad_out1, grad_gains1, grad_up1, grad_down1)
    grads0 = weight_grads(grad_in0, grad_out0, grad_gains0, grad_up0, grad_down0)
    owned, other = [], []
    for one, two in zip(grads0, grads1):
        owned.append(jnp.where(first, one, two))
        other.append(swap(jnp.where(first, two, one)))
    shard_in, shard_out = mine_first(owned[0], other[0])
    shard_gains = shard_out[:, model : model + 4].T
    shard_out = shard_out[:, :model]
    halves = jnp.stack(mine_first(owned[1], other[1]))
    ups = units // 2 // model
    shard_up = halves[:, : ups * part].reshape(2, ups, part, model).transpose(2, 0, 1, 3)
    shard_up = shard_up.reshape(part, 2, blocks, half).transpose(0, 2, 1, 3).reshape(part, units)
    shard_down = halves[:, ups * part :].reshape(2 * half, model)

    entries = [
        (table, grad_table, table_rows, table_cols, vocab_here * z_count),
        (attention_in[0], shard_in, attention_in_rows[0], attention_in_cols[0], model),
        (attention_out[0], shard_out, attention_out_rows[0], attention_out_cols[0], model),
        (hidden_in[0], shard_up, hidden_in_rows[0], hidden_in_cols[0], model),
        (hidden_out[0], shard_down, hidden_out_rows[0], hidden_out_cols[0], units),
    ]
    sums = [factored_sums(*entry[:3]) for entry in entries]
    gain_weight = gains[0]
    gain_stat_new = DECAY * gains_stat[0] + (1.0 - DECAY) * (shard_gains * shard_gains + SQUARE_EPS)
    gain_update = shard_gains * lax.rsqrt(gain_stat_new)

    def packed(group):
        flat = [item.reshape(-1) for item in group]
        return jnp.concatenate(flat), [item.shape for item in group]

    def unpacked(flat, shapes):
        items, start = [], 0
        for shape in shapes:
            size = 1
            for length in shape:
                size *= length
            items.append(flat[start : start + size].reshape(shape))
            start += size
        return items

    table_group, table_shapes = packed(sums[0][1:])
    layer_group, layer_shapes = packed(
        [item for entry in sums[1:] for item in entry[1:]]
        + [jnp.sum(gain_weight * gain_weight, -1), jnp.sum(gain_update * gain_update, -1)]
    )
    everything = summed(jnp.concatenate([table_group, layer_group]), ("dp",))
    table_sums = unpacked(everything[: table_group.shape[0]], table_shapes)
    layer_sums = unpacked(summed(everything[table_group.shape[0] :], ("ctx",)), layer_shapes)
    groups = [table_sums] + [layer_sums[4 * k : 4 * k + 4] for k in range(4)]
    gain_squares, gain_update_sums = layer_sums[16:]
    outs = []
    for (weight, gradient, _, col_stat, row_count), own, group in zip(entries, sums, groups):
        cols_new, new = factored_new(weight, gradient, own[0], col_stat, group, row_count)
        outs.append((gradient, own[0], cols_new, new))
    gain_clipping = jnp.maximum(1.0, jnp.sqrt(gain_update_sums / model))
    gain_size = jnp.maximum(SCALE_FLOOR, jnp.sqrt(gain_squares / model))
    gain_new = gain_weight - RELATIVE_RATE * gain_size[:, None] * (
        gain_update / gain_clipping[:, None]
    )
    layered = [item[None] for out in outs[1:] for item in out]
    return (
        loss_sum,
        loss_count,
        *outs[0],
        *layered,
        shard_gains[None],
        gain_stat_new[None],
        gain_new[None],
    )


def solution(mesh):
    rows = P("section", BLOCKS, None)
    row = P("section", BLOCKS)
    shared = P("section", None)
    side = P("section", None, BLOCKS)
    matrix_in = (rows, row, shared)
    matrix_out = (rows, row, shared, rows)
    placed = (
        P(None, None, "ctx"),
        P(None, "dp", None),
        P(None, "dp", "ctx"),
        P(None, None, "ctx"),
        P("dp", None),
        P("dp"),
        P(),
        *(matrix_in * 4),
        side,
        side,
    )
    return jax.shard_map(
        body,
        mesh=mesh,
        in_specs=placed,
        out_specs=(
            P(),
            P(),
            P("dp", None),
            P("dp"),
            P(),
            P("dp", None),
            *(matrix_out * 4),
            side,
            side,
            side,
        ),
        check_vma=False,
    )
```

```python
import functools

import jax
import jax.numpy as jnp
from jax import lax
from jax.experimental import pallas as pl
from jax.experimental.pallas import tpu as pltpu
from jax.sharding import PartitionSpec as P

HD = 64
WINDOW = 512
STEP = 10
NORM_EPS = 1e-05
SQUARE_EPS = 1e-30
SCALE_FLOOR = 0.001
RELATIVE_RATE = 0.5
MASKED = -1e30
DECAY = 1.0 - STEP ** (-0.8)
BLOCKS = ("dp", "ctx")
LANES = 128
DEAD = -(1 << 30)
MIB = 1 << 20


def bfloat(values):
    return values.astype(jnp.bfloat16)


def single(values):
    return values.astype(jnp.float32)


def matmul(left, right):
    return jnp.dot(left, right, preferred_element_type=jnp.float32)


def matmul_left(left, right):
    return lax.dot_general(
        left, right, (((0,), (0,)), ((), ())), preferred_element_type=jnp.float32
    )


def matmul_right(left, right):
    return lax.dot_general(
        left, right, (((1,), (1,)), ((), ())), preferred_element_type=jnp.float32
    )


def layer_norm(values, gain, shift):
    center = values - jnp.mean(values, -1, keepdims=True)
    spread = jnp.mean(center * center, -1, keepdims=True)
    return center * lax.rsqrt(spread + NORM_EPS) * gain + shift


def gelu_tanh(values):
    return jax.nn.gelu(values, approximate=True)


def at(values, index, axis):
    return lax.dynamic_index_in_dim(values, index, axis, keepdims=False)


def swap(values):
    return lax.ppermute(values, "section", [(0, 1), (1, 0)])


def cross(values, axis, bits):
    return lax.ppermute(values, axis, [(i, i ^ bits) for i in range(lax.axis_size(axis))])


def shifted(values, axis, distance):
    devices = range(lax.axis_size(axis))
    return lax.ppermute(
        values, axis, [(i, i + distance) for i in devices if i + distance in devices]
    )


def by_fours():
    return lax.axis_size("dp") == 4 and lax.axis_size("ctx") == 4


def mine_first(mine, theirs):
    first = lax.axis_index("section") == 0
    return jnp.where(first, mine, theirs), jnp.where(first, theirs, mine)


def after(values, *earlier):
    return lax.optimization_barrier((values, *earlier))[0]


def column_pieces(part):
    if not by_fours():
        return (lax.all_gather(part, "dp", axis=0),)
    return tuple(cross(part, "dp", k) for k in (1, 2, 3))


def column_join(part, pieces):
    if not by_fours():
        return pieces[0]
    return in_order((part, *pieces), "dp")


def plane_near(column):
    if not by_fours():
        return (lax.all_gather(column, "ctx", axis=1),)
    return cross(column, "ctx", 1), cross(column, "ctx", 2)


def plane_far(near):
    if not by_fours():
        return ()
    beside, above = near
    return cross(above[:2], "ctx", 1), cross(beside[2:], "ctx", 2)


def plane_list(column, near, far):
    if not by_fours():
        return near[0].reshape((-1,) + column.shape[1:])
    return (column, *near, jnp.concatenate(far))


def plane_near_half(column, side):
    if not by_fours():
        return plane_near(column) if side == 0 else ()
    return plane_near(column[2 * side : 2 * side + 2])


def plane_far_half(first, second):
    if not by_fours():
        return ()
    return cross(first[1], "ctx", 1), cross(second[0], "ctx", 2)


def plane_halves(column, near, far):
    if not by_fours():
        return plane_list(column, near[0], far)
    return (column, *zip(*near), tuple(far))


def in_order(pieces, axis, at_axis=0):
    i = lax.axis_index(axis)
    return jnp.stack(
        [lax.select_n(i, *[pieces[place ^ k] for k in range(4)]) for place in range(4)], at_axis
    )


def weights_kernel(place_ref, *refs):
    *pieces, in_ref, out_ref = refs
    c, first = place_ref[0], place_ref[1] == 0
    columns, part = pieces[0].shape[:2]

    def lay(ref, pieces):
        for k, piece in enumerate(pieces):
            for z in range(columns):
                rows = pl.ds(pl.multiple_of((4 * z + (c ^ k)) * part, 16), part)
                ref[rows, :] = piece[z]

    @pl.when(first)
    def _():
        lay(in_ref, pieces[:4])
        lay(out_ref, pieces[4:])

    @pl.when(~first)
    def _():
        lay(in_ref, pieces[4:])
        lay(out_ref, pieces[:4])


def attention_weights(mine, theirs, model, layer):
    if by_fours():
        columns, both, wide = mine[0].shape
        place = jnp.stack([lax.axis_index("ctx"), lax.axis_index("section")])
        weight_in, weight_out = pl.pallas_call(
            weights_kernel,
            grid_spec=pltpu.PrefetchScalarGridSpec(
                num_scalar_prefetch=1,
                grid=(1,),
                in_specs=[pl.BlockSpec((columns, both // 2, wide), lambda *_: (0, layer, 0))] * 8,
                out_specs=[whole_block((model, wide))] * 2,
            ),
            out_shape=[jax.ShapeDtypeStruct((model, wide), jnp.bfloat16)] * 2,
            compiler_params=vmem(24),
            cost_estimate=small_cost(
                flops=0, bytes_accessed=8 * model * wide, transcendentals=0
            ),
        )(place, *mine, *theirs)
    else:
        part = mine.shape[1] // 2
        weights = mine_first(mine, theirs)
        weight_in, weight_out = (
            w[:, layer * part : (layer + 1) * part].reshape(model, -1) for w in weights
        )
    return weight_in, weight_out[:, :model], single(weight_out[:, model : model + 4]).T


def gather_blocks(part):
    return gather_ctx(column_join(part, column_pieces(part))).swapaxes(0, 1).reshape(
        (-1,) + part.shape
    )


def gather_ctx(part):
    if not by_fours():
        return lax.all_gather(part, "ctx", axis=0)
    return in_order([part] + [cross(part, "ctx", k) for k in (1, 2, 3)], "ctx")


def scattered(parts):
    return single(lax.psum_scatter(parts, BLOCKS, scatter_dimension=0))


def corner(parts, rows, z, y=None, x=None):
    grid = parts.reshape((4, 2, 2) + parts.shape[1:])
    first, count = rows
    start = (z, 0 if y is None else y, 0 if x is None else x, first, 0)
    size = (2, 2 if y is None else 1, 2 if x is None else 1, count, parts.shape[2])
    return lax.dynamic_slice(grid, start, size)


def plane_bits():
    c = lax.axis_index("ctx")
    return c & 1, c >> 1


def half_first(parts, rows):
    x, y = plane_bits()
    return (
        cross(corner(parts, rows, 0, x=1 - x), "ctx", 1),
        cross(corner(parts, rows, 2, y=1 - y), "ctx", 2),
    )


def half_kept(parts, rows, got):
    x, y = plane_bits()
    near = bfloat(single(corner(parts, rows, 0, x=x)) + single(got[0]))
    far = bfloat(single(corner(parts, rows, 2, y=y)) + single(got[1]))
    near, far = near[:, :, 0], far[:, 0]
    return (at(near, y, 1), at(far, x, 1)), (at(near, 1 - y, 1), at(far, 1 - x, 1))


def half_send(halves):
    return cross(halves[0], "ctx", 2), cross(halves[1], "ctx", 1)


def half_column(kept, got):
    return jnp.concatenate([bfloat(single(one) + single(two)) for one, two in zip(kept, got)])


def row_pieces(parts):
    if not by_fours():
        return (lax.psum_scatter(bfloat(parts), "dp", scatter_dimension=0),)
    z = lax.axis_index("dp")
    low = bfloat(parts)
    return tuple(cross(at(low, z ^ k, 0), "dp", k) for k in (1, 2, 3))


def row_sum(parts, pieces):
    total = single(pieces[0])
    for piece in pieces[1:]:
        total = total + single(piece)
    return single(at(parts, lax.axis_index("dp"), 0)) + total if by_fours() else total


def scatter_rows(parts):
    return row_sum(parts, row_pieces(parts))


def summed(values, axes):
    if not by_fours():
        return lax.psum(values, axes)
    for axis in axes:
        one, two, three = (cross(values, axis, k) for k in (1, 2, 3))
        values = (values + one) + (two + three)
    return values


def doc_numbers(lengths, places):
    bounds = jnp.cumsum(lengths)
    return jnp.sum((places[:, None] >= bounds[None, :]).astype(jnp.int32), -1)


def pair_bias(lengths, query_places, key_places):
    query_docs = doc_numbers(lengths, query_places)
    key_docs = doc_numbers(lengths, key_places)
    allowed = (
        (key_places[None, :] <= query_places[:, None])
        & (key_places[None, :] > query_places[:, None] - WINDOW)
        & (key_places[None, :] >= 0)
        & (key_docs[None, :] == query_docs[:, None])
    )
    return jnp.where(allowed, 0.0, MASKED)


def earlier_count(local_len):
    return min(lax.axis_size("ctx") - 1, -(-(WINDOW - 1) // local_len))


def key_rows(keyval):
    reach = earlier_count(keyval.shape[0])
    return jnp.concatenate(
        [shifted(keyval, "ctx", k) for k in range(reach, 0, -1)] + [keyval]
    )


def key_rows_back(grads, local_len):
    reach = earlier_count(local_len)
    starts = [(reach - k) * local_len for k in range(1, reach + 1)]
    return tuple(
        shifted(grads[start : start + local_len], "ctx", -(k + 1))
        for k, start in enumerate(starts)
    )


def key_rows_sum(grads, pieces, local_len):
    total = grads[earlier_count(local_len) * local_len :]
    for piece in pieces:
        total = total + piece
    return bfloat(total)


def whole_block(shape):
    return pl.BlockSpec(shape, lambda *_: (0,) * len(shape))


def vmem(mebibytes):
    return pltpu.CompilerParams(vmem_limit_bytes=mebibytes * MIB)


def small_cost(flops, bytes_accessed, transcendentals):
    return pl.CostEstimate(
        flops=flops // 16, bytes_accessed=bytes_accessed // 16, transcendentals=0 * transcendentals
    )


def row_block(rows, most):
    block = most
    while rows % block:
        block //= 2
    return block


def turned(values):
    return pltpu.roll(values, HD, 1)


def softmax_rows(scores):
    exponents = jnp.exp(scores - jnp.max(scores, -1, keepdims=True))
    return exponents / jnp.sum(exponents, -1, keepdims=True)


def attend_kernel(query_ref, keyval_ref, bias_ref, out_ref):
    keyval = keyval_ref[...]
    bias = bias_ref[...]
    pair = single(query_ref[...])
    left = lax.broadcasted_iota(jnp.int32, pair.shape, 1) < HD
    outs = []
    for heads in (pair, turned(pair)):
        query = bfloat(jnp.where(left, heads, 0.0))
        probs = softmax_rows(matmul_right(query, keyval) + bias)
        outs.append(matmul(bfloat(probs), keyval))
    out_ref[...] = bfloat(jnp.where(left, turned(outs[0]), outs[1]))


def attend(query, keyval, bias):
    rows, columns = query.shape
    pair = 2 * HD
    return pl.pallas_call(
        attend_kernel,
        grid=(columns // pair,),
        in_specs=[
            pl.BlockSpec((rows, pair), lambda i: (0, i)),
            whole_block(keyval.shape),
            whole_block(bias.shape),
        ],
        out_specs=pl.BlockSpec((rows, pair), lambda i: (0, i)),
        out_shape=jax.ShapeDtypeStruct((rows, columns), jnp.bfloat16),
        compiler_params=vmem(40),
        cost_estimate=small_cost(
            flops=4 * rows * columns * keyval.shape[0],
            bytes_accessed=8 * rows * columns,
            transcendentals=rows * columns * keyval.shape[0] // HD,
        ),
    )(query, keyval, bias)


def attend_back_kernel(query_ref, keyval_ref, bias_ref, grad_ref, grad_query_ref, grad_keyval_ref):
    keyval = keyval_ref[...]
    bias = bias_ref[...]
    pair = single(query_ref[...])
    grads = single(grad_ref[...])
    left = lax.broadcasted_iota(jnp.int32, pair.shape, 1) < HD
    total = jnp.where(pl.program_id(0) == 0, 0.0, grad_keyval_ref[...])
    outs = []
    for heads, grad_heads in ((pair, turned(grads)), (turned(pair), grads)):
        query = bfloat(jnp.where(left, heads, 0.0))
        grad = bfloat(jnp.where(left, 0.0, grad_heads))
        probs = softmax_rows(matmul_right(query, keyval) + bias)
        grad_probs = matmul_right(grad, keyval)
        inner = jnp.sum(probs * grad_probs, -1, keepdims=True)
        grad_scores = bfloat(probs * (grad_probs - inner))
        outs.append(matmul(grad_scores, keyval))
        total = total + matmul_left(grad_scores, query) + matmul_left(bfloat(probs), grad)
    grad_keyval_ref[...] = total
    grad_query = single(bfloat(jnp.where(left, outs[0], turned(outs[1])))) * HD ** (-0.5)
    grad_query_ref[...] = bfloat(grad_query)


def attend_back(query, keyval, bias, grad_out):
    rows, columns = query.shape
    pair = 2 * HD
    pairs = pl.BlockSpec((rows, pair), lambda i: (0, i))
    return pl.pallas_call(
        attend_back_kernel,
        grid=(columns // pair,),
        in_specs=[pairs, whole_block(keyval.shape), whole_block(bias.shape), pairs],
        out_specs=[pairs, whole_block(keyval.shape)],
        out_shape=[
            jax.ShapeDtypeStruct((rows, columns), jnp.bfloat16),
            jax.ShapeDtypeStruct(keyval.shape, jnp.float32),
        ],
        compiler_params=vmem(48),
        cost_estimate=small_cost(
            flops=10 * rows * columns * keyval.shape[0],
            bytes_accessed=8 * rows * columns,
            transcendentals=rows * columns * keyval.shape[0] // HD,
        ),
    )(query, keyval, bias, grad_out)


def lower_kernel(table_ref, *refs):
    low_ref, square_ref = refs[-2:]
    weights = table_ref[...]
    low_ref[...] = bfloat(weights)
    squares = jnp.sum((weights * weights).reshape(-1, 8, weights.shape[1]), 0)
    square_ref[...] = jnp.where(pl.program_id(0) == 0, 0.0, square_ref[...]) + squares


def lowered(table, low, index, count):
    vocab_here, model = table.shape
    block = row_block(vocab_here, 1024)
    steps = vocab_here // block
    first, last = index * steps // count, (index + 1) * steps // count
    rows = pl.BlockSpec((block, model), lambda i: (i + first, 0))
    return pl.pallas_call(
        lower_kernel,
        grid=(last - first,),
        in_specs=[rows] + ([] if low is None else [pl.BlockSpec(memory_space=pl.ANY)]),
        out_specs=[rows, whole_block((8, model))],
        out_shape=[
            jax.ShapeDtypeStruct(table.shape, jnp.bfloat16),
            jax.ShapeDtypeStruct((8, model), jnp.float32),
        ],
        input_output_aliases={} if low is None else {1: 0},
        compiler_params=vmem(40),
        cost_estimate=small_cost(
            flops=2 * vocab_here * model // count,
            bytes_accessed=6 * vocab_here * model // count,
            transcendentals=0,
        ),
    )(*((table,) if low is None else (table, low)))


def head_stats_kernel(chosen_ref, target_ref, low_ref, stats_ref):
    step = pl.program_id(0)
    rows = low_ref.shape[0]

    @pl.when(step == 0)
    def _():
        stats_ref[...] = jnp.zeros_like(stats_ref)
        stats_ref[0:1, :] = jnp.full((1, stats_ref.shape[1]), MASKED, jnp.float32)

    logits = matmul(low_ref[...], chosen_ref[...])
    places = lax.broadcasted_iota(jnp.int32, logits.shape, 0)
    matches = places == target_ref[...] - step * rows
    before, totals = stats_ref[0:1, :], stats_ref[1:2, :]
    highest = jnp.maximum(before, jnp.max(logits, 0, keepdims=True))
    stats_ref[1:2, :] = totals * jnp.exp(before - highest) + jnp.sum(
        jnp.exp(logits - highest), 0, keepdims=True
    )
    stats_ref[0:1, :] = highest
    stats_ref[2:3, :] = stats_ref[2:3, :] + jnp.sum(
        jnp.where(matches, logits, 0.0), 0, keepdims=True
    )


def head_stats(chosen_across, target_row, low):
    vocab_here, model = low.shape
    slots = chosen_across.shape[1]
    block = row_block(vocab_here, 1024)
    return pl.pallas_call(
        head_stats_kernel,
        grid=(vocab_here // block,),
        in_specs=[
            whole_block(chosen_across.shape),
            whole_block((1, slots)),
            pl.BlockSpec((block, model), lambda i: (i, 0)),
        ],
        out_specs=whole_block((8, slots)),
        out_shape=jax.ShapeDtypeStruct((8, slots), jnp.float32),
        compiler_params=vmem(40),
        cost_estimate=small_cost(
            flops=2 * slots * vocab_here * model,
            bytes_accessed=2 * vocab_here * model,
            transcendentals=slots * vocab_here,
        ),
    )(chosen_across, target_row, low)


def head_rows_kernel(chosen_ref, target_ref, logsum_ref, low_ref, grad_ref):
    step = pl.program_id(0)
    rows = low_ref.shape[0]
    low = low_ref[...]
    logits = matmul_right(chosen_ref[...], low)
    places = lax.broadcasted_iota(jnp.int32, logits.shape, 1) + step * rows
    target = target_ref[...]
    matches = jnp.where(places == target, 1.0, 0.0)
    grads = jnp.where(target != DEAD, jnp.exp(logits - logsum_ref[...]) - matches, 0.0)
    before = jnp.where(step == 0, 0.0, grad_ref[...])
    grad_ref[...] = before + matmul(bfloat(grads), low)


def head_rows(chosen, target_column, logsum_column, low):
    vocab_here, model = low.shape
    slots = chosen.shape[0]
    block = row_block(vocab_here, 1024)
    return pl.pallas_call(
        head_rows_kernel,
        grid=(vocab_here // block,),
        in_specs=[
            whole_block(chosen.shape),
            whole_block((slots, 1)),
            whole_block((slots, 1)),
            pl.BlockSpec((block, model), lambda i: (i, 0)),
        ],
        out_specs=whole_block((slots, model)),
        out_shape=jax.ShapeDtypeStruct((slots, model), jnp.float32),
        compiler_params=vmem(40),
        cost_estimate=small_cost(
            flops=4 * slots * vocab_here * model,
            bytes_accessed=2 * vocab_here * model,
            transcendentals=slots * vocab_here,
        ),
    )(chosen, target_column, logsum_column, low)


def head_table_kernel(first, chosen_ref, across_ref, target_ref, logsum_ref, low_ref, *refs):
    step = pl.program_id(0) + first
    grad_ref = refs[-1]
    rows = low_ref.shape[0]
    logits = matmul(low_ref[...], across_ref[...])
    places = lax.broadcasted_iota(jnp.int32, logits.shape, 0) + step * rows
    target = target_ref[...]
    matches = jnp.where(places == target, 1.0, 0.0)
    grads = jnp.where(target != DEAD, jnp.exp(logits - logsum_ref[...]) - matches, 0.0)
    grad_ref[...] = matmul(bfloat(grads), chosen_ref[...])


def head_table(chosen, chosen_across, target_row, logsum_row, low, grads, index, count):
    vocab_here, model = low.shape
    slots = chosen.shape[0]
    block = row_block(vocab_here, 1024)
    steps = vocab_here // block
    first, last = index * steps // count, (index + 1) * steps // count
    rows = pl.BlockSpec((block, model), lambda i: (i + first, 0))
    return pl.pallas_call(
        functools.partial(head_table_kernel, first),
        grid=(last - first,),
        in_specs=[
            whole_block(chosen.shape),
            whole_block(chosen_across.shape),
            whole_block((1, slots)),
            whole_block((1, slots)),
            rows,
        ]
        + ([] if grads is None else [pl.BlockSpec(memory_space=pl.ANY)]),
        out_specs=rows,
        out_shape=jax.ShapeDtypeStruct(low.shape, jnp.float32),
        input_output_aliases={} if grads is None else {5: 0},
        compiler_params=vmem(48),
        cost_estimate=small_cost(
            flops=4 * slots * vocab_here * model // count,
            bytes_accessed=6 * vocab_here * model // count,
            transcendentals=slots * vocab_here // count,
        ),
    )(*((chosen, chosen_across, target_row, logsum_row, low) + (() if grads is None else (grads,))))


def table_sums_kernel(first, place_ref, starts_ref, ids_ref, order_ref, head_ref, stat_ref, *refs):
    pieces = refs[:8]
    grad_ref, rows_ref, sums_ref, wide_ref = refs[-4:]
    step = pl.program_id(0) + first
    rows, model = head_ref.shape
    room = pieces[0].shape[1]

    @pl.when(pl.program_id(0) == 0)
    def _():
        for side in range(2):
            section = place_ref[1] if side == 0 else 1 - place_ref[1]
            for k in range(4):
                for z in range(4):
                    block = (4 * section + z) * 4 + (place_ref[0] ^ k)
                    row = pl.multiple_of(block * room, 16)
                    wide_ref[pl.ds(row, room), :] = single(pieces[4 * side + k][z])
        sums_ref[...] = jnp.zeros_like(sums_ref)

    grad_ref[...] = head_ref[...]
    start, end = starts_ref[step], starts_ref[step + 1]

    @pl.loop(0, (end - start + 3) // 4)
    def _(i):
        places, values = [], []
        for k in range(4):
            j = jnp.minimum(start + 4 * i + k, end - 1)
            row = wide_ref[pl.ds(order_ref[j], 1), :]
            values.append(jnp.where(start + 4 * i + k < end, row, 0.0))
            places.append(pl.ds(ids_ref[j] - step * rows, 1))
        for place, row in zip(places, values):
            grad_ref[place, :] = grad_ref[place, :] + row

    stats = stat_ref[...]
    columns = jnp.zeros((8, model), jnp.float32)
    scaled = jnp.zeros((8, model), jnp.float32)
    for k in range(rows // LANES):
        part = grad_ref[k * LANES : (k + 1) * LANES, :]
        square = part * part
        mean = jnp.sum(square + SQUARE_EPS, -1, keepdims=True) * (1.0 / model)
        stat = jnp.transpose(jnp.broadcast_to(stats[k : k + 1, :], (LANES, LANES)))
        new = DECAY * stat + (1.0 - DECAY) * mean
        rows_ref[k : k + 1, :] = jnp.transpose(new)[0:1, :]
        columns = columns + jnp.sum((square + SQUARE_EPS).reshape(LANES // 8, 8, model), 0)
        ratio = square * (1.0 / new[:, 0:1])
        scaled = scaled + jnp.sum(ratio.reshape(LANES // 8, 8, model), 0)
    sums_ref[0:8, :] = sums_ref[0:8, :] + columns
    sums_ref[8:16, :] = sums_ref[8:16, :] + scaled


def table_sums(starts, ids, order, pieces, head, row_stat, block, earlier, index, count):
    vocab_here, model = head.shape
    steps = vocab_here // block
    first, last = index * steps // count, (index + 1) * steps // count
    rows = pl.BlockSpec((block, model), lambda i, *_: (i + first, 0))
    stats = pl.BlockSpec((block // LANES, LANES), lambda i, *_: (i + first, 0))
    kept = [] if earlier is None else [pl.BlockSpec(memory_space=pl.ANY)] * 2
    return pl.pallas_call(
        functools.partial(table_sums_kernel, first),
        grid_spec=pltpu.PrefetchScalarGridSpec(
            num_scalar_prefetch=4,
            grid=(last - first,),
            in_specs=[rows, stats]
            + [
                pl.BlockSpec(piece.shape, lambda *_: (0, 0, 0), pipeline_mode=pl.Buffered(1))
                for piece in pieces
            ]
            + kept,
            out_specs=[rows, stats, pl.BlockSpec((16, model), lambda *_: (0, 0))],
            scratch_shapes=[pltpu.VMEM((32 * pieces[0].shape[1], model), jnp.float32)],
        ),
        out_shape=[
            jax.ShapeDtypeStruct(head.shape, jnp.float32),
            jax.ShapeDtypeStruct((vocab_here // LANES, LANES), jnp.float32),
            jax.ShapeDtypeStruct((16, model), jnp.float32),
        ],
        input_output_aliases={} if earlier is None else {14: 0, 15: 1},
        compiler_params=vmem(56),
        cost_estimate=small_cost(
            flops=8 * vocab_here * model // count,
            bytes_accessed=8 * vocab_here * model // count,
            transcendentals=0,
        ),
    )(
        jnp.stack([lax.axis_index("ctx"), lax.axis_index("section")]),
        starts,
        ids,
        order,
        head,
        row_stat.reshape(-1, LANES),
        *pieces,
        *(earlier or ()),
    )


def gelu_slope(values):
    factor = (2.0 / jnp.pi) ** 0.5
    inner = jnp.tanh(factor * (values + 0.044715 * values * values * values))
    slope = factor * (1.0 + 3.0 * 0.044715 * values * values)
    return 0.5 * (1.0 + inner) + 0.5 * values * (1.0 - inner * inner) * slope


def put_together(c, step, pieces, up_ref, down_ref):
    model = up_ref.shape[0]
    columns, packed = pieces[0].shape[:2]
    part, half = model // (8 * columns), packed // 2
    for k in range(4):
        for z in range(2 * columns):
            piece = pieces[2 * k + z // columns]
            rows = pl.ds(pl.multiple_of((4 * z + (c ^ k)) * part, 16), part)
            place = pl.ds(pl.multiple_of(step * part, 16), part)
            up_ref[rows, :] = piece[z % columns, place, :]
    for side in range(2):

        @pl.when(step == side)
        def _():
            for k in range(4):
                for z in range(columns):
                    rows = pl.ds(pl.multiple_of((4 * z + (c ^ k)) * half, 16), half)
                    down_ref[rows, :] = pieces[2 * k + side][z, half : 2 * half, :]


def half_specs(hidden):
    if not isinstance(hidden, tuple):
        grid = hidden.reshape((4, 4) + hidden.shape[1:])
        shape = (2, None) + hidden.shape[1:]
        specs = [
            pl.BlockSpec(shape, lambda *_, k=k, side=side: (side, k, 0, 0))
            for k in range(4)
            for side in range(2)
        ]
        return jnp.zeros(1, jnp.int32), [grid] * 8, specs
    arrays, specs = [], []
    for piece in hidden:
        for side in range(2):
            array = piece[side] if isinstance(piece, tuple) else piece
            shape = (2,) + array.shape[1:]
            place = 0 if isinstance(piece, tuple) else side
            arrays.append(array)
            specs.append(pl.BlockSpec(shape, lambda *_, place=place: (place, 0, 0)))
    return lax.axis_index("ctx").reshape(1), arrays, specs


def hidden_kernel(place_ref, both_ref, *refs):
    *pieces, upper_ref, partial_ref, up_ref, down_ref = refs
    step = pl.program_id(0)
    put_together(place_ref[0], step, pieces, up_ref, down_ref)
    upper = matmul(both_ref[...], up_ref[...])
    upper_ref[...] = upper
    before = jnp.where(step == 0, 0.0, partial_ref[...])
    partial_ref[...] = before + matmul(bfloat(gelu_tanh(upper)), down_ref[...])


def hidden_forward(both, hidden):
    rows, model = both.shape
    blocks = lax.axis_size("dp") * lax.axis_size("ctx")
    if not by_fours():
        up, down = hidden_weights(hidden)
        upper = matmul(both, up)
        return upper, matmul(bfloat(gelu_tanh(upper)), down)
    packed = (hidden[0] if isinstance(hidden, tuple) else hidden).shape[1]
    size = blocks * packed * model
    steps = size // (2 * model * model)
    square = pltpu.VMEM((model, model), jnp.bfloat16)
    place, arrays, specs = half_specs(hidden)
    return pl.pallas_call(
        hidden_kernel,
        grid_spec=pltpu.PrefetchScalarGridSpec(
            num_scalar_prefetch=1,
            grid=(steps,),
            in_specs=[whole_block(both.shape)] + specs,
            out_specs=[pl.BlockSpec((rows, model), lambda j, _: (0, j)), whole_block(both.shape)],
            scratch_shapes=[square, square],
        ),
        out_shape=[
            jax.ShapeDtypeStruct((rows, steps * model), jnp.float32),
            jax.ShapeDtypeStruct((rows, model), jnp.float32),
        ],
        compiler_params=vmem(48),
        cost_estimate=small_cost(
            flops=2 * rows * size,
            bytes_accessed=2 * size + 8 * rows * steps * model,
            transcendentals=rows * steps * model,
        ),
    )(place, both, *arrays)


def hidden_back_kernel(place_ref, both_ref, upper_ref, grad_ref, *refs):
    *pieces, partial_ref, grads_ref, up_ref, down_ref = refs
    step = pl.program_id(0)
    model = both_ref.shape[1]
    blocks, half = grads_ref.shape[0], grads_ref.shape[1] // 2
    rows, per_step = model // blocks, model // half
    put_together(place_ref[0], step, pieces, up_ref, down_ref)
    both, upper, grad = both_ref[...], upper_ref[...], grad_ref[...]
    active = bfloat(gelu_tanh(upper))
    grad_upper = bfloat(matmul_right(grad, down_ref[...]) * gelu_slope(upper))
    before = jnp.where(step == 0, 0.0, partial_ref[...])
    partial_ref[...] = before + matmul_right(grad_upper, up_ref[...])
    grad_up = bfloat(matmul_left(both, grad_upper)).reshape(blocks, rows, model)
    grads_ref[:, pl.ds(pl.multiple_of(step * rows, 16), rows), :] = grad_up
    grad_down = bfloat(matmul_left(active, grad)).reshape(per_step, half, model)
    grads_ref[pl.ds(step * per_step, per_step), half : 2 * half, :] = grad_down


def hidden_backward(both, upper, grad_both, hidden):
    rows, model = both.shape
    blocks = lax.axis_size("dp") * lax.axis_size("ctx")
    if not by_fours():
        up, down = hidden_weights(hidden)
        active = bfloat(gelu_tanh(upper))
        grad_upper = bfloat(matmul_right(grad_both, down) * gelu_slope(upper))
        grad_up, grad_down = matmul_left(both, grad_upper), matmul_left(active, grad_both)
        parts = [
            grad_up[:, k : k + model].reshape(blocks, -1, model)
            for k in range(0, grad_up.shape[1], model)
        ]
        packed = jnp.concatenate(parts + [grad_down.reshape(blocks, -1, model)], 1)
        return matmul_right(grad_upper, up), bfloat(packed)
    packed = (hidden[0] if isinstance(hidden, tuple) else hidden).shape[1]
    size = blocks * packed * model
    steps = size // (2 * model * model)
    square = pltpu.VMEM((model, model), jnp.bfloat16)
    grads = (blocks, packed, model)
    place, arrays, specs = half_specs(hidden)
    return pl.pallas_call(
        hidden_back_kernel,
        grid_spec=pltpu.PrefetchScalarGridSpec(
            num_scalar_prefetch=1,
            grid=(steps,),
            in_specs=[
                whole_block(both.shape),
                pl.BlockSpec((rows, model), lambda j, _: (0, j)),
                whole_block(both.shape),
            ]
            + specs,
            out_specs=[whole_block(both.shape), whole_block(grads)],
            scratch_shapes=[square, square],
        ),
        out_shape=[
            jax.ShapeDtypeStruct((rows, model), jnp.float32),
            jax.ShapeDtypeStruct(grads, jnp.bfloat16),
        ],
        compiler_params=vmem(56),
        cost_estimate=small_cost(
            flops=4 * rows * size,
            bytes_accessed=4 * size + 4 * rows * steps * model,
            transcendentals=2 * rows * steps * model,
        ),
    )(place, both, upper, grad_both, *arrays)


def hidden_weights(hidden):
    blocks, packed, model = hidden.shape
    part = model // blocks
    parts = [hidden[:, k : k + part].reshape(model, model) for k in range(0, packed // 2, part)]
    return jnp.concatenate(parts, 1), hidden[:, packed // 2 :].reshape(-1, model)


def both_rows(values):
    return jnp.concatenate([values, swap(values)])


def own_rows(partial, pieces=1):
    rows = partial.shape[0] // 2
    return partial[:rows] + swap(partial[rows:])


def factored_sums(weight, gradient, row_stat):
    square = gradient * gradient + SQUARE_EPS
    rows_new = DECAY * row_stat + (1.0 - DECAY) * jnp.mean(square, -1)
    columns = jnp.sum(square, 0)
    scaled = jnp.sum(gradient * gradient / rows_new[:, None], 0)
    return rows_new, columns, scaled, jnp.sum(rows_new), jnp.sum(weight * weight)


def factored_new(weight, gradient, rows_new, col_stat, sums, row_count):
    columns, scaled, rows_sum, weight_sum = sums
    entries = row_count * weight.shape[1]
    cols_new = DECAY * col_stat + (1.0 - DECAY) * columns / row_count
    mean_rows = rows_sum / row_count
    update_sum = mean_rows * jnp.sum(scaled / cols_new)
    clipping = jnp.maximum(1.0, jnp.sqrt(update_sum / entries))
    size = jnp.maximum(SCALE_FLOOR, jnp.sqrt(weight_sum / entries))
    update = gradient * lax.rsqrt(rows_new[:, None] * cols_new[None, :] / mean_rows)
    return cols_new, weight - RELATIVE_RATE * size * (update / clipping)


def distinct_slots(ids, vocab_here):
    count = ids.shape[1]
    shard = ids // vocab_here
    earlier = jnp.arange(count)[None, :] < jnp.arange(count)[:, None]
    same = ids[:, :, None] == ids[:, None, :]
    first = ~jnp.any(same & earlier, -1)
    mates = (shard[:, :, None] == shard[:, None, :]) & first[:, None, :] & earlier
    rank = jnp.sum(mates.astype(jnp.int32), -1)
    slot = jnp.sum(jnp.where(same & first[:, None, :], rank[:, None, :], 0), -1)
    return slot, shard


def asked_ids(local, slot, here, room):
    places = jnp.arange(room, dtype=jnp.int32)[None, :, None]
    matches = (slot[:, None, :] == places) & here[:, None, :]
    return jnp.min(jnp.where(matches, local[:, None, :], 1 << 30), -1)


def picked_kernel(ids_ref, table_ref, out_ref, rows_ref, sem):
    count = rows_ref.shape[0]

    @pl.loop(0, count // 8)
    def _(i):
        for k in range(8):
            row = table_ref.at[pl.ds(ids_ref[8 * i + k], 1), :]
            pltpu.make_async_copy(row, rows_ref.at[pl.ds(8 * i + k, 1), :], sem).start()

    pltpu.make_async_copy(table_ref.at[pl.ds(0, count), :], rows_ref, sem).wait()
    out_ref[...] = bfloat(rows_ref[...])


def picked_rows(ids, table):
    shape = (ids.shape[0], table.shape[1])
    return pl.pallas_call(
        picked_kernel,
        grid_spec=pltpu.PrefetchScalarGridSpec(
            num_scalar_prefetch=1,
            grid=(1,),
            in_specs=[pl.BlockSpec(memory_space=pl.ANY)],
            out_specs=whole_block(shape),
            scratch_shapes=[pltpu.VMEM(shape, jnp.float32), pltpu.SemaphoreType.DMA],
        ),
        out_shape=jax.ShapeDtypeStruct(shape, jnp.bfloat16),
        compiler_params=vmem(24),
        cost_estimate=small_cost(
            flops=0, bytes_accessed=4 * shape[0] * shape[1], transcendentals=0
        ),
    )(ids, table)


def spilled_inside(ids, slot, room, vocab_here):
    local = ids - lax.axis_index("dp") * vocab_here
    return local, (local >= 0) & (local < vocab_here) & (slot >= room)


def spilled_rows(token_ids, slot, room, table):
    ids = at(token_ids, lax.axis_index("section"), 0)
    local, inside = spilled_inside(ids, slot, room, table.shape[0])
    rows = jnp.take(table, jnp.clip(local, 0, table.shape[0] - 1), axis=0)
    rows = jnp.where(inside[..., None], bfloat(rows), 0)
    return single(lax.psum_scatter(rows, "dp", scatter_dimension=0))


def spilled_grads(token_ids, slot, room, grad_start, vocab_here):
    ids = at(token_ids, lax.axis_index("section"), 0)
    local, inside = spilled_inside(ids, slot, room, vocab_here)
    column = lax.all_gather(grad_start, "dp")
    total = jax.ops.segment_sum(
        single(column.reshape(-1, column.shape[-1])),
        jnp.where(inside, local, vocab_here).reshape(-1),
        num_segments=vocab_here,
    )
    return single(lax.psum(bfloat(total), ("section", "ctx")))


def put_rows(ref, row, vector):
    for k in range(vector.shape[1] // LANES):
        ref[row + k : row + k + 1, :] = vector[:, k * LANES : (k + 1) * LANES]


def got_rows(ref, row, width):
    count = width // LANES
    return jnp.concatenate([ref[row + k : row + k + 1, :] for k in range(count)], 1)


def total(values):
    return jnp.sum(jnp.sum(values, 0, keepdims=True), 1, keepdims=True)


def pair(first, second):
    lanes = lax.broadcasted_iota(jnp.int32, (first.shape[0], LANES), 1)
    return jnp.where(lanes == 0, first, jnp.where(lanes == 1, second, 0.0))


def sum_rows(widths):
    starts = [0]
    for width in widths:
        starts.append(starts[-1] + 2 * width // LANES)
    scalars = -(-starts[-1] // 8) * 8
    return starts, scalars, scalars + 8


def layer_sums_kernel(*refs):
    grads, weights, stats = refs[:5], refs[5:10], refs[10:15]
    first_ref, second_ref, table_rows_ref, square_ref = refs[15:19]
    packed_ref, *new_refs = refs[19:]
    model = first_ref.shape[1]
    starts, scalars, table = sum_rows([ref.shape[1] for ref in grads[:4]])
    packed_ref[...] = jnp.zeros_like(packed_ref)
    for k in range(4):
        grad, weight = grads[k][...], weights[k][...]
        square = grad * grad
        full = square + SQUARE_EPS
        mean = jnp.sum(full, -1, keepdims=True) * (1.0 / grad.shape[1])
        new = DECAY * stats[k][...] + (1.0 - DECAY) * mean
        new_refs[k][...] = new
        count = grad.shape[1] // LANES
        put_rows(packed_ref, starts[k], jnp.sum(full, 0, keepdims=True))
        scaled = jnp.sum(square * (1.0 / new), 0, keepdims=True)
        put_rows(packed_ref, starts[k] + count, scaled)
        packed_ref[scalars + k : scalars + k + 1, :] = pair(total(new), total(weight * weight))
    grad, weight = grads[4][...], weights[4][...]
    new = DECAY * stats[4][...] + (1.0 - DECAY) * (grad * grad + SQUARE_EPS)
    new_refs[4][...] = new
    update = grad * lax.rsqrt(new)
    packed_ref[scalars + 4 : scalars + 8, :] = pair(
        jnp.sum(weight * weight, 1, keepdims=True), jnp.sum(update * update, 1, keepdims=True)
    )
    sums = first_ref[...] + second_ref[...]
    put_rows(packed_ref, table, jnp.sum(sums[0:8], 0, keepdims=True))
    put_rows(packed_ref, table + model // LANES, jnp.sum(sums[8:16], 0, keepdims=True))
    place = table + 2 * model // LANES
    packed_ref[place : place + 1, :] = pair(total(table_rows_ref[...]), total(square_ref[...]))


def layer_sums(grads, weights, stats, sums_first, sums_second, table_rows_new, squares):
    shapes = [stat.shape for stat in stats]
    _, _, table = sum_rows([grad.shape[1] for grad in grads[:4]])
    height = table + -(-(2 * sums_first.shape[1] // LANES + 1) // 8) * 8
    return pl.pallas_call(
        layer_sums_kernel,
        out_shape=[jax.ShapeDtypeStruct((height, LANES), jnp.float32)]
        + [jax.ShapeDtypeStruct(shape, jnp.float32) for shape in shapes],
        compiler_params=vmem(40),
        cost_estimate=small_cost(flops=0, bytes_accessed=1 << 22, transcendentals=0),
    )(*grads, *weights, *stats, sums_first, sums_second, table_rows_new, squares)


def factored_sizes(ref, start, scalar, col_stat, row_count):
    width = col_stat.shape[1]
    columns = got_rows(ref, start, width)
    scaled = got_rows(ref, start + width // LANES, width)
    rows_sum, weight_sum = ref[scalar : scalar + 1, 0:1], ref[scalar : scalar + 1, 1:2]
    new = DECAY * col_stat + (1.0 - DECAY) * columns * (1.0 / row_count)
    mean_rows = rows_sum * (1.0 / row_count)
    entries = row_count * width
    update_sum = mean_rows * jnp.sum(scaled / new, 1, keepdims=True)
    clipping = jnp.maximum(1.0, jnp.sqrt(update_sum * (1.0 / entries)))
    size = jnp.maximum(SCALE_FLOOR, jnp.sqrt(weight_sum * (1.0 / entries)))
    return new, mean_rows, RELATIVE_RATE * size / clipping


def layer_new_kernel(counts, totals_ref, *refs):
    grads, weights, rows, cols = refs[:5], refs[5:10], refs[10:15], refs[15:19]
    new_refs, col_refs = refs[19:24], refs[24:28]
    starts, scalars, _ = sum_rows([ref.shape[1] for ref in grads[:4]])
    for k in range(4):
        cols_new, mean_rows, rate = factored_sizes(
            totals_ref, starts[k], scalars + k, cols[k][...], counts[k]
        )
        col_refs[k][...] = cols_new
        scale = lax.rsqrt(rows[k][...] * cols_new / mean_rows)
        new_refs[k][...] = weights[k][...] - rate * (grads[k][...] * scale)
    model = counts[4]
    squares = totals_ref[scalars + 4 : scalars + 8, 0:1]
    updates = totals_ref[scalars + 4 : scalars + 8, 1:2]
    clipping = jnp.maximum(1.0, jnp.sqrt(updates * (1.0 / model)))
    size = jnp.maximum(SCALE_FLOOR, jnp.sqrt(squares * (1.0 / model)))
    update = grads[4][...] * lax.rsqrt(rows[4][...])
    new_refs[4][...] = weights[4][...] - RELATIVE_RATE * size / clipping * update


def layer_new(totals, grads, weights, rows, cols, counts):
    outs = [grad.shape for grad in grads] + [col.shape for col in cols]
    return pl.pallas_call(
        functools.partial(layer_new_kernel, counts),
        out_shape=[jax.ShapeDtypeStruct(shape, jnp.float32) for shape in outs],
        compiler_params=vmem(40),
        cost_estimate=small_cost(flops=0, bytes_accessed=1 << 22, transcendentals=0),
    )(totals, *grads, *weights, *rows, *cols)


def table_new_kernel(start, row_count, totals_ref, table_ref, grad_ref, rows_ref, cols_ref, *refs):
    new_ref, col_ref = refs
    scalar = start + 2 * cols_ref.shape[1] // LANES
    cols_new, mean_rows, rate = factored_sizes(totals_ref, start, scalar, cols_ref[...], row_count)
    col_ref[...] = cols_new
    across = rate * lax.rsqrt(cols_new)
    down = lax.rsqrt(rows_ref[...] / mean_rows)
    for k in range(rows_ref.shape[0]):
        place = slice(k * LANES, (k + 1) * LANES)
        scale = jnp.transpose(jnp.broadcast_to(down[k : k + 1, :], (LANES, LANES)))[:, 0:1]
        new_ref[place, :] = table_ref[place, :] - grad_ref[place, :] * scale * across


def table_new(totals, start, table, grad, rows_new, cols, row_count):
    vocab_here, model = table.shape
    block = row_block(vocab_here, 1024)
    rows = pl.BlockSpec((block, model), lambda i: (i, 0))
    return pl.pallas_call(
        functools.partial(table_new_kernel, start, row_count),
        grid=(vocab_here // block,),
        in_specs=[
            whole_block(totals.shape),
            rows,
            rows,
            pl.BlockSpec((block // LANES, LANES), lambda i: (i, 0)),
            whole_block(cols.shape),
        ],
        out_specs=[rows, whole_block(cols.shape)],
        out_shape=[
            jax.ShapeDtypeStruct(table.shape, jnp.float32),
            jax.ShapeDtypeStruct(cols.shape, jnp.float32),
        ],
        compiler_params=vmem(48),
        cost_estimate=small_cost(
            flops=4 * vocab_here * model,
            bytes_accessed=12 * vocab_here * model,
            transcendentals=0,
        ),
    )(totals, table, grad, rows_new, cols)


def body(
    token_ids,
    doc_lengths,
    picks,
    targets,
    table,
    table_rows,
    table_cols,
    attention_in,
    attention_in_rows,
    attention_in_cols,
    attention_out,
    attention_out_rows,
    attention_out_cols,
    hidden_in,
    hidden_in_rows,
    hidden_in_cols,
    hidden_out,
    hidden_out_rows,
    hidden_out_cols,
    gains,
    gains_stat,
):
    section = lax.axis_index("section")
    first = section == 0
    z, c = lax.axis_index("dp"), lax.axis_index("ctx")
    z_count, c_count = lax.axis_size("dp"), lax.axis_size("ctx")
    blocks = z_count * c_count
    model = table.shape[1]
    part = attention_in.shape[1]
    units = hidden_in.shape[2]
    half = units // (2 * blocks)
    wide = attention_in.shape[2]
    local_len = token_ids.shape[2]
    slots = picks.shape[2]
    vocab_here = table.shape[0]
    vocab_base = z * vocab_here

    low_in = bfloat(attention_in[0])
    low_out = jnp.concatenate(
        [bfloat(attention_out[0]), bfloat(gains[0]).T, jnp.zeros((part, wide - model - 4), jnp.bfloat16)], 1
    )
    barrier = lax.optimization_barrier
    at_p = jnp.concatenate(
        mine_first(
            jnp.where(first, low_in, low_out), swap(jnp.where(first, low_out, low_in))
        )
    )
    at_p, hidden_in_now, hidden_out_now = barrier((at_p, hidden_in, hidden_out))
    at_z = column_pieces(at_p)
    low_up = bfloat(hidden_in_now[0]).reshape(part, blocks, 2, half)
    low_down = bfloat(hidden_out_now[0])

    def unit_half(index):
        up = at(low_up, index, 2).reshape(part, -1, model)
        down = lax.dynamic_slice_in_dim(low_down, index * half, half, 0)
        return jnp.concatenate([up[:, k] for k in range(up.shape[1])] + [down])

    hid_p0, hid_p1 = mine_first(unit_half(section), swap(unit_half(1 - section)))

    room = local_len * 3 // 128 * 16

    hidden_w0 = lax.all_gather(hid_p0, BLOCKS, axis=0)

    if by_fours():
        slot, shard = distinct_slots(at(token_ids, section, 0), vocab_here)
        asked = asked_ids(at(token_ids, section, 0) - vocab_base, slot, shard == z, room)
        spilled = jnp.max(slot) >= room
        wanted = jnp.minimum(asked, vocab_here - 1).reshape(-1)
        place = at(jnp.where(slot < room, shard * room + slot, -1), z, 0)
        placed = bfloat(
            single(place[:, None] == jnp.arange(z_count * room, dtype=jnp.int32)[None, :])
        )
        notes = [asked.reshape(-1), spilled.astype(jnp.int32)[None], targets.reshape(-1)]
        notes = jnp.concatenate(notes)
        notes = jnp.stack(mine_first(notes, swap(notes)))
        x, y = plane_bits()
        beside = cross(notes, "ctx", 1)
        notes = jnp.stack([jnp.where(x == 0, notes, beside), jnp.where(x == 0, beside, notes)])
        above = cross(notes, "ctx", 2)
        notes = jnp.concatenate([jnp.where(y == 0, notes, above), jnp.where(y == 0, above, notes)])
        looked = picked_rows(after(wanted, at_p), table).reshape(z_count, room, model)
    else:
        my_ids = at(token_ids, section, 0) - vocab_base
        inside = (my_ids >= 0) & (my_ids < vocab_here)
        looked = jnp.take(table, jnp.clip(my_ids, 0, vocab_here - 1), axis=0)
        looked = jnp.where(inside[..., None], bfloat(looked), 0)
        notes = []

    at_z, hid_p1, looked, notes, table_now = barrier((at_z, hid_p1, looked, notes, table))
    at_c = column_join(at_p, at_z)
    at_n = plane_near(at_c)
    start_pieces = row_pieces(looked)
    low_first, square_first = lowered(table_now, None, 0, 3)
    at_n, start_pieces, low_first, hid_p1 = barrier((at_n, start_pieces, low_first, hid_p1))
    at_f = plane_far(at_n)
    table_low, square_second = lowered(table, low_first, 1, 3)
    at_f, table_low, at_c = barrier((at_f, table_low, at_c))
    at_w = plane_list(at_c, at_n, at_f)
    at_o = swap(at_w)
    table_low, square_third = lowered(table, table_low, 2, 3)
    at_o, table_low, hid_p1 = barrier((at_o, table_low, hid_p1))
    hid_z1 = column_pieces(hid_p1)
    if by_fours():
        target_notes = notes[:, 0, asked.size + 1 :]
        asked_all = notes[..., : asked.size].reshape(c_count, 2, z_count, room)
        local = jnp.minimum(asked_all.transpose(1, 2, 0, 3).reshape(-1), vocab_here)
        order = jnp.arange(local.shape[0], dtype=jnp.int32)
        local, order = lax.sort((local, order), num_keys=1)
        block = row_block(vocab_here, 1024)
        edges = jnp.arange(vocab_here // block + 1, dtype=jnp.int32) * block
        starts = jnp.sum((local[None, :] < edges[:, None]).astype(jnp.int32), 1)
    else:
        local = order = starts = notes
    in0, out0, gains0 = attention_weights(at_w, at_o, model, 0)
    if by_fours():
        spilled = jnp.max(notes[..., asked.size]) > 0
        found = column_join(at(looked, z, 0), start_pieces)
        start = matmul(placed, found.reshape(-1, model))
        start = start + lax.cond(
            spilled,
            lambda: spilled_rows(token_ids, slot, room, table),
            lambda: jnp.zeros_like(start),
        )
    else:
        target_notes = lax.all_gather(targets, "ctx")
        start = row_sum(looked, start_pieces)
    lengths = at(doc_lengths, section, 0)[0]
    my_picks = at(picks, section, 0)[0]

    places = c * local_len + jnp.arange(local_len, dtype=jnp.int32)
    reach = earlier_count(local_len)
    key_places = (c - reach) * local_len + jnp.arange((reach + 1) * local_len, dtype=jnp.int32)
    bias = pair_bias(lengths, places, key_places)
    pick_bias = pair_bias(lengths, c * local_len + jnp.maximum(my_picks, 0), key_places)
    onehot = (my_picks[:, None] == jnp.arange(local_len, dtype=jnp.int32)[None, :]).astype(
        jnp.bfloat16
    )

    normed0 = bfloat(layer_norm(start, gains0[0], gains0[1]))
    mixed_in = matmul(normed0, in0)
    query0 = bfloat(mixed_in[:, :model] * HD ** (-0.5))
    keyval0, query0, local, order, starts = barrier(
        (bfloat(mixed_in[:, model:]), query0, local, order, starts)
    )
    keyval0, query0 = barrier((key_rows(keyval0), query0))
    attended0 = attend(query0, keyval0, bias)
    mixed0 = start + matmul(attended0, out0)
    normed_two0 = bfloat(layer_norm(mixed0, gains0[2], gains0[3]))
    hid_z1, mixed0, normed_two0 = barrier((hid_z1, mixed0, normed_two0))
    hid_c1 = column_join(hid_p1, hid_z1)
    both0, hid_c1 = barrier((both_rows(normed_two0), hid_c1))
    hid_n1 = plane_near_half(hid_c1, 0)
    upper0, partial = hidden_forward(both0, hidden_w0)
    in1, out1, gains1 = attention_weights(at_w, at_o, model, 1)
    hid_n1, partial, in1, out1, hid_c1 = barrier((hid_n1, partial, in1, out1, hid_c1))
    hid_m1 = plane_near_half(hid_c1, 1)
    result0 = mixed0 + own_rows(partial)

    inputs1_low = bfloat(result0)
    inputs1 = single(inputs1_low)
    normed1 = bfloat(layer_norm(inputs1, gains1[0], gains1[1]))
    keyval1 = bfloat(matmul(normed1, in1[:, model:]))
    picked_normed = bfloat(matmul(onehot, normed1))
    picked = matmul(onehot, inputs1_low)
    query1 = bfloat(matmul(picked_normed, in1[:, :model]) * HD ** (-0.5))
    keyval1, query1 = barrier((keyval1, query1))
    keyval1, hid_n1, hid_m1 = barrier((key_rows(keyval1), hid_n1, hid_m1))
    hid_f1 = plane_far_half(hid_n1, hid_m1)
    hidden_w1 = plane_halves(hid_c1, (hid_n1, hid_m1), hid_f1)
    all_targets = target_notes.reshape((c_count,) + targets.shape).transpose(1, 2, 0, 3).reshape(-1)
    heads1 = query1.reshape(slots, -1, HD).transpose(1, 0, 2).reshape(-1, HD)
    heads1 = jnp.concatenate([heads1, jnp.zeros_like(heads1)], 1)
    pick_bias = jnp.tile(pick_bias, (model // HD, 1))

    def side_by_side(heads):
        return heads.reshape(-1, slots, HD).transpose(1, 0, 2).reshape(slots, model)

    attended1 = side_by_side(attend(heads1, keyval1, pick_bias)[:, :HD])
    mixed1 = picked + matmul(attended1, out1)
    normed_two1 = bfloat(layer_norm(mixed1, gains1[2], gains1[3]))
    both1 = both_rows(normed_two1)
    upper1, partial = hidden_forward(both1, hidden_w1)
    result1 = mixed1 + own_rows(partial)

    chosen_mine = gather_blocks(bfloat(result1)).reshape(-1, model)
    chosen = jnp.concatenate(mine_first(chosen_mine, swap(chosen_mine)))
    live = all_targets >= 0
    local_target = jnp.where(live, all_targets - vocab_base, DEAD)
    across = chosen.T
    stats = head_stats(across, local_target[None], table_low)

    def combine(one, two):
        top = jnp.maximum(one[0], two[0])
        both = one[1] * jnp.exp(one[0] - top) + two[1] * jnp.exp(two[0] - top)
        return jnp.stack([top, both, one[2] + two[2]])

    if by_fours():
        stats = stats[:3]
        one, two, three = (cross(stats, "dp", k) for k in (1, 2, 3))
        stats = combine(combine(stats, one), combine(two, three))
    else:
        stats = lax.scan(
            lambda total, share: (combine(total, share), None),
            jnp.stack([jnp.full_like(stats[0], MASKED), 0 * stats[0], 0 * stats[0]]),
            lax.all_gather(stats, "dp"),
        )[0]
    logsum = stats[0] + jnp.log(stats[1])
    loss_sum = jnp.sum(jnp.where(live, logsum - stats[2], 0.0))
    loss_count = jnp.sum(single(live))

    def own_slots(values):
        shape = (2, z_count, c_count, slots) + values.shape[1:]
        return at(at(values.reshape(shape), section, 0), c, 1).reshape((-1,) + values.shape[1:])

    grad_chosen = head_rows(
        own_slots(chosen), own_slots(local_target)[:, None], own_slots(logsum)[:, None], table_low
    )
    grad_result1 = scatter_rows(grad_chosen.reshape(z_count, slots, model))

    def attention_grads(grad_in, grad_out, grad_gains):
        grad_out = jnp.concatenate(
            [
                bfloat(grad_out),
                bfloat(grad_gains).T,
                jnp.zeros((model, wide - model - 4), jnp.bfloat16),
            ],
            1,
        )
        grad_in = bfloat(grad_in)
        return jnp.where(first, grad_in, grad_out), jnp.where(first, grad_out, grad_in)

    def attention_sum(kept, sent):
        return bfloat(single(kept) + single(sent)).reshape(blocks, part, wide)

    low = bfloat(grad_result1)
    partial, hidden_grads1 = hidden_backward(both1, upper1, both_rows(low), hidden_w1)
    hidden1 = scattered(hidden_grads1)
    _, pull = jax.vjp(layer_norm, mixed1, gains1[2], gains1[3])
    grad_mixed1, grad_gain2, grad_shift2 = pull(own_rows(partial))
    grad_mixed1 = grad_mixed1 + grad_result1
    grad_low = bfloat(grad_mixed1)
    grad_out1 = matmul_left(attended1, grad_low)
    grad_heads = bfloat(matmul_right(grad_low, out1)).reshape(slots, -1, HD)
    grad_heads = grad_heads.transpose(1, 0, 2).reshape(-1, HD)
    grad_heads = jnp.concatenate([grad_heads, jnp.zeros_like(grad_heads)], 1)
    grad_query, grad_keyval = attend_back(heads1, keyval1, pick_bias, grad_heads)
    grad_query = side_by_side(grad_query[:, :HD])
    grad_keyval = key_rows_sum(grad_keyval, key_rows_back(grad_keyval, local_len), local_len)
    grad_in1 = jnp.concatenate(
        [matmul_left(picked_normed, grad_query), matmul_left(normed1, grad_keyval)], 1
    )
    spread = jnp.dot(
        single(onehot).T,
        jnp.concatenate([matmul_right(grad_query, in1[:, :model]), grad_mixed1], 1),
        precision=lax.Precision.HIGHEST,
    )
    grad_normed = matmul_right(grad_keyval, in1[:, model:]) + spread[:, :model]
    _, pull = jax.vjp(layer_norm, inputs1, gains1[0], gains1[1])
    grad_inputs1, grad_gain1, grad_shift1 = pull(grad_normed)
    grad_result0 = single(bfloat(grad_inputs1 + spread[:, model:]))
    grad_gains1 = jnp.stack([grad_gain1, grad_shift1, grad_gain2, grad_shift2])
    kept1, sent1 = attention_grads(grad_in1, grad_out1, grad_gains1)

    low = bfloat(grad_result0)
    partial, hidden_grads0 = hidden_backward(both0, upper0, both_rows(low), hidden_w0)
    ups, downs = (0, 2 * part), (2 * part, half)
    partial, hidden_grads0, sent1 = barrier((own_rows(partial), hidden_grads0, swap(sent1)))
    up_s = half_first(hidden_grads0, ups) if by_fours() else ()
    _, pull = jax.vjp(layer_norm, mixed0, gains0[2], gains0[3])
    grad_mixed0, grad_gain2, grad_shift2 = pull(partial)
    grad_mixed0 = grad_mixed0 + grad_result0
    grad_low = bfloat(grad_mixed0)
    grad_out0 = matmul_left(attended0, grad_low)
    grad_query, grad_keyval = attend_back(
        query0, keyval0, bias, bfloat(matmul_right(grad_low, out0))
    )
    up_s, grad_query, grad_keyval = barrier((up_s, grad_query, grad_keyval))
    returned, hidden_grads0 = barrier((key_rows_back(grad_keyval, local_len), hidden_grads0))
    if by_fours():
        down_s = half_first(hidden_grads0, downs)
        up_k, up_h = half_kept(hidden_grads0, ups, up_s)
    grad_keyval = key_rows_sum(grad_keyval, returned, local_len)
    grad_mixed_in = jnp.concatenate([grad_query, grad_keyval], 1)
    grad_in0 = matmul_left(normed0, grad_mixed_in)
    _, pull = jax.vjp(layer_norm, start, gains0[0], gains0[1])
    grad_start, grad_gain1, grad_shift1 = pull(matmul_right(grad_mixed_in, in0))
    grad_start = bfloat(grad_start + grad_mixed0)
    grad_gains0 = jnp.stack([grad_gain1, grad_shift1, grad_gain2, grad_shift2])
    kept0, sent0 = attention_grads(grad_in0, grad_out0, grad_gains0)
    def head_part(grads, index, count):
        return head_table(
            chosen, across, local_target[None], logsum[None], table_low, grads, index, count
        )

    table_square = square_first + square_second + square_third
    if by_fours():
        sent = bfloat(matmul_left(placed, grad_start)).reshape(z_count, room, model)
        row_z = row_pieces(sent)
        chosen = after(chosen, sent)
        grad_head = head_part(None, 0, 3)
        row_z, grad_head, down_s, up_h = barrier((row_z, grad_head, down_s, up_h))
        column = column_join(at(sent, z, 0), row_z)
        other = swap(column)
        near = plane_near(column)
        up_t = half_send(up_h)
        down_k, down_h = half_kept(hidden_grads0, downs, down_s)
        grad_head = head_part(grad_head, 1, 3)
        near, grad_head, up_t, other, down_h, hidden1 = barrier(
            (near, grad_head, up_t, other, down_h, hidden1)
        )
        far = plane_far(near)
        up_v = half_column(up_k, up_t)
        up_q = row_pieces(up_v)
        grad_head = head_part(grad_head, 2, 3)
        grad_head = lax.while_loop(
            lambda carry: carry[0] < spilled.astype(jnp.int32),
            lambda carry: (
                carry[0] + 1,
                carry[1] + spilled_grads(token_ids, slot, room, grad_start, vocab_here),
            ),
            (jnp.zeros((), jnp.int32), grad_head),
        )[1]
        far, grad_head, down_h = barrier((far, grad_head, down_h))
        far = jnp.concatenate(far)
        others = swap((*near, far))
        down_t = half_send(down_h)
        attention_both = jnp.concatenate(
            [attention_sum(kept0, swap(sent0)), attention_sum(kept1, sent1)], 1
        )
        others, down_t, up_q, attention_both = barrier((others, down_t, up_q, attention_both))
        down_v = half_column(down_k, down_t)
        down_q = row_pieces(down_v)
        every = (0, 2 * part)
        at_s = half_first(attention_both, every)
        hidden0 = row_sum(up_v, up_q)
        pieces = (column, *near, far, other, *others)
        parts = (starts, local, order, pieces, grad_head, table_rows, block)
        grad_table, rows_new, sums_first = table_sums(*parts, None, 0, 2)
        down_q, at_s, grad_table, rows_new = barrier((down_q, at_s, grad_table, rows_new))
        at_k, at_h = half_kept(attention_both, every, at_s)
        at_t = half_send(at_h)
        grad_table, rows_new, sums_second = table_sums(*parts, (grad_table, rows_new), 1, 2)
        at_t, grad_table, rows_new = barrier((at_t, grad_table, rows_new))
        at_v = half_column(at_k, at_t)
        attention = row_sum(at_v, row_pieces(at_v))
        hidden0 = jnp.concatenate([hidden0, row_sum(down_v, down_q)])
    else:
        hidden0 = scattered(hidden_grads0)
        attention_both = jnp.concatenate(
            [attention_sum(kept0, swap(sent0)), attention_sum(kept1, sent1)], 1
        )
        attention = scattered(attention_both)
        column = lax.all_gather(grad_start, "dp").reshape(-1, model)
        local = jnp.where(inside, my_ids, vocab_here).reshape(-1)
        lookup_grad = jax.ops.segment_sum(single(column), local, num_segments=vocab_here)
        lookup_grad = single(lax.psum(bfloat(lookup_grad), ("section", "ctx")))
        grad_table = head_part(None, 0, 1) + lookup_grad
        table_sum = (
            *factored_sums(table, grad_table, table_rows)[:4],
            jnp.sum(table_square),
        )

    grads0, grads1 = (attention[:part], hidden0), (attention[part:], hidden1)
    owned, other = [], []
    for one, two in zip(grads0, grads1):
        owned.append(jnp.where(first, one, two))
        other.append(swap(jnp.where(first, two, one)))
    shard_in, shard_out = mine_first(owned[0], other[0])
    shard_gains = shard_out[:, model : model + 4].T
    shard_out = shard_out[:, :model]
    halves = jnp.stack(mine_first(owned[1], other[1]))
    ups = units // 2 // model
    shard_up = halves[:, : ups * part].reshape(2, ups, part, model).transpose(2, 0, 1, 3)
    shard_up = shard_up.reshape(part, 2, blocks, half).transpose(0, 2, 1, 3).reshape(part, units)
    shard_down = halves[:, ups * part :].reshape(2 * half, model)

    if by_fours():
        grads = (shard_in, shard_out, shard_up, shard_down, shard_gains)
        weights = (attention_in[0], attention_out[0], hidden_in[0], hidden_out[0], gains[0])
        rows = (attention_in_rows, attention_out_rows, hidden_in_rows, hidden_out_rows)
        rows = [stat.reshape(-1, 1) for stat in rows] + [gains_stat[0]]
        sums, *rows_news = layer_sums(
            grads, weights, rows, sums_first, sums_second, rows_new, table_square
        )
        sums = summed(sums, ("dp",))
        _, _, table_start = sum_rows([grad.shape[1] for grad in grads[:4]])
        layer_totals = summed(sums[:table_start], ("ctx",))
        table_news, table_cols_new = table_new(
            sums, table_start, table, grad_table, rows_new, table_cols[None], vocab_here * z_count
        )
        cols = (attention_in_cols, attention_out_cols, hidden_in_cols, hidden_out_cols)
        *news, in_cols, out_cols, up_cols, down_cols = layer_new(
            layer_totals, grads, weights, rows_news, cols, (model, model, model, units, model)
        )
        layered = []
        for k, cols_new in enumerate((in_cols, out_cols, up_cols, down_cols)):
            layered += [grads[k][None], rows_news[k].reshape(1, -1), cols_new, news[k][None]]
        return (
            loss_sum,
            loss_count,
            grad_table,
            rows_new.reshape(-1),
            table_cols_new[0],
            table_news,
            *layered,
            shard_gains[None],
            rows_news[4][None],
            news[4][None],
        )
    entries = [
        (table, grad_table, table_rows, table_cols, vocab_here * z_count),
        (attention_in[0], shard_in, attention_in_rows[0], attention_in_cols[0], model),
        (attention_out[0], shard_out, attention_out_rows[0], attention_out_cols[0], model),
        (hidden_in[0], shard_up, hidden_in_rows[0], hidden_in_cols[0], model),
        (hidden_out[0], shard_down, hidden_out_rows[0], hidden_out_cols[0], units),
    ]
    sums = [table_sum] + [factored_sums(*entry[:3]) for entry in entries[1:]]
    gain_weight = gains[0]
    gain_stat_new = DECAY * gains_stat[0] + (1.0 - DECAY) * (shard_gains * shard_gains + SQUARE_EPS)
    gain_update = shard_gains * lax.rsqrt(gain_stat_new)

    def packed(group):
        rows = []
        for item in group:
            flat = item.reshape(-1)
            if flat.shape[0] % LANES:
                flat = jnp.pad(flat, (0, LANES - flat.shape[0]))
            rows.append(flat.reshape(-1, LANES))
        return jnp.concatenate(rows), [item.shape for item in group]

    def unpacked(rows, shapes):
        items, start = [], 0
        for shape in shapes:
            size = 1
            for length in shape:
                size *= length
            count = -(-size // LANES)
            items.append(rows[start : start + count].reshape(-1)[:size].reshape(shape))
            start += count
        return items

    table_group, table_shapes = packed(sums[0][1:])
    layer_group, layer_shapes = packed(
        [item for entry in sums[1:] for item in entry[1:]]
        + [jnp.sum(gain_weight * gain_weight, -1), jnp.sum(gain_update * gain_update, -1)]
    )
    everything = summed(jnp.concatenate([table_group, layer_group]), ("dp",))
    table_totals = unpacked(everything[: table_group.shape[0]], table_shapes)
    layer_parts = unpacked(summed(everything[table_group.shape[0] :], ("ctx",)), layer_shapes)
    groups = [table_totals] + [layer_parts[4 * k : 4 * k + 4] for k in range(4)]
    gain_squares, gain_update_sums = layer_parts[16:]
    outs = []
    for (weight, gradient, _, col_stat, row_count), own, group in zip(entries, sums, groups):
        cols_new, new = factored_new(weight, gradient, own[0], col_stat, group, row_count)
        outs.append((gradient, own[0], cols_new, new))
    gain_clipping = jnp.maximum(1.0, jnp.sqrt(gain_update_sums / model))
    gain_size = jnp.maximum(SCALE_FLOOR, jnp.sqrt(gain_squares / model))
    gain_new = gain_weight - RELATIVE_RATE * gain_size[:, None] * (
        gain_update / gain_clipping[:, None]
    )
    layered = [item[None] for out in outs[1:] for item in out]
    return (
        loss_sum,
        loss_count,
        *outs[0],
        *layered,
        shard_gains[None],
        gain_stat_new[None],
        gain_new[None],
    )


def solution(mesh):
    rows = P("section", BLOCKS, None)
    row = P("section", BLOCKS)
    shared = P("section", None)
    side = P("section", None, BLOCKS)
    matrix_in = (rows, row, shared)
    matrix_out = (rows, row, shared, rows)
    placed = (
        P(None, None, "ctx"),
        P(None, "dp", None),
        P(None, "dp", "ctx"),
        P(None, None, "ctx"),
        P("dp", None),
        P("dp"),
        P(),
        *(matrix_in * 4),
        side,
        side,
    )
    return jax.shard_map(
        body,
        mesh=mesh,
        in_specs=placed,
        out_specs=(
            P(),
            P(),
            P("dp", None),
            P("dp"),
            P(),
            P("dp", None),
            *(matrix_out * 4),
            side,
            side,
            side,
        ),
        check_vma=False,
    )
```

```python
import functools

import jax
import jax.numpy as jnp
from jax import lax
from jax.experimental import pallas as pl
from jax.experimental.pallas import tpu as pltpu
from jax.sharding import PartitionSpec as P

HD = 64
WINDOW = 512
STEP = 10
NORM_EPS = 1e-05
SQUARE_EPS = 1e-30
SCALE_FLOOR = 0.001
RELATIVE_RATE = 0.5
MASKED = -1e30
DECAY = 1.0 - STEP ** (-0.8)
BLOCKS = ("dp", "ctx")
LANES = 128
DEAD = -(1 << 30)
MIB = 1 << 20


def bfloat(values):
    return values.astype(jnp.bfloat16)


def single(values):
    return values.astype(jnp.float32)


def matmul(left, right):
    return jnp.dot(left, right, preferred_element_type=jnp.float32)


def matmul_left(left, right):
    return lax.dot_general(
        left, right, (((0,), (0,)), ((), ())), preferred_element_type=jnp.float32
    )


def matmul_right(left, right):
    return lax.dot_general(
        left, right, (((1,), (1,)), ((), ())), preferred_element_type=jnp.float32
    )


def layer_norm(values, gain, shift):
    center = values - jnp.mean(values, -1, keepdims=True)
    spread = jnp.mean(center * center, -1, keepdims=True)
    return center * lax.rsqrt(spread + NORM_EPS) * gain + shift


def gelu_tanh(values):
    return jax.nn.gelu(values, approximate=True)


def at(values, index, axis):
    return lax.dynamic_index_in_dim(values, index, axis, keepdims=False)


def swap(values):
    return lax.ppermute(values, "section", [(0, 1), (1, 0)])


def cross(values, axis, bits):
    return lax.ppermute(values, axis, [(i, i ^ bits) for i in range(lax.axis_size(axis))])


def shifted(values, axis, distance):
    devices = range(lax.axis_size(axis))
    return lax.ppermute(
        values, axis, [(i, i + distance) for i in devices if i + distance in devices]
    )


def by_fours():
    return lax.axis_size("dp") == 4 and lax.axis_size("ctx") == 4


def mine_first(mine, theirs):
    first = lax.axis_index("section") == 0
    return jnp.where(first, mine, theirs), jnp.where(first, theirs, mine)


def after(values, *earlier):
    return lax.optimization_barrier((values, *earlier))[0]


def column_pieces(part):
    if not by_fours():
        return (lax.all_gather(part, "dp", axis=0),)
    return tuple(cross(part, "dp", k) for k in (1, 2, 3))


def column_join(part, pieces):
    if not by_fours():
        return pieces[0]
    return in_order((part, *pieces), "dp")


def plane_near(column):
    if not by_fours():
        return (lax.all_gather(column, "ctx", axis=1),)
    return cross(column, "ctx", 1), cross(column, "ctx", 2)


def plane_far(near):
    if not by_fours():
        return ()
    beside, above = near
    return cross(above[:2], "ctx", 1), cross(beside[2:], "ctx", 2)


def plane_list(column, near, far):
    if not by_fours():
        return near[0].reshape((-1,) + column.shape[1:])
    return (column, *near, jnp.concatenate(far))


def plane_near_half(column, side):
    if not by_fours():
        return plane_near(column) if side == 0 else ()
    return plane_near(column[2 * side : 2 * side + 2])


def plane_far_half(first, second):
    if not by_fours():
        return ()
    return cross(first[1], "ctx", 1), cross(second[0], "ctx", 2)


def plane_halves(column, near, far):
    if not by_fours():
        return plane_list(column, near[0], far)
    return (column, *zip(*near), tuple(far))


def in_order(pieces, axis, at_axis=0):
    i = lax.axis_index(axis)
    return jnp.stack(
        [lax.select_n(i, *[pieces[place ^ k] for k in range(4)]) for place in range(4)], at_axis
    )


def weights_kernel(place_ref, *refs):
    mine, theirs, in_ref, out_ref = refs
    c, first = place_ref[0], place_ref[1] == 0
    part = mine.shape[1]

    def lay(ref, pieces):
        for k in range(4):
            for z in range(4):
                rows = pl.ds(pl.multiple_of((4 * z + (c ^ k)) * part, 16), part)
                ref[rows, :] = pieces[4 * k + z]

    @pl.when(first)
    def _():
        lay(in_ref, mine)
        lay(out_ref, theirs)

    @pl.when(~first)
    def _():
        lay(in_ref, theirs)
        lay(out_ref, mine)


def attention_weights(mine, theirs, model, layer):
    if by_fours():
        blocks, both, wide = mine.shape
        place = jnp.stack([lax.axis_index("ctx"), lax.axis_index("section")])
        weight_in, weight_out = pl.pallas_call(
            weights_kernel,
            grid_spec=pltpu.PrefetchScalarGridSpec(
                num_scalar_prefetch=1,
                grid=(1,),
                in_specs=[pl.BlockSpec((blocks, both // 2, wide), lambda *_: (0, layer, 0))] * 2,
                out_specs=[whole_block((model, wide))] * 2,
            ),
            out_shape=[jax.ShapeDtypeStruct((model, wide), jnp.bfloat16)] * 2,
            compiler_params=vmem(24),
            cost_estimate=small_cost(
                flops=0, bytes_accessed=8 * model * wide, transcendentals=0
            ),
        )(place, mine, theirs)
    else:
        part = mine.shape[1] // 2
        weights = mine_first(mine, theirs)
        weight_in, weight_out = (
            w[:, layer * part : (layer + 1) * part].reshape(model, -1) for w in weights
        )
    return weight_in, weight_out[:, :model], single(weight_out[:, model : model + 4]).T


def gather_blocks(part):
    return gather_ctx(column_join(part, column_pieces(part))).swapaxes(0, 1).reshape(
        (-1,) + part.shape
    )


def gather_ctx(part):
    if not by_fours():
        return lax.all_gather(part, "ctx", axis=0)
    return in_order([part] + [cross(part, "ctx", k) for k in (1, 2, 3)], "ctx")


def scattered(parts):
    return single(lax.psum_scatter(parts, BLOCKS, scatter_dimension=0))


def corner(parts, rows, z, y=None, x=None):
    grid = parts.reshape((4, 2, 2) + parts.shape[1:])
    first, count = rows
    start = (z, 0 if y is None else y, 0 if x is None else x, first, 0)
    size = (2, 2 if y is None else 1, 2 if x is None else 1, count, parts.shape[2])
    return lax.dynamic_slice(grid, start, size)


def plane_bits():
    c = lax.axis_index("ctx")
    return c & 1, c >> 1


def half_first(parts, rows):
    x, y = plane_bits()
    return (
        cross(corner(parts, rows, 0, x=1 - x), "ctx", 1),
        cross(corner(parts, rows, 2, y=1 - y), "ctx", 2),
    )


def half_kept(parts, rows, got):
    x, y = plane_bits()
    near = bfloat(single(corner(parts, rows, 0, x=x)) + single(got[0]))
    far = bfloat(single(corner(parts, rows, 2, y=y)) + single(got[1]))
    near, far = near[:, :, 0], far[:, 0]
    return (at(near, y, 1), at(far, x, 1)), (at(near, 1 - y, 1), at(far, 1 - x, 1))


def half_send(halves):
    return cross(halves[0], "ctx", 2), cross(halves[1], "ctx", 1)


def half_column(kept, got):
    return jnp.concatenate([bfloat(single(one) + single(two)) for one, two in zip(kept, got)])


def row_pieces(parts):
    if not by_fours():
        return (lax.psum_scatter(bfloat(parts), "dp", scatter_dimension=0),)
    z = lax.axis_index("dp")
    low = bfloat(parts)
    return tuple(cross(at(low, z ^ k, 0), "dp", k) for k in (1, 2, 3))


def row_sum(parts, pieces):
    total = single(pieces[0])
    for piece in pieces[1:]:
        total = total + single(piece)
    return single(at(parts, lax.axis_index("dp"), 0)) + total if by_fours() else total


def scatter_rows(parts):
    return row_sum(parts, row_pieces(parts))


def summed(values, axes):
    if not by_fours():
        return lax.psum(values, axes)
    for axis in axes:
        one, two, three = (cross(values, axis, k) for k in (1, 2, 3))
        values = (values + one) + (two + three)
    return values


def doc_numbers(lengths, places):
    bounds = jnp.cumsum(lengths)
    return jnp.sum((places[:, None] >= bounds[None, :]).astype(jnp.int32), -1)


def pair_bias(lengths, query_places, key_places):
    query_docs = doc_numbers(lengths, query_places)
    key_docs = doc_numbers(lengths, key_places)
    allowed = (
        (key_places[None, :] <= query_places[:, None])
        & (key_places[None, :] > query_places[:, None] - WINDOW)
        & (key_places[None, :] >= 0)
        & (key_docs[None, :] == query_docs[:, None])
    )
    return jnp.where(allowed, 0.0, MASKED)


def earlier_count(local_len):
    return min(lax.axis_size("ctx") - 1, -(-(WINDOW - 1) // local_len))


def key_rows(keyval):
    reach = earlier_count(keyval.shape[0])
    return jnp.concatenate(
        [shifted(keyval, "ctx", k) for k in range(reach, 0, -1)] + [keyval]
    )


def key_rows_back(grads, local_len):
    reach = earlier_count(local_len)
    starts = [(reach - k) * local_len for k in range(1, reach + 1)]
    return tuple(
        shifted(grads[start : start + local_len], "ctx", -(k + 1))
        for k, start in enumerate(starts)
    )


def key_rows_sum(grads, pieces, local_len):
    total = grads[earlier_count(local_len) * local_len :]
    for piece in pieces:
        total = total + piece
    return bfloat(total)


def whole_block(shape):
    return pl.BlockSpec(shape, lambda *_: (0,) * len(shape))


def vmem(mebibytes):
    return pltpu.CompilerParams(vmem_limit_bytes=mebibytes * MIB)


def small_cost(flops, bytes_accessed, transcendentals):
    return pl.CostEstimate(
        flops=flops // 16, bytes_accessed=bytes_accessed // 16, transcendentals=0 * transcendentals
    )


def row_block(rows, most):
    block = most
    while rows % block:
        block //= 2
    return block


def turned(values):
    return pltpu.roll(values, HD, 1)


def softmax_rows(scores):
    exponents = jnp.exp(scores - jnp.max(scores, -1, keepdims=True))
    return exponents * (1.0 / jnp.sum(exponents, -1, keepdims=True))


def attend_kernel(query_ref, keyval_ref, bias_ref, out_ref):
    keyval = keyval_ref[...]
    bias = bias_ref[...]
    pair = single(query_ref[...])
    left = lax.broadcasted_iota(jnp.int32, pair.shape, 1) < HD
    outs = []
    for heads in (pair, turned(pair)):
        query = bfloat(jnp.where(left, heads, 0.0))
        probs = softmax_rows(matmul_right(query, keyval) + bias)
        outs.append(matmul(bfloat(probs), keyval))
    out_ref[...] = bfloat(jnp.where(left, turned(outs[0]), outs[1]))


def attend(query, keyval, bias):
    rows, columns = query.shape
    pair = 2 * HD
    return pl.pallas_call(
        attend_kernel,
        grid=(columns // pair,),
        in_specs=[
            pl.BlockSpec((rows, pair), lambda i: (0, i)),
            whole_block(keyval.shape),
            whole_block(bias.shape),
        ],
        out_specs=pl.BlockSpec((rows, pair), lambda i: (0, i)),
        out_shape=jax.ShapeDtypeStruct((rows, columns), jnp.bfloat16),
        compiler_params=vmem(40),
        cost_estimate=small_cost(
            flops=4 * rows * columns * keyval.shape[0],
            bytes_accessed=8 * rows * columns,
            transcendentals=rows * columns * keyval.shape[0] // HD,
        ),
    )(query, keyval, bias)


def attend_back_kernel(query_ref, keyval_ref, bias_ref, grad_ref, grad_query_ref, grad_keyval_ref):
    keyval = keyval_ref[...]
    bias = bias_ref[...]
    pair = single(query_ref[...])
    grads = single(grad_ref[...])
    left = lax.broadcasted_iota(jnp.int32, pair.shape, 1) < HD
    total = jnp.where(pl.program_id(0) == 0, 0.0, grad_keyval_ref[...])
    outs = []
    for heads, grad_heads in ((pair, turned(grads)), (turned(pair), grads)):
        query = bfloat(jnp.where(left, heads, 0.0))
        grad = bfloat(jnp.where(left, 0.0, grad_heads))
        probs = softmax_rows(matmul_right(query, keyval) + bias)
        grad_probs = matmul_right(grad, keyval)
        inner = jnp.sum(probs * grad_probs, -1, keepdims=True)
        grad_scores = bfloat(probs * (grad_probs - inner))
        outs.append(matmul(grad_scores, keyval))
        total = total + matmul_left(grad_scores, query) + matmul_left(bfloat(probs), grad)
    grad_keyval_ref[...] = total
    grad_query = single(bfloat(jnp.where(left, outs[0], turned(outs[1])))) * HD ** (-0.5)
    grad_query_ref[...] = bfloat(grad_query)


def attend_back(query, keyval, bias, grad_out):
    rows, columns = query.shape
    pair = 2 * HD
    pairs = pl.BlockSpec((rows, pair), lambda i: (0, i))
    return pl.pallas_call(
        attend_back_kernel,
        grid=(columns // pair,),
        in_specs=[pairs, whole_block(keyval.shape), whole_block(bias.shape), pairs],
        out_specs=[pairs, whole_block(keyval.shape)],
        out_shape=[
            jax.ShapeDtypeStruct((rows, columns), jnp.bfloat16),
            jax.ShapeDtypeStruct(keyval.shape, jnp.float32),
        ],
        compiler_params=vmem(48),
        cost_estimate=small_cost(
            flops=10 * rows * columns * keyval.shape[0],
            bytes_accessed=8 * rows * columns,
            transcendentals=rows * columns * keyval.shape[0] // HD,
        ),
    )(query, keyval, bias, grad_out)


def lower_kernel(table_ref, *refs):
    low_ref, square_ref = refs[-2:]
    weights = table_ref[...]
    low_ref[...] = bfloat(weights)
    squares = jnp.sum((weights * weights).reshape(-1, 8, weights.shape[1]), 0)
    square_ref[...] = jnp.where(pl.program_id(0) == 0, 0.0, square_ref[...]) + squares


def lowered(table, low, index, count):
    vocab_here, model = table.shape
    block = row_block(vocab_here, 1024)
    steps = vocab_here // block
    first, last = index * steps // count, (index + 1) * steps // count
    rows = pl.BlockSpec((block, model), lambda i: (i + first, 0))
    return pl.pallas_call(
        lower_kernel,
        grid=(last - first,),
        in_specs=[rows] + ([] if low is None else [pl.BlockSpec(memory_space=pl.ANY)]),
        out_specs=[rows, whole_block((8, model))],
        out_shape=[
            jax.ShapeDtypeStruct(table.shape, jnp.bfloat16),
            jax.ShapeDtypeStruct((8, model), jnp.float32),
        ],
        input_output_aliases={} if low is None else {1: 0},
        compiler_params=vmem(40),
        cost_estimate=small_cost(
            flops=2 * vocab_here * model // count,
            bytes_accessed=6 * vocab_here * model // count,
            transcendentals=0,
        ),
    )(*((table,) if low is None else (table, low)))


def head_stats_kernel(chosen_ref, target_ref, low_ref, stats_ref):
    step = pl.program_id(0)
    rows = low_ref.shape[0]

    @pl.when(step == 0)
    def _():
        stats_ref[...] = jnp.zeros_like(stats_ref)
        stats_ref[0:1, :] = jnp.full((1, stats_ref.shape[1]), MASKED, jnp.float32)

    logits = matmul(low_ref[...], chosen_ref[...])
    places = lax.broadcasted_iota(jnp.int32, logits.shape, 0)
    matches = places == target_ref[...] - step * rows
    before, totals = stats_ref[0:1, :], stats_ref[1:2, :]
    highest = jnp.maximum(before, jnp.max(logits, 0, keepdims=True))
    stats_ref[1:2, :] = totals * jnp.exp(before - highest) + jnp.sum(
        jnp.exp(logits - highest), 0, keepdims=True
    )
    stats_ref[0:1, :] = highest
    stats_ref[2:3, :] = stats_ref[2:3, :] + jnp.sum(
        jnp.where(matches, logits, 0.0), 0, keepdims=True
    )


def head_stats(chosen_across, target_row, low):
    vocab_here, model = low.shape
    slots = chosen_across.shape[1]
    block = row_block(vocab_here, 1024)
    return pl.pallas_call(
        head_stats_kernel,
        grid=(vocab_here // block,),
        in_specs=[
            whole_block(chosen_across.shape),
            whole_block((1, slots)),
            pl.BlockSpec((block, model), lambda i: (i, 0)),
        ],
        out_specs=whole_block((8, slots)),
        out_shape=jax.ShapeDtypeStruct((8, slots), jnp.float32),
        compiler_params=vmem(40),
        cost_estimate=small_cost(
            flops=2 * slots * vocab_here * model,
            bytes_accessed=2 * vocab_here * model,
            transcendentals=slots * vocab_here,
        ),
    )(chosen_across, target_row, low)


def head_rows_kernel(chosen_ref, target_ref, logsum_ref, low_ref, grad_ref):
    step = pl.program_id(0)
    rows = low_ref.shape[0]
    low = low_ref[...]
    logits = matmul_right(chosen_ref[...], low)
    places = lax.broadcasted_iota(jnp.int32, logits.shape, 1) + step * rows
    target = target_ref[...]
    matches = jnp.where(places == target, 1.0, 0.0)
    grads = jnp.where(target != DEAD, jnp.exp(logits - logsum_ref[...]) - matches, 0.0)
    before = jnp.where(step == 0, 0.0, grad_ref[...])
    grad_ref[...] = before + matmul(bfloat(grads), low)


def head_rows(chosen, target_column, logsum_column, low):
    vocab_here, model = low.shape
    slots = chosen.shape[0]
    block = row_block(vocab_here, 1024)
    return pl.pallas_call(
        head_rows_kernel,
        grid=(vocab_here // block,),
        in_specs=[
            whole_block(chosen.shape),
            whole_block((slots, 1)),
            whole_block((slots, 1)),
            pl.BlockSpec((block, model), lambda i: (i, 0)),
        ],
        out_specs=whole_block((slots, model)),
        out_shape=jax.ShapeDtypeStruct((slots, model), jnp.float32),
        compiler_params=vmem(40),
        cost_estimate=small_cost(
            flops=4 * slots * vocab_here * model,
            bytes_accessed=2 * vocab_here * model,
            transcendentals=slots * vocab_here,
        ),
    )(chosen, target_column, logsum_column, low)


def head_table_kernel(first, chosen_ref, across_ref, target_ref, logsum_ref, low_ref, *refs):
    step = pl.program_id(0) + first
    grad_ref = refs[-1]
    rows = low_ref.shape[0]
    logits = matmul(low_ref[...], across_ref[...])
    places = lax.broadcasted_iota(jnp.int32, logits.shape, 0) + step * rows
    target = target_ref[...]
    matches = jnp.where(places == target, 1.0, 0.0)
    grads = jnp.where(target != DEAD, jnp.exp(logits - logsum_ref[...]) - matches, 0.0)
    grad_ref[...] = matmul(bfloat(grads), chosen_ref[...])


def head_table(chosen, chosen_across, target_row, logsum_row, low, grads, index, count):
    vocab_here, model = low.shape
    slots = chosen.shape[0]
    block = row_block(vocab_here, 1024)
    steps = vocab_here // block
    first, last = index * steps // count, (index + 1) * steps // count
    rows = pl.BlockSpec((block, model), lambda i: (i + first, 0))
    return pl.pallas_call(
        functools.partial(head_table_kernel, first),
        grid=(last - first,),
        in_specs=[
            whole_block(chosen.shape),
            whole_block(chosen_across.shape),
            whole_block((1, slots)),
            whole_block((1, slots)),
            rows,
        ]
        + ([] if grads is None else [pl.BlockSpec(memory_space=pl.ANY)]),
        out_specs=rows,
        out_shape=jax.ShapeDtypeStruct(low.shape, jnp.float32),
        input_output_aliases={} if grads is None else {5: 0},
        compiler_params=vmem(48),
        cost_estimate=small_cost(
            flops=4 * slots * vocab_here * model // count,
            bytes_accessed=6 * vocab_here * model // count,
            transcendentals=slots * vocab_here // count,
        ),
    )(*((chosen, chosen_across, target_row, logsum_row, low) + (() if grads is None else (grads,))))


def table_sums_kernel(first, place_ref, starts_ref, ids_ref, order_ref, head_ref, stat_ref, *refs):
    pieces = refs[:8]
    grad_ref, rows_ref, sums_ref, wide_ref = refs[-4:]
    step = pl.program_id(0) + first
    rows, model = head_ref.shape
    room = pieces[0].shape[1]

    @pl.when(pl.program_id(0) == 0)
    def _():
        for side in range(2):
            section = place_ref[1] if side == 0 else 1 - place_ref[1]
            for k in range(4):
                for z in range(4):
                    block = (4 * section + z) * 4 + (place_ref[0] ^ k)
                    row = pl.multiple_of(block * room, 16)
                    wide_ref[pl.ds(row, room), :] = single(pieces[4 * side + k][z])
        sums_ref[...] = jnp.zeros_like(sums_ref)

    grad_ref[...] = head_ref[...]
    start, end = starts_ref[step], starts_ref[step + 1]

    @pl.loop(0, (end - start + 3) // 4)
    def _(i):
        places, values = [], []
        for k in range(4):
            j = jnp.minimum(start + 4 * i + k, end - 1)
            row = wide_ref[pl.ds(order_ref[j], 1), :]
            values.append(jnp.where(start + 4 * i + k < end, row, 0.0))
            places.append(pl.ds(ids_ref[j] - step * rows, 1))
        for place, row in zip(places, values):
            grad_ref[place, :] = grad_ref[place, :] + row

    stats = stat_ref[...]
    columns = jnp.zeros((8, model), jnp.float32)
    scaled = jnp.zeros((8, model), jnp.float32)
    for k in range(rows // LANES):
        part = grad_ref[k * LANES : (k + 1) * LANES, :]
        square = part * part
        mean = jnp.sum(square + SQUARE_EPS, -1, keepdims=True) * (1.0 / model)
        stat = jnp.transpose(jnp.broadcast_to(stats[k : k + 1, :], (LANES, LANES)))
        new = DECAY * stat + (1.0 - DECAY) * mean
        rows_ref[k : k + 1, :] = jnp.transpose(new)[0:1, :]
        columns = columns + jnp.sum((square + SQUARE_EPS).reshape(LANES // 8, 8, model), 0)
        ratio = square * (1.0 / new[:, 0:1])
        scaled = scaled + jnp.sum(ratio.reshape(LANES // 8, 8, model), 0)
    sums_ref[0:8, :] = sums_ref[0:8, :] + columns
    sums_ref[8:16, :] = sums_ref[8:16, :] + scaled


def table_sums(starts, ids, order, pieces, head, row_stat, block, earlier, index, count):
    vocab_here, model = head.shape
    steps = vocab_here // block
    first, last = index * steps // count, (index + 1) * steps // count
    rows = pl.BlockSpec((block, model), lambda i, *_: (i + first, 0))
    stats = pl.BlockSpec((block // LANES, LANES), lambda i, *_: (i + first, 0))
    kept = [] if earlier is None else [pl.BlockSpec(memory_space=pl.ANY)] * 2
    return pl.pallas_call(
        functools.partial(table_sums_kernel, first),
        grid_spec=pltpu.PrefetchScalarGridSpec(
            num_scalar_prefetch=4,
            grid=(last - first,),
            in_specs=[rows, stats]
            + [
                pl.BlockSpec(piece.shape, lambda *_: (0, 0, 0), pipeline_mode=pl.Buffered(1))
                for piece in pieces
            ]
            + kept,
            out_specs=[rows, stats, pl.BlockSpec((16, model), lambda *_: (0, 0))],
            scratch_shapes=[pltpu.VMEM((32 * pieces[0].shape[1], model), jnp.float32)],
        ),
        out_shape=[
            jax.ShapeDtypeStruct(head.shape, jnp.float32),
            jax.ShapeDtypeStruct((vocab_here // LANES, LANES), jnp.float32),
            jax.ShapeDtypeStruct((16, model), jnp.float32),
        ],
        input_output_aliases={} if earlier is None else {14: 0, 15: 1},
        compiler_params=vmem(56),
        cost_estimate=small_cost(
            flops=8 * vocab_here * model // count,
            bytes_accessed=8 * vocab_here * model // count,
            transcendentals=0,
        ),
    )(
        jnp.stack([lax.axis_index("ctx"), lax.axis_index("section")]),
        starts,
        ids,
        order,
        head,
        row_stat.reshape(-1, LANES),
        *pieces,
        *(earlier or ()),
    )


def gelu_slope(values):
    factor = (2.0 / jnp.pi) ** 0.5
    inner = jnp.tanh(factor * (values + 0.044715 * values * values * values))
    slope = factor * (1.0 + 3.0 * 0.044715 * values * values)
    return 0.5 * (1.0 + inner) + 0.5 * values * (1.0 - inner * inner) * slope


def put_together(c, step, pieces, up_ref, down_ref):
    model = up_ref.shape[0]
    columns, packed = pieces[0].shape[:2]
    part, half = model // (8 * columns), packed // 2
    for k in range(4):
        for z in range(2 * columns):
            piece = pieces[2 * k + z // columns]
            rows = pl.ds(pl.multiple_of((4 * z + (c ^ k)) * part, 16), part)
            place = pl.ds(pl.multiple_of(step * part, 16), part)
            up_ref[rows, :] = piece[z % columns, place, :]
    for side in range(2):

        @pl.when(step == side)
        def _():
            for k in range(4):
                for z in range(columns):
                    rows = pl.ds(pl.multiple_of((4 * z + (c ^ k)) * half, 16), half)
                    down_ref[rows, :] = pieces[2 * k + side][z, half : 2 * half, :]


def half_specs(hidden):
    if not isinstance(hidden, tuple):
        grid = hidden.reshape((4, 4) + hidden.shape[1:])
        shape = (2, None) + hidden.shape[1:]
        specs = [
            pl.BlockSpec(shape, lambda *_, k=k, side=side: (side, k, 0, 0))
            for k in range(4)
            for side in range(2)
        ]
        return jnp.zeros(1, jnp.int32), [grid] * 8, specs
    arrays, specs = [], []
    for piece in hidden:
        for side in range(2):
            array = piece[side] if isinstance(piece, tuple) else piece
            shape = (2,) + array.shape[1:]
            place = 0 if isinstance(piece, tuple) else side
            arrays.append(array)
            specs.append(pl.BlockSpec(shape, lambda *_, place=place: (place, 0, 0)))
    return lax.axis_index("ctx").reshape(1), arrays, specs


def hidden_kernel(place_ref, both_ref, *refs):
    *pieces, upper_ref, partial_ref, up_ref, down_ref = refs
    step = pl.program_id(0)
    put_together(place_ref[0], step, pieces, up_ref, down_ref)
    upper = matmul(both_ref[...], up_ref[...])
    upper_ref[...] = upper
    before = jnp.where(step == 0, 0.0, partial_ref[...])
    partial_ref[...] = before + matmul(bfloat(gelu_tanh(upper)), down_ref[...])


def hidden_forward(both, hidden):
    rows, model = both.shape
    blocks = lax.axis_size("dp") * lax.axis_size("ctx")
    if not by_fours():
        up, down = hidden_weights(hidden)
        upper = matmul(both, up)
        return upper, matmul(bfloat(gelu_tanh(upper)), down)
    packed = (hidden[0] if isinstance(hidden, tuple) else hidden).shape[1]
    size = blocks * packed * model
    steps = size // (2 * model * model)
    square = pltpu.VMEM((model, model), jnp.bfloat16)
    place, arrays, specs = half_specs(hidden)
    return pl.pallas_call(
        hidden_kernel,
        grid_spec=pltpu.PrefetchScalarGridSpec(
            num_scalar_prefetch=1,
            grid=(steps,),
            in_specs=[whole_block(both.shape)] + specs,
            out_specs=[pl.BlockSpec((rows, model), lambda j, _: (0, j)), whole_block(both.shape)],
            scratch_shapes=[square, square],
        ),
        out_shape=[
            jax.ShapeDtypeStruct((rows, steps * model), jnp.float32),
            jax.ShapeDtypeStruct((rows, model), jnp.float32),
        ],
        compiler_params=vmem(48),
        cost_estimate=small_cost(
            flops=2 * rows * size,
            bytes_accessed=2 * size + 8 * rows * steps * model,
            transcendentals=rows * steps * model,
        ),
    )(place, both, *arrays)


def hidden_back_kernel(place_ref, both_ref, upper_ref, grad_ref, *refs):
    *pieces, partial_ref, grads_ref, up_ref, down_ref = refs
    step = pl.program_id(0)
    model = both_ref.shape[1]
    blocks, half = grads_ref.shape[0], grads_ref.shape[1] // 2
    rows, per_step = model // blocks, model // half
    put_together(place_ref[0], step, pieces, up_ref, down_ref)
    both, upper, grad = both_ref[...], upper_ref[...], grad_ref[...]
    active = bfloat(gelu_tanh(upper))
    grad_upper = bfloat(matmul_right(grad, down_ref[...]) * gelu_slope(upper))
    before = jnp.where(step == 0, 0.0, partial_ref[...])
    partial_ref[...] = before + matmul_right(grad_upper, up_ref[...])
    grad_up = bfloat(matmul_left(both, grad_upper)).reshape(blocks, rows, model)
    grads_ref[:, pl.ds(pl.multiple_of(step * rows, 16), rows), :] = grad_up
    grad_down = bfloat(matmul_left(active, grad)).reshape(per_step, half, model)
    grads_ref[pl.ds(step * per_step, per_step), half : 2 * half, :] = grad_down


def hidden_backward(both, upper, grad_both, hidden):
    rows, model = both.shape
    blocks = lax.axis_size("dp") * lax.axis_size("ctx")
    if not by_fours():
        up, down = hidden_weights(hidden)
        active = bfloat(gelu_tanh(upper))
        grad_upper = bfloat(matmul_right(grad_both, down) * gelu_slope(upper))
        grad_up, grad_down = matmul_left(both, grad_upper), matmul_left(active, grad_both)
        parts = [
            grad_up[:, k : k + model].reshape(blocks, -1, model)
            for k in range(0, grad_up.shape[1], model)
        ]
        packed = jnp.concatenate(parts + [grad_down.reshape(blocks, -1, model)], 1)
        return matmul_right(grad_upper, up), bfloat(packed)
    packed = (hidden[0] if isinstance(hidden, tuple) else hidden).shape[1]
    size = blocks * packed * model
    steps = size // (2 * model * model)
    square = pltpu.VMEM((model, model), jnp.bfloat16)
    grads = (blocks, packed, model)
    place, arrays, specs = half_specs(hidden)
    return pl.pallas_call(
        hidden_back_kernel,
        grid_spec=pltpu.PrefetchScalarGridSpec(
            num_scalar_prefetch=1,
            grid=(steps,),
            in_specs=[
                whole_block(both.shape),
                pl.BlockSpec((rows, model), lambda j, _: (0, j)),
                whole_block(both.shape),
            ]
            + specs,
            out_specs=[whole_block(both.shape), whole_block(grads)],
            scratch_shapes=[square, square],
        ),
        out_shape=[
            jax.ShapeDtypeStruct((rows, model), jnp.float32),
            jax.ShapeDtypeStruct(grads, jnp.bfloat16),
        ],
        compiler_params=vmem(56),
        cost_estimate=small_cost(
            flops=4 * rows * size,
            bytes_accessed=4 * size + 4 * rows * steps * model,
            transcendentals=2 * rows * steps * model,
        ),
    )(place, both, upper, grad_both, *arrays)


def hidden_weights(hidden):
    blocks, packed, model = hidden.shape
    part = model // blocks
    parts = [hidden[:, k : k + part].reshape(model, model) for k in range(0, packed // 2, part)]
    return jnp.concatenate(parts, 1), hidden[:, packed // 2 :].reshape(-1, model)


def both_rows(values):
    return jnp.concatenate([values, swap(values)])


def own_rows(partial, pieces=1):
    rows = partial.shape[0] // 2
    return partial[:rows] + swap(partial[rows:])


def factored_sums(weight, gradient, row_stat):
    square = gradient * gradient + SQUARE_EPS
    rows_new = DECAY * row_stat + (1.0 - DECAY) * jnp.mean(square, -1)
    columns = jnp.sum(square, 0)
    scaled = jnp.sum(gradient * gradient / rows_new[:, None], 0)
    return rows_new, columns, scaled, jnp.sum(rows_new), jnp.sum(weight * weight)


def factored_new(weight, gradient, rows_new, col_stat, sums, row_count):
    columns, scaled, rows_sum, weight_sum = sums
    entries = row_count * weight.shape[1]
    cols_new = DECAY * col_stat + (1.0 - DECAY) * columns / row_count
    mean_rows = rows_sum / row_count
    update_sum = mean_rows * jnp.sum(scaled / cols_new)
    clipping = jnp.maximum(1.0, jnp.sqrt(update_sum / entries))
    size = jnp.maximum(SCALE_FLOOR, jnp.sqrt(weight_sum / entries))
    update = gradient * lax.rsqrt(rows_new[:, None] * cols_new[None, :] / mean_rows)
    return cols_new, weight - RELATIVE_RATE * size * (update / clipping)


def distinct_slots(ids, vocab_here):
    count = ids.shape[1]
    shard = ids // vocab_here
    earlier = jnp.arange(count)[None, :] < jnp.arange(count)[:, None]
    same = ids[:, :, None] == ids[:, None, :]
    first = ~jnp.any(same & earlier, -1)
    mates = (shard[:, :, None] == shard[:, None, :]) & first[:, None, :] & earlier
    rank = jnp.sum(mates.astype(jnp.int32), -1)
    slot = jnp.sum(jnp.where(same & first[:, None, :], rank[:, None, :], 0), -1)
    return slot, shard


def asked_ids(local, slot, here, room):
    places = jnp.arange(room, dtype=jnp.int32)[None, :, None]
    matches = (slot[:, None, :] == places) & here[:, None, :]
    return jnp.min(jnp.where(matches, local[:, None, :], 1 << 30), -1)


def attention_sum_kernel(kept0_ref, sent0_ref, kept1_ref, sent1_ref, out_ref):
    part = kept0_ref.shape[1]
    out_ref[:, :part] = bfloat(single(kept0_ref[...]) + single(sent0_ref[...]))
    out_ref[:, part:] = bfloat(single(kept1_ref[...]) + single(sent1_ref[...]))


def attention_sums(grads, blocks):
    wide = grads[0].shape[1]
    grads = [grad.reshape(blocks, -1, wide) for grad in grads]
    part = grads[0].shape[1]
    if part % 16:
        total = [bfloat(single(grads[k]) + single(grads[k + 1])) for k in (0, 2)]
        return jnp.concatenate(total, 1)
    step = row_block(blocks, 4)
    return pl.pallas_call(
        attention_sum_kernel,
        grid=(blocks // step,),
        in_specs=[pl.BlockSpec((step, part, wide), lambda i: (i, 0, 0))] * 4,
        out_specs=pl.BlockSpec((step, 2 * part, wide), lambda i: (i, 0, 0)),
        out_shape=jax.ShapeDtypeStruct((blocks, 2 * part, wide), jnp.bfloat16),
        compiler_params=vmem(24),
        cost_estimate=small_cost(
            flops=0, bytes_accessed=8 * grads[0].size, transcendentals=0
        ),
    )(*grads)


def picked_kernel(ids_ref, table_ref, out_ref, rows_ref, sem):
    count = rows_ref.shape[0]

    @pl.loop(0, count // 8)
    def _(i):
        for k in range(8):
            row = table_ref.at[pl.ds(ids_ref[8 * i + k], 1), :]
            pltpu.make_async_copy(row, rows_ref.at[pl.ds(8 * i + k, 1), :], sem).start()

    pltpu.make_async_copy(table_ref.at[pl.ds(0, count), :], rows_ref, sem).wait()
    out_ref[...] = bfloat(rows_ref[...])


def picked_rows(ids, table):
    shape = (ids.shape[0], table.shape[1])
    return pl.pallas_call(
        picked_kernel,
        grid_spec=pltpu.PrefetchScalarGridSpec(
            num_scalar_prefetch=1,
            grid=(1,),
            in_specs=[pl.BlockSpec(memory_space=pl.ANY)],
            out_specs=whole_block(shape),
            scratch_shapes=[pltpu.VMEM(shape, jnp.float32), pltpu.SemaphoreType.DMA],
        ),
        out_shape=jax.ShapeDtypeStruct(shape, jnp.bfloat16),
        compiler_params=vmem(24),
        cost_estimate=small_cost(
            flops=0, bytes_accessed=4 * shape[0] * shape[1], transcendentals=0
        ),
    )(ids, table)


def spilled_inside(ids, slot, room, vocab_here):
    local = ids - lax.axis_index("dp") * vocab_here
    return local, (local >= 0) & (local < vocab_here) & (slot >= room)


def spilled_rows(token_ids, slot, room, table):
    ids = at(token_ids, lax.axis_index("section"), 0)
    local, inside = spilled_inside(ids, slot, room, table.shape[0])
    rows = jnp.take(table, jnp.clip(local, 0, table.shape[0] - 1), axis=0)
    rows = jnp.where(inside[..., None], bfloat(rows), 0)
    return single(lax.psum_scatter(rows, "dp", scatter_dimension=0))


def spilled_grads(token_ids, slot, room, grad_start, vocab_here):
    ids = at(token_ids, lax.axis_index("section"), 0)
    local, inside = spilled_inside(ids, slot, room, vocab_here)
    column = lax.all_gather(grad_start, "dp")
    total = jax.ops.segment_sum(
        single(column.reshape(-1, column.shape[-1])),
        jnp.where(inside, local, vocab_here).reshape(-1),
        num_segments=vocab_here,
    )
    return single(lax.psum(bfloat(total), ("section", "ctx")))


def put_rows(ref, row, vector):
    for k in range(vector.shape[1] // LANES):
        ref[row + k : row + k + 1, :] = vector[:, k * LANES : (k + 1) * LANES]


def got_rows(ref, row, width):
    count = width // LANES
    return jnp.concatenate([ref[row + k : row + k + 1, :] for k in range(count)], 1)


def total(values):
    return jnp.sum(jnp.sum(values, 0, keepdims=True), 1, keepdims=True)


def pair(first, second):
    lanes = lax.broadcasted_iota(jnp.int32, (first.shape[0], LANES), 1)
    return jnp.where(lanes == 0, first, jnp.where(lanes == 1, second, 0.0))


def sum_rows(widths):
    starts = [0]
    for width in widths:
        starts.append(starts[-1] + 2 * width // LANES)
    scalars = -(-starts[-1] // 8) * 8
    return starts, scalars, scalars + 8


def layer_sums_kernel(*refs):
    grads, weights, stats = refs[:5], refs[5:10], refs[10:15]
    first_ref, second_ref, table_rows_ref, square_ref = refs[15:19]
    packed_ref, *new_refs = refs[19:]
    model = first_ref.shape[1]
    starts, scalars, table = sum_rows([ref.shape[1] for ref in grads[:4]])
    packed_ref[...] = jnp.zeros_like(packed_ref)
    for k in range(4):
        grad, weight = grads[k][...], weights[k][...]
        square = grad * grad
        full = square + SQUARE_EPS
        mean = jnp.sum(full, -1, keepdims=True) * (1.0 / grad.shape[1])
        new = DECAY * stats[k][...] + (1.0 - DECAY) * mean
        new_refs[k][...] = new
        count = grad.shape[1] // LANES
        put_rows(packed_ref, starts[k], jnp.sum(full, 0, keepdims=True))
        scaled = jnp.sum(square * (1.0 / new), 0, keepdims=True)
        put_rows(packed_ref, starts[k] + count, scaled)
        packed_ref[scalars + k : scalars + k + 1, :] = pair(total(new), total(weight * weight))
    grad, weight = grads[4][...], weights[4][...]
    new = DECAY * stats[4][...] + (1.0 - DECAY) * (grad * grad + SQUARE_EPS)
    new_refs[4][...] = new
    update = grad * lax.rsqrt(new)
    packed_ref[scalars + 4 : scalars + 8, :] = pair(
        jnp.sum(weight * weight, 1, keepdims=True), jnp.sum(update * update, 1, keepdims=True)
    )
    sums = first_ref[...] + second_ref[...]
    put_rows(packed_ref, table, jnp.sum(sums[0:8], 0, keepdims=True))
    put_rows(packed_ref, table + model // LANES, jnp.sum(sums[8:16], 0, keepdims=True))
    place = table + 2 * model // LANES
    packed_ref[place : place + 1, :] = pair(total(table_rows_ref[...]), total(square_ref[...]))


def layer_sums(grads, weights, stats, sums_first, sums_second, table_rows_new, squares):
    shapes = [stat.shape for stat in stats]
    _, _, table = sum_rows([grad.shape[1] for grad in grads[:4]])
    height = table + -(-(2 * sums_first.shape[1] // LANES + 1) // 8) * 8
    return pl.pallas_call(
        layer_sums_kernel,
        out_shape=[jax.ShapeDtypeStruct((height, LANES), jnp.float32)]
        + [jax.ShapeDtypeStruct(shape, jnp.float32) for shape in shapes],
        compiler_params=vmem(40),
        cost_estimate=small_cost(flops=0, bytes_accessed=1 << 22, transcendentals=0),
    )(*grads, *weights, *stats, sums_first, sums_second, table_rows_new, squares)


def factored_sizes(ref, start, scalar, col_stat, row_count):
    width = col_stat.shape[1]
    columns = got_rows(ref, start, width)
    scaled = got_rows(ref, start + width // LANES, width)
    rows_sum, weight_sum = ref[scalar : scalar + 1, 0:1], ref[scalar : scalar + 1, 1:2]
    new = DECAY * col_stat + (1.0 - DECAY) * columns * (1.0 / row_count)
    mean_rows = rows_sum * (1.0 / row_count)
    entries = row_count * width
    update_sum = mean_rows * jnp.sum(scaled / new, 1, keepdims=True)
    clipping = jnp.maximum(1.0, jnp.sqrt(update_sum * (1.0 / entries)))
    size = jnp.maximum(SCALE_FLOOR, jnp.sqrt(weight_sum * (1.0 / entries)))
    return new, mean_rows, RELATIVE_RATE * size / clipping


def layer_new_kernel(counts, totals_ref, *refs):
    grads, weights, rows, cols = refs[:5], refs[5:10], refs[10:15], refs[15:19]
    new_refs, col_refs = refs[19:24], refs[24:28]
    starts, scalars, _ = sum_rows([ref.shape[1] for ref in grads[:4]])
    for k in range(4):
        cols_new, mean_rows, rate = factored_sizes(
            totals_ref, starts[k], scalars + k, cols[k][...], counts[k]
        )
        col_refs[k][...] = cols_new
        scale = lax.rsqrt(rows[k][...] * cols_new / mean_rows)
        new_refs[k][...] = weights[k][...] - rate * (grads[k][...] * scale)
    model = counts[4]
    squares = totals_ref[scalars + 4 : scalars + 8, 0:1]
    updates = totals_ref[scalars + 4 : scalars + 8, 1:2]
    clipping = jnp.maximum(1.0, jnp.sqrt(updates * (1.0 / model)))
    size = jnp.maximum(SCALE_FLOOR, jnp.sqrt(squares * (1.0 / model)))
    update = grads[4][...] * lax.rsqrt(rows[4][...])
    new_refs[4][...] = weights[4][...] - RELATIVE_RATE * size / clipping * update


def layer_new(totals, grads, weights, rows, cols, counts):
    outs = [grad.shape for grad in grads] + [col.shape for col in cols]
    return pl.pallas_call(
        functools.partial(layer_new_kernel, counts),
        out_shape=[jax.ShapeDtypeStruct(shape, jnp.float32) for shape in outs],
        compiler_params=vmem(40),
        cost_estimate=small_cost(flops=0, bytes_accessed=1 << 22, transcendentals=0),
    )(totals, *grads, *weights, *rows, *cols)


def table_new_kernel(start, row_count, totals_ref, table_ref, grad_ref, rows_ref, cols_ref, *refs):
    new_ref, col_ref = refs
    scalar = start + 2 * cols_ref.shape[1] // LANES
    cols_new, mean_rows, rate = factored_sizes(totals_ref, start, scalar, cols_ref[...], row_count)
    col_ref[...] = cols_new
    across = rate * lax.rsqrt(cols_new)
    down = lax.rsqrt(rows_ref[...] / mean_rows)
    for k in range(rows_ref.shape[0]):
        place = slice(k * LANES, (k + 1) * LANES)
        scale = jnp.transpose(jnp.broadcast_to(down[k : k + 1, :], (LANES, LANES)))[:, 0:1]
        new_ref[place, :] = table_ref[place, :] - grad_ref[place, :] * scale * across


def table_new(totals, start, table, grad, rows_new, cols, row_count):
    vocab_here, model = table.shape
    block = row_block(vocab_here, 1024)
    rows = pl.BlockSpec((block, model), lambda i: (i, 0))
    return pl.pallas_call(
        functools.partial(table_new_kernel, start, row_count),
        grid=(vocab_here // block,),
        in_specs=[
            whole_block(totals.shape),
            rows,
            rows,
            pl.BlockSpec((block // LANES, LANES), lambda i: (i, 0)),
            whole_block(cols.shape),
        ],
        out_specs=[rows, whole_block(cols.shape)],
        out_shape=[
            jax.ShapeDtypeStruct(table.shape, jnp.float32),
            jax.ShapeDtypeStruct(cols.shape, jnp.float32),
        ],
        compiler_params=vmem(48),
        cost_estimate=small_cost(
            flops=4 * vocab_here * model,
            bytes_accessed=12 * vocab_here * model,
            transcendentals=0,
        ),
    )(totals, table, grad, rows_new, cols)


def body(
    token_ids,
    doc_lengths,
    picks,
    targets,
    table,
    table_rows,
    table_cols,
    attention_in,
    attention_in_rows,
    attention_in_cols,
    attention_out,
    attention_out_rows,
    attention_out_cols,
    hidden_in,
    hidden_in_rows,
    hidden_in_cols,
    hidden_out,
    hidden_out_rows,
    hidden_out_cols,
    gains,
    gains_stat,
):
    section = lax.axis_index("section")
    first = section == 0
    z, c = lax.axis_index("dp"), lax.axis_index("ctx")
    z_count, c_count = lax.axis_size("dp"), lax.axis_size("ctx")
    blocks = z_count * c_count
    model = table.shape[1]
    part = attention_in.shape[1]
    units = hidden_in.shape[2]
    half = units // (2 * blocks)
    wide = attention_in.shape[2]
    local_len = token_ids.shape[2]
    slots = picks.shape[2]
    vocab_here = table.shape[0]
    vocab_base = z * vocab_here

    low_in = bfloat(attention_in[0])
    low_out = jnp.concatenate(
        [bfloat(attention_out[0]), bfloat(gains[0]).T, jnp.zeros((part, wide - model - 4), jnp.bfloat16)], 1
    )
    barrier = lax.optimization_barrier
    at_p = jnp.concatenate(
        mine_first(
            jnp.where(first, low_in, low_out), swap(jnp.where(first, low_out, low_in))
        )
    )
    at_p, hidden_in_now, hidden_out_now = barrier((at_p, hidden_in, hidden_out))
    at_z = column_pieces(at_p)
    low_up = bfloat(hidden_in_now[0]).reshape(part, blocks, 2, half)
    low_down = bfloat(hidden_out_now[0])

    def unit_half(index):
        up = at(low_up, index, 2).reshape(part, -1, model)
        down = lax.dynamic_slice_in_dim(low_down, index * half, half, 0)
        return jnp.concatenate([up[:, k] for k in range(up.shape[1])] + [down])

    hid_p0, hid_p1 = mine_first(unit_half(section), swap(unit_half(1 - section)))

    room = local_len * 3 // 128 * 16

    hidden_w0 = lax.all_gather(hid_p0, BLOCKS, axis=0)

    if by_fours():
        slot, shard = distinct_slots(at(token_ids, section, 0), vocab_here)
        asked = asked_ids(at(token_ids, section, 0) - vocab_base, slot, shard == z, room)
        spilled = jnp.max(slot) >= room
        wanted = jnp.minimum(asked, vocab_here - 1).reshape(-1)
        place = at(jnp.where(slot < room, shard * room + slot, -1), z, 0)
        placed = bfloat(
            single(place[:, None] == jnp.arange(z_count * room, dtype=jnp.int32)[None, :])
        )
        notes = [asked.reshape(-1), spilled.astype(jnp.int32)[None], targets.reshape(-1)]
        notes = jnp.concatenate(notes)
        notes = jnp.stack(mine_first(notes, swap(notes)))
        x, y = plane_bits()
        beside = cross(notes, "ctx", 1)
        notes = jnp.stack([jnp.where(x == 0, notes, beside), jnp.where(x == 0, beside, notes)])
        above = cross(notes, "ctx", 2)
        notes = jnp.concatenate([jnp.where(y == 0, notes, above), jnp.where(y == 0, above, notes)])
        looked = picked_rows(after(wanted, at_p), table).reshape(z_count, room, model)
    else:
        my_ids = at(token_ids, section, 0) - vocab_base
        inside = (my_ids >= 0) & (my_ids < vocab_here)
        looked = jnp.take(table, jnp.clip(my_ids, 0, vocab_here - 1), axis=0)
        looked = jnp.where(inside[..., None], bfloat(looked), 0)
        notes = []

    at_z, hid_p1, looked, notes, table_now = barrier((at_z, hid_p1, looked, notes, table))
    at_c = column_join(at_p, at_z)
    at_n = plane_near(at_c)
    start_pieces = row_pieces(looked)
    low_first, square_first = lowered(table_now, None, 0, 3)
    at_n, start_pieces, low_first, hid_p1 = barrier((at_n, start_pieces, low_first, hid_p1))
    at_f = plane_far(at_n)
    hid_z1 = column_pieces(hid_p1)
    table_low, square_second = lowered(table, low_first, 1, 3)
    at_f, table_low, at_c = barrier((at_f, table_low, at_c))
    at_w = plane_list(at_c, at_n, at_f)
    if by_fours():
        at_w = jnp.concatenate(at_w)
    at_o = swap(at_w)
    table_low, square_third = lowered(table, table_low, 2, 3)
    at_o, table_low = barrier((at_o, table_low))
    if by_fours():
        target_notes = notes[:, 0, asked.size + 1 :]
        asked_all = notes[..., : asked.size].reshape(c_count, 2, z_count, room)
        local = jnp.minimum(asked_all.transpose(1, 2, 0, 3).reshape(-1), vocab_here)
        order = jnp.arange(local.shape[0], dtype=jnp.int32)
        local, order = lax.sort((local, order), num_keys=1)
        block = row_block(vocab_here, 1024)
        edges = jnp.arange(vocab_here // block + 1, dtype=jnp.int32) * block
        starts = jnp.sum((local[None, :] < edges[:, None]).astype(jnp.int32), 1)
    else:
        local = order = starts = notes
    in0, out0, gains0 = attention_weights(at_w, at_o, model, 0)
    if by_fours():
        spilled = jnp.max(notes[..., asked.size]) > 0
        found = column_join(at(looked, z, 0), start_pieces)
        start = matmul(placed, found.reshape(-1, model))
        start = start + lax.cond(
            spilled,
            lambda: spilled_rows(token_ids, slot, room, table),
            lambda: jnp.zeros_like(start),
        )
    else:
        target_notes = lax.all_gather(targets, "ctx")
        start = row_sum(looked, start_pieces)
    lengths = at(doc_lengths, section, 0)[0]
    my_picks = at(picks, section, 0)[0]

    places = c * local_len + jnp.arange(local_len, dtype=jnp.int32)
    reach = earlier_count(local_len)
    key_places = (c - reach) * local_len + jnp.arange((reach + 1) * local_len, dtype=jnp.int32)
    bias = pair_bias(lengths, places, key_places)
    pick_bias = pair_bias(lengths, c * local_len + jnp.maximum(my_picks, 0), key_places)
    onehot = (my_picks[:, None] == jnp.arange(local_len, dtype=jnp.int32)[None, :]).astype(
        jnp.bfloat16
    )

    normed0 = bfloat(layer_norm(start, gains0[0], gains0[1]))
    mixed_in = matmul(normed0, in0)
    query0 = bfloat(mixed_in[:, :model] * HD ** (-0.5))
    keyval0, query0, local, order, starts = barrier(
        (bfloat(mixed_in[:, model:]), query0, local, order, starts)
    )
    keyval0, query0, hid_z1 = barrier((key_rows(keyval0), query0, hid_z1))
    hid_c1 = column_join(hid_p1, hid_z1)
    hid_n1 = plane_near_half(hid_c1, 0)
    attended0 = attend(query0, keyval0, bias)
    mixed0 = start + matmul(attended0, out0)
    normed_two0 = bfloat(layer_norm(mixed0, gains0[2], gains0[3]))
    hid_n1, mixed0, normed_two0 = barrier((hid_n1, mixed0, normed_two0))
    both0, hid_c1 = barrier((both_rows(normed_two0), hid_c1))
    hid_m1 = plane_near_half(hid_c1, 1)
    upper0, partial = hidden_forward(both0, hidden_w0)
    in1, out1, gains1 = attention_weights(at_w, at_o, model, 1)
    hid_m1, partial, in1, out1 = barrier((hid_m1, partial, in1, out1))
    hid_f1 = plane_far_half(hid_n1, hid_m1)
    result0 = mixed0 + own_rows(partial)

    inputs1_low = bfloat(result0)
    inputs1 = single(inputs1_low)
    normed1 = bfloat(layer_norm(inputs1, gains1[0], gains1[1]))
    keyval1 = bfloat(matmul(normed1, in1[:, model:]))
    picked_normed = bfloat(matmul(onehot, normed1))
    picked = matmul(onehot, inputs1_low)
    query1 = bfloat(matmul(picked_normed, in1[:, :model]) * HD ** (-0.5))
    keyval1, query1, hid_f1 = barrier((keyval1, query1, hid_f1))
    keyval1 = key_rows(keyval1)
    hidden_w1 = plane_halves(hid_c1, (hid_n1, hid_m1), hid_f1)
    all_targets = target_notes.reshape((c_count,) + targets.shape).transpose(1, 2, 0, 3).reshape(-1)
    heads1 = query1.reshape(slots, -1, HD).transpose(1, 0, 2).reshape(-1, HD)
    heads1 = jnp.concatenate([heads1, jnp.zeros_like(heads1)], 1)
    pick_bias = jnp.tile(pick_bias, (model // HD, 1))

    def side_by_side(heads):
        return heads.reshape(-1, slots, HD).transpose(1, 0, 2).reshape(slots, model)

    attended1 = side_by_side(attend(heads1, keyval1, pick_bias)[:, :HD])
    mixed1 = picked + matmul(attended1, out1)
    normed_two1 = bfloat(layer_norm(mixed1, gains1[2], gains1[3]))
    both1 = both_rows(normed_two1)
    upper1, partial = hidden_forward(both1, hidden_w1)
    result1 = mixed1 + own_rows(partial)

    chosen_mine = gather_blocks(bfloat(result1)).reshape(-1, model)
    chosen = jnp.concatenate(mine_first(chosen_mine, swap(chosen_mine)))
    live = all_targets >= 0
    local_target = jnp.where(live, all_targets - vocab_base, DEAD)
    across = chosen.T
    stats = head_stats(across, local_target[None], table_low)

    def combine(one, two):
        top = jnp.maximum(one[0], two[0])
        both = one[1] * jnp.exp(one[0] - top) + two[1] * jnp.exp(two[0] - top)
        return jnp.stack([top, both, one[2] + two[2]])

    if by_fours():
        stats = stats[:3]
        one, two, three = (cross(stats, "dp", k) for k in (1, 2, 3))
        stats = combine(combine(stats, one), combine(two, three))
    else:
        stats = lax.scan(
            lambda total, share: (combine(total, share), None),
            jnp.stack([jnp.full_like(stats[0], MASKED), 0 * stats[0], 0 * stats[0]]),
            lax.all_gather(stats, "dp"),
        )[0]
    logsum = stats[0] + jnp.log(stats[1])
    loss_sum = jnp.sum(jnp.where(live, logsum - stats[2], 0.0))
    loss_count = jnp.sum(single(live))

    def own_slots(values):
        shape = (2, z_count, c_count, slots) + values.shape[1:]
        return at(at(values.reshape(shape), section, 0), c, 1).reshape((-1,) + values.shape[1:])

    grad_chosen = head_rows(
        own_slots(chosen), own_slots(local_target)[:, None], own_slots(logsum)[:, None], table_low
    )
    grad_result1 = scatter_rows(grad_chosen.reshape(z_count, slots, model))

    def attention_grads(grad_in, grad_out, grad_gains):
        grad_out = jnp.concatenate(
            [
                bfloat(grad_out),
                bfloat(grad_gains).T,
                jnp.zeros((model, wide - model - 4), jnp.bfloat16),
            ],
            1,
        )
        grad_in = bfloat(grad_in)
        return jnp.where(first, grad_in, grad_out), jnp.where(first, grad_out, grad_in)

    low = bfloat(grad_result1)
    partial, hidden_grads1 = hidden_backward(both1, upper1, both_rows(low), hidden_w1)
    hidden1 = scattered(hidden_grads1)
    _, pull = jax.vjp(layer_norm, mixed1, gains1[2], gains1[3])
    grad_mixed1, grad_gain2, grad_shift2 = pull(own_rows(partial))
    grad_mixed1 = grad_mixed1 + grad_result1
    grad_low = bfloat(grad_mixed1)
    grad_out1 = matmul_left(attended1, grad_low)
    grad_heads = bfloat(matmul_right(grad_low, out1)).reshape(slots, -1, HD)
    grad_heads = grad_heads.transpose(1, 0, 2).reshape(-1, HD)
    grad_heads = jnp.concatenate([grad_heads, jnp.zeros_like(grad_heads)], 1)
    grad_query, grad_keyval = attend_back(heads1, keyval1, pick_bias, grad_heads)
    grad_query = side_by_side(grad_query[:, :HD])
    grad_keyval = key_rows_sum(grad_keyval, key_rows_back(grad_keyval, local_len), local_len)
    grad_in1 = jnp.concatenate(
        [matmul_left(picked_normed, grad_query), matmul_left(normed1, grad_keyval)], 1
    )
    spread = jnp.dot(
        single(onehot).T,
        jnp.concatenate([matmul_right(grad_query, in1[:, :model]), grad_mixed1], 1),
        precision=lax.Precision.HIGHEST,
    )
    grad_normed = matmul_right(grad_keyval, in1[:, model:]) + spread[:, :model]
    _, pull = jax.vjp(layer_norm, inputs1, gains1[0], gains1[1])
    grad_inputs1, grad_gain1, grad_shift1 = pull(grad_normed)
    grad_result0 = single(bfloat(grad_inputs1 + spread[:, model:]))
    grad_gains1 = jnp.stack([grad_gain1, grad_shift1, grad_gain2, grad_shift2])
    kept1, sent1 = attention_grads(grad_in1, grad_out1, grad_gains1)

    low = bfloat(grad_result0)
    partial, hidden_grads0 = hidden_backward(both0, upper0, both_rows(low), hidden_w0)
    every, wide_rows = (0, 2 * part + half), (0, 2 * part)
    partial, hidden_grads0, sent1 = barrier((own_rows(partial), hidden_grads0, swap(sent1)))
    hid_s = half_first(hidden_grads0, every) if by_fours() else ()
    _, pull = jax.vjp(layer_norm, mixed0, gains0[2], gains0[3])
    grad_mixed0, grad_gain2, grad_shift2 = pull(partial)
    grad_mixed0 = grad_mixed0 + grad_result0
    grad_low = bfloat(grad_mixed0)
    grad_out0 = matmul_left(attended0, grad_low)
    grad_query, grad_keyval = attend_back(
        query0, keyval0, bias, bfloat(matmul_right(grad_low, out0))
    )
    grad_query, grad_keyval = barrier((grad_query, grad_keyval))
    returned, hid_s = barrier((key_rows_back(grad_keyval, local_len), hid_s))
    if by_fours():
        hid_k, hid_h = half_kept(hidden_grads0, every, hid_s)
    grad_keyval = key_rows_sum(grad_keyval, returned, local_len)
    grad_mixed_in = jnp.concatenate([grad_query, grad_keyval], 1)
    grad_in0 = matmul_left(normed0, grad_mixed_in)
    _, pull = jax.vjp(layer_norm, start, gains0[0], gains0[1])
    grad_start, grad_gain1, grad_shift1 = pull(matmul_right(grad_mixed_in, in0))
    grad_start = bfloat(grad_start + grad_mixed0)
    grad_gains0 = jnp.stack([grad_gain1, grad_shift1, grad_gain2, grad_shift2])
    kept0, sent0 = attention_grads(grad_in0, grad_out0, grad_gains0)
    def owned(one, two):
        return mine_first(jnp.where(first, one, two), swap(jnp.where(first, two, one)))

    def hidden_shards(one, two):
        halves = jnp.stack(owned(one, two))
        ups = units // 2 // model
        up = halves[:, : ups * part].reshape(2, ups, part, model).transpose(2, 0, 1, 3)
        up = up.reshape(part, 2, blocks, half).transpose(0, 2, 1, 3).reshape(part, units)
        return up, halves[:, ups * part :].reshape(2 * half, model)

    def head_part(grads, index, count):
        return head_table(
            chosen, across, local_target[None], logsum[None], table_low, grads, index, count
        )

    table_square = square_first + square_second + square_third
    if by_fours():
        sent = bfloat(matmul_left(placed, grad_start)).reshape(z_count, room, model)
        sent, hid_h = barrier((sent, hid_h))
        row_z = row_pieces(sent)
        hid_t = half_send(hid_h)
        chosen = after(chosen, sent)
        grad_head = head_part(None, 0, 3)
        row_z, grad_head, hid_t, kept0, sent0 = barrier((row_z, grad_head, hid_t, kept0, sent0))
        column = column_join(at(sent, z, 0), row_z)
        near = plane_near(column)
        other, sent0 = swap((column, sent0))
        hid_v = half_column(hid_k, hid_t)
        grad_head = head_part(grad_head, 1, 3)
        near, grad_head, other, sent0, hid_v = barrier((near, grad_head, other, sent0, hid_v))
        far = plane_far(near)
        attention_both = attention_sums((kept0, sent0, kept1, sent1), blocks)
        at_s = half_first(attention_both, wide_rows)
        grad_head = head_part(grad_head, 2, 3)
        grad_head = lax.while_loop(
            lambda carry: carry[0] < spilled.astype(jnp.int32),
            lambda carry: (
                carry[0] + 1,
                carry[1] + spilled_grads(token_ids, slot, room, grad_start, vocab_here),
            ),
            (jnp.zeros((), jnp.int32), grad_head),
        )[1]
        far, grad_head, hidden1 = barrier((far, grad_head, hidden1))
        far = jnp.concatenate(far)
        others, hid_v = barrier((swap((*near, far)), hid_v))
        hid_q = row_pieces(hid_v)
        pieces = (column, *near, far, other, *others)
        parts = (starts, local, order, pieces, grad_head, table_rows, block)
        grad_table, rows_new, sums_first = table_sums(*parts, None, 0, 3)
        at_s, hid_q, grad_table, rows_new = barrier((at_s, hid_q, grad_table, rows_new))
        at_k, at_h = half_kept(attention_both, wide_rows, at_s)
        at_t = half_send(at_h)
        grad_table, rows_new, sums_second = table_sums(*parts, (grad_table, rows_new), 1, 3)
        at_t, grad_table, rows_new = barrier((at_t, grad_table, rows_new))
        at_v = half_column(at_k, at_t)
        at_q = row_pieces(at_v)
        shard_up, shard_down = hidden_shards(row_sum(hid_v, hid_q), hidden1)
        grad_table, rows_new, sums_third = table_sums(*parts, (grad_table, rows_new), 2, 3)
        sums_second = sums_second + sums_third
        at_q, grad_table, rows_new, shard_up, shard_down = barrier(
            (at_q, grad_table, rows_new, shard_up, shard_down)
        )
        attention = row_sum(at_v, at_q)
    else:
        hidden0 = scattered(hidden_grads0)
        attention_both = attention_sums((kept0, swap(sent0), kept1, sent1), blocks)
        attention = scattered(attention_both)
        column = lax.all_gather(grad_start, "dp").reshape(-1, model)
        local = jnp.where(inside, my_ids, vocab_here).reshape(-1)
        lookup_grad = jax.ops.segment_sum(single(column), local, num_segments=vocab_here)
        lookup_grad = single(lax.psum(bfloat(lookup_grad), ("section", "ctx")))
        grad_table = head_part(None, 0, 1) + lookup_grad
        table_sum = (
            *factored_sums(table, grad_table, table_rows)[:4],
            jnp.sum(table_square),
        )

    if not by_fours():
        shard_up, shard_down = hidden_shards(hidden0, hidden1)
    shard_in, shard_out = owned(attention[:part], attention[part:])
    shard_gains = shard_out[:, model : model + 4].T
    shard_out = shard_out[:, :model]

    if by_fours():
        grads = (shard_in, shard_out, shard_up, shard_down, shard_gains)
        weights = (attention_in[0], attention_out[0], hidden_in[0], hidden_out[0], gains[0])
        rows = (attention_in_rows, attention_out_rows, hidden_in_rows, hidden_out_rows)
        rows = [stat.reshape(-1, 1) for stat in rows] + [gains_stat[0]]
        sums, *rows_news = layer_sums(
            grads, weights, rows, sums_first, sums_second, rows_new, table_square
        )
        sums = summed(sums, ("dp",))
        _, _, table_start = sum_rows([grad.shape[1] for grad in grads[:4]])
        layer_totals = summed(sums[:table_start], ("ctx",))
        table_news, table_cols_new = table_new(
            sums, table_start, table, grad_table, rows_new, table_cols[None], vocab_here * z_count
        )
        cols = (attention_in_cols, attention_out_cols, hidden_in_cols, hidden_out_cols)
        *news, in_cols, out_cols, up_cols, down_cols = layer_new(
            layer_totals, grads, weights, rows_news, cols, (model, model, model, units, model)
        )
        layered = []
        for k, cols_new in enumerate((in_cols, out_cols, up_cols, down_cols)):
            layered += [grads[k][None], rows_news[k].reshape(1, -1), cols_new, news[k][None]]
        return (
            loss_sum,
            loss_count,
            grad_table,
            rows_new.reshape(-1),
            table_cols_new[0],
            table_news,
            *layered,
            shard_gains[None],
            rows_news[4][None],
            news[4][None],
        )
    entries = [
        (table, grad_table, table_rows, table_cols, vocab_here * z_count),
        (attention_in[0], shard_in, attention_in_rows[0], attention_in_cols[0], model),
        (attention_out[0], shard_out, attention_out_rows[0], attention_out_cols[0], model),
        (hidden_in[0], shard_up, hidden_in_rows[0], hidden_in_cols[0], model),
        (hidden_out[0], shard_down, hidden_out_rows[0], hidden_out_cols[0], units),
    ]
    sums = [table_sum] + [factored_sums(*entry[:3]) for entry in entries[1:]]
    gain_weight = gains[0]
    gain_stat_new = DECAY * gains_stat[0] + (1.0 - DECAY) * (shard_gains * shard_gains + SQUARE_EPS)
    gain_update = shard_gains * lax.rsqrt(gain_stat_new)

    def packed(group):
        rows = []
        for item in group:
            flat = item.reshape(-1)
            if flat.shape[0] % LANES:
                flat = jnp.pad(flat, (0, LANES - flat.shape[0]))
            rows.append(flat.reshape(-1, LANES))
        return jnp.concatenate(rows), [item.shape for item in group]

    def unpacked(rows, shapes):
        items, start = [], 0
        for shape in shapes:
            size = 1
            for length in shape:
                size *= length
            count = -(-size // LANES)
            items.append(rows[start : start + count].reshape(-1)[:size].reshape(shape))
            start += count
        return items

    table_group, table_shapes = packed(sums[0][1:])
    layer_group, layer_shapes = packed(
        [item for entry in sums[1:] for item in entry[1:]]
        + [jnp.sum(gain_weight * gain_weight, -1), jnp.sum(gain_update * gain_update, -1)]
    )
    everything = summed(jnp.concatenate([table_group, layer_group]), ("dp",))
    table_totals = unpacked(everything[: table_group.shape[0]], table_shapes)
    layer_parts = unpacked(summed(everything[table_group.shape[0] :], ("ctx",)), layer_shapes)
    groups = [table_totals] + [layer_parts[4 * k : 4 * k + 4] for k in range(4)]
    gain_squares, gain_update_sums = layer_parts[16:]
    outs = []
    for (weight, gradient, _, col_stat, row_count), own, group in zip(entries, sums, groups):
        cols_new, new = factored_new(weight, gradient, own[0], col_stat, group, row_count)
        outs.append((gradient, own[0], cols_new, new))
    gain_clipping = jnp.maximum(1.0, jnp.sqrt(gain_update_sums / model))
    gain_size = jnp.maximum(SCALE_FLOOR, jnp.sqrt(gain_squares / model))
    gain_new = gain_weight - RELATIVE_RATE * gain_size[:, None] * (
        gain_update / gain_clipping[:, None]
    )
    layered = [item[None] for out in outs[1:] for item in out]
    return (
        loss_sum,
        loss_count,
        *outs[0],
        *layered,
        shard_gains[None],
        gain_stat_new[None],
        gain_new[None],
    )


def solution(mesh):
    rows = P("section", BLOCKS, None)
    row = P("section", BLOCKS)
    shared = P("section", None)
    side = P("section", None, BLOCKS)
    matrix_in = (rows, row, shared)
    matrix_out = (rows, row, shared, rows)
    placed = (
        P(None, None, "ctx"),
        P(None, "dp", None),
        P(None, "dp", "ctx"),
        P(None, None, "ctx"),
        P("dp", None),
        P("dp"),
        P(),
        *(matrix_in * 4),
        side,
        side,
    )
    return jax.shard_map(
        body,
        mesh=mesh,
        in_specs=placed,
        out_specs=(
            P(),
            P(),
            P("dp", None),
            P("dp"),
            P(),
            P("dp", None),
            *(matrix_out * 4),
            side,
            side,
            side,
        ),
        check_vma=False,
    )
```

```python
import functools

import jax
import jax.numpy as jnp
from jax import lax
from jax.experimental import pallas as pl
from jax.experimental.pallas import tpu as pltpu
from jax.sharding import PartitionSpec as P

HD = 64
WINDOW = 512
STEP = 10
NORM_EPS = 1e-05
SQUARE_EPS = 1e-30
SCALE_FLOOR = 0.001
RELATIVE_RATE = 0.5
MASKED = -1e30
DECAY = 1.0 - STEP ** (-0.8)
BLOCKS = ("dp", "ctx")
LANES = 128
DEAD = -(1 << 30)
MIB = 1 << 20


def bfloat(values):
    return values.astype(jnp.bfloat16)


def single(values):
    return values.astype(jnp.float32)


def matmul(left, right):
    return jnp.dot(left, right, preferred_element_type=jnp.float32)


def matmul_left(left, right):
    return lax.dot_general(
        left, right, (((0,), (0,)), ((), ())), preferred_element_type=jnp.float32
    )


def matmul_right(left, right):
    return lax.dot_general(
        left, right, (((1,), (1,)), ((), ())), preferred_element_type=jnp.float32
    )


def layer_norm(values, gain, shift):
    center = values - jnp.mean(values, -1, keepdims=True)
    spread = jnp.mean(center * center, -1, keepdims=True)
    return center * lax.rsqrt(spread + NORM_EPS) * gain + shift


def gelu_tanh(values):
    return jax.nn.gelu(values, approximate=True)


def at(values, index, axis):
    return lax.dynamic_index_in_dim(values, index, axis, keepdims=False)


def swap(values):
    return lax.ppermute(values, "section", [(0, 1), (1, 0)])


def cross(values, axis, bits):
    return lax.ppermute(values, axis, [(i, i ^ bits) for i in range(lax.axis_size(axis))])


def shifted(values, axis, distance):
    devices = range(lax.axis_size(axis))
    return lax.ppermute(
        values, axis, [(i, i + distance) for i in devices if i + distance in devices]
    )


def by_fours():
    return lax.axis_size("dp") == 4 and lax.axis_size("ctx") == 4


def mine_first(mine, theirs):
    first = lax.axis_index("section") == 0
    return jnp.where(first, mine, theirs), jnp.where(first, theirs, mine)


def after(values, *earlier):
    return lax.optimization_barrier((values, *earlier))[0]


def column_pieces(part):
    if not by_fours():
        return (lax.all_gather(part, "dp", axis=0),)
    return tuple(cross(part, "dp", k) for k in (1, 2, 3))


def column_join(part, pieces):
    if not by_fours():
        return pieces[0]
    return in_order((part, *pieces), "dp")


def plane_near(column):
    if not by_fours():
        return (lax.all_gather(column, "ctx", axis=1),)
    return cross(column, "ctx", 1), cross(column, "ctx", 2)


def plane_far(near):
    if not by_fours():
        return ()
    beside, above = near
    return cross(above[:2], "ctx", 1), cross(beside[2:], "ctx", 2)


def plane_list(column, near, far):
    if not by_fours():
        return near[0].reshape((-1,) + column.shape[1:])
    return (column, *near, jnp.concatenate(far))


def plane_near_half(column, side):
    if not by_fours():
        return plane_near(column) if side == 0 else ()
    return plane_near(column[2 * side : 2 * side + 2])


def plane_far_half(first, second):
    if not by_fours():
        return ()
    return cross(first[1], "ctx", 1), cross(second[0], "ctx", 2)


def plane_halves(column, near, far):
    if not by_fours():
        return plane_list(column, near[0], far)
    return (column, *zip(*near), tuple(far))


def in_order(pieces, axis, at_axis=0):
    i = lax.axis_index(axis)
    return jnp.stack(
        [lax.select_n(i, *[pieces[place ^ k] for k in range(4)]) for place in range(4)], at_axis
    )


def weights_kernel(place_ref, *refs):
    mine, theirs, in_ref, out_ref = refs
    c, first = place_ref[0], place_ref[1] == 0
    part = mine.shape[1]

    def lay(ref, pieces):
        for k in range(4):
            for z in range(4):
                rows = pl.ds(pl.multiple_of((4 * z + (c ^ k)) * part, 16), part)
                ref[rows, :] = pieces[4 * k + z]

    @pl.when(first)
    def _():
        lay(in_ref, mine)
        lay(out_ref, theirs)

    @pl.when(~first)
    def _():
        lay(in_ref, theirs)
        lay(out_ref, mine)


def attention_weights(mine, theirs, model, layer):
    if by_fours():
        blocks, both, wide = mine.shape
        place = jnp.stack([lax.axis_index("ctx"), lax.axis_index("section")])
        weight_in, weight_out = pl.pallas_call(
            weights_kernel,
            grid_spec=pltpu.PrefetchScalarGridSpec(
                num_scalar_prefetch=1,
                grid=(1,),
                in_specs=[pl.BlockSpec((blocks, both // 2, wide), lambda *_: (0, layer, 0))] * 2,
                out_specs=[whole_block((model, wide))] * 2,
            ),
            out_shape=[jax.ShapeDtypeStruct((model, wide), jnp.bfloat16)] * 2,
            compiler_params=vmem(24),
            cost_estimate=small_cost(
                flops=0, bytes_accessed=8 * model * wide, transcendentals=0
            ),
        )(place, mine, theirs)
    else:
        part = mine.shape[1] // 2
        weights = mine_first(mine, theirs)
        weight_in, weight_out = (
            w[:, layer * part : (layer + 1) * part].reshape(model, -1) for w in weights
        )
    return weight_in, weight_out[:, :model], single(weight_out[:, model : model + 4]).T


def gather_blocks(part):
    return gather_ctx(column_join(part, column_pieces(part))).swapaxes(0, 1).reshape(
        (-1,) + part.shape
    )


def gather_ctx(part):
    if not by_fours():
        return lax.all_gather(part, "ctx", axis=0)
    return in_order([part] + [cross(part, "ctx", k) for k in (1, 2, 3)], "ctx")


def scattered(parts):
    return single(lax.psum_scatter(parts, BLOCKS, scatter_dimension=0))


def corner(parts, rows, z, y=None, x=None):
    grid = parts.reshape((4, 2, 2) + parts.shape[1:])
    first, count = rows
    start = (z, 0 if y is None else y, 0 if x is None else x, first, 0)
    size = (2, 2 if y is None else 1, 2 if x is None else 1, count, parts.shape[2])
    return lax.dynamic_slice(grid, start, size)


def plane_bits():
    c = lax.axis_index("ctx")
    return c & 1, c >> 1


def half_first(parts, rows):
    x, y = plane_bits()
    return (
        cross(corner(parts, rows, 0, x=1 - x), "ctx", 1),
        cross(corner(parts, rows, 2, y=1 - y), "ctx", 2),
    )


def half_kept(parts, rows, got):
    x, y = plane_bits()
    near = bfloat(single(corner(parts, rows, 0, x=x)) + single(got[0]))
    far = bfloat(single(corner(parts, rows, 2, y=y)) + single(got[1]))
    near, far = near[:, :, 0], far[:, 0]
    return (at(near, y, 1), at(far, x, 1)), (at(near, 1 - y, 1), at(far, 1 - x, 1))


def half_send(halves):
    return cross(halves[0], "ctx", 2), cross(halves[1], "ctx", 1)


def half_column(kept, got):
    return jnp.concatenate([bfloat(single(one) + single(two)) for one, two in zip(kept, got)])


def row_pieces(parts):
    if not by_fours():
        return (lax.psum_scatter(bfloat(parts), "dp", scatter_dimension=0),)
    z = lax.axis_index("dp")
    low = bfloat(parts)
    return tuple(cross(at(low, z ^ k, 0), "dp", k) for k in (1, 2, 3))


def row_sum(parts, pieces):
    total = single(pieces[0])
    for piece in pieces[1:]:
        total = total + single(piece)
    return single(at(parts, lax.axis_index("dp"), 0)) + total if by_fours() else total


def scatter_rows(parts):
    return row_sum(parts, row_pieces(parts))


def summed(values, axes):
    if not by_fours():
        return lax.psum(values, axes)
    for axis in axes:
        one, two, three = (cross(values, axis, k) for k in (1, 2, 3))
        values = (values + one) + (two + three)
    return values


def doc_numbers(lengths, places):
    bounds = jnp.cumsum(lengths)
    return jnp.sum((places[:, None] >= bounds[None, :]).astype(jnp.int32), -1)


def pair_bias(lengths, query_places, key_places):
    query_docs = doc_numbers(lengths, query_places)
    key_docs = doc_numbers(lengths, key_places)
    allowed = (
        (key_places[None, :] <= query_places[:, None])
        & (key_places[None, :] > query_places[:, None] - WINDOW)
        & (key_places[None, :] >= 0)
        & (key_docs[None, :] == query_docs[:, None])
    )
    return jnp.where(allowed, 0.0, MASKED)


def earlier_count(local_len):
    return min(lax.axis_size("ctx") - 1, -(-(WINDOW - 1) // local_len))


def key_rows(keyval):
    reach = earlier_count(keyval.shape[0])
    return jnp.concatenate(
        [shifted(keyval, "ctx", k) for k in range(reach, 0, -1)] + [keyval]
    )


def key_rows_back(grads, local_len):
    reach = earlier_count(local_len)
    starts = [(reach - k) * local_len for k in range(1, reach + 1)]
    return tuple(
        shifted(grads[start : start + local_len], "ctx", -(k + 1))
        for k, start in enumerate(starts)
    )


def key_rows_sum(grads, pieces, local_len):
    total = grads[earlier_count(local_len) * local_len :]
    for piece in pieces:
        total = total + piece
    return bfloat(total)


def whole_block(shape):
    return pl.BlockSpec(shape, lambda *_: (0,) * len(shape))


def vmem(mebibytes):
    return pltpu.CompilerParams(vmem_limit_bytes=mebibytes * MIB)


def small_cost(flops, bytes_accessed, transcendentals):
    return pl.CostEstimate(
        flops=flops // 16, bytes_accessed=bytes_accessed // 16, transcendentals=0 * transcendentals
    )


def row_block(rows, most):
    block = most
    while rows % block:
        block //= 2
    return block


def turned(values):
    return pltpu.roll(values, HD, 1)


def softmax_rows(scores):
    exponents = jnp.exp(scores - jnp.max(scores, -1, keepdims=True))
    return exponents * (1.0 / jnp.sum(exponents, -1, keepdims=True))


def attend_kernel(query_ref, keyval_ref, bias_ref, out_ref):
    keyval = keyval_ref[...]
    bias = bias_ref[...]
    pair = single(query_ref[...])
    left = lax.broadcasted_iota(jnp.int32, pair.shape, 1) < HD
    outs = []
    for heads in (pair, turned(pair)):
        query = bfloat(jnp.where(left, heads, 0.0))
        probs = softmax_rows(matmul_right(query, keyval) + bias)
        outs.append(matmul(bfloat(probs), keyval))
    out_ref[...] = bfloat(jnp.where(left, turned(outs[0]), outs[1]))


def attend(query, keyval, bias):
    rows, columns = query.shape
    pair = 2 * HD
    return pl.pallas_call(
        attend_kernel,
        grid=(columns // pair,),
        in_specs=[
            pl.BlockSpec((rows, pair), lambda i: (0, i)),
            whole_block(keyval.shape),
            whole_block(bias.shape),
        ],
        out_specs=pl.BlockSpec((rows, pair), lambda i: (0, i)),
        out_shape=jax.ShapeDtypeStruct((rows, columns), jnp.bfloat16),
        compiler_params=vmem(40),
        cost_estimate=small_cost(
            flops=4 * rows * columns * keyval.shape[0],
            bytes_accessed=8 * rows * columns,
            transcendentals=rows * columns * keyval.shape[0] // HD,
        ),
    )(query, keyval, bias)


def attend_back_kernel(query_ref, keyval_ref, bias_ref, grad_ref, grad_query_ref, grad_keyval_ref):
    keyval = keyval_ref[...]
    bias = bias_ref[...]
    pair = single(query_ref[...])
    grads = single(grad_ref[...])
    left = lax.broadcasted_iota(jnp.int32, pair.shape, 1) < HD
    total = jnp.where(pl.program_id(0) == 0, 0.0, grad_keyval_ref[...])
    outs = []
    for heads, grad_heads in ((pair, turned(grads)), (turned(pair), grads)):
        query = bfloat(jnp.where(left, heads, 0.0))
        grad = bfloat(jnp.where(left, 0.0, grad_heads))
        probs = softmax_rows(matmul_right(query, keyval) + bias)
        grad_probs = matmul_right(grad, keyval)
        inner = jnp.sum(probs * grad_probs, -1, keepdims=True)
        grad_scores = bfloat(probs * (grad_probs - inner))
        outs.append(matmul(grad_scores, keyval))
        total = total + matmul_left(grad_scores, query) + matmul_left(bfloat(probs), grad)
    grad_keyval_ref[...] = total
    grad_query = single(bfloat(jnp.where(left, outs[0], turned(outs[1])))) * HD ** (-0.5)
    grad_query_ref[...] = bfloat(grad_query)


def attend_back(query, keyval, bias, grad_out):
    rows, columns = query.shape
    pair = 2 * HD
    pairs = pl.BlockSpec((rows, pair), lambda i: (0, i))
    return pl.pallas_call(
        attend_back_kernel,
        grid=(columns // pair,),
        in_specs=[pairs, whole_block(keyval.shape), whole_block(bias.shape), pairs],
        out_specs=[pairs, whole_block(keyval.shape)],
        out_shape=[
            jax.ShapeDtypeStruct((rows, columns), jnp.bfloat16),
            jax.ShapeDtypeStruct(keyval.shape, jnp.float32),
        ],
        compiler_params=vmem(48),
        cost_estimate=small_cost(
            flops=10 * rows * columns * keyval.shape[0],
            bytes_accessed=8 * rows * columns,
            transcendentals=rows * columns * keyval.shape[0] // HD,
        ),
    )(query, keyval, bias, grad_out)


def lower_kernel(table_ref, *refs):
    low_ref, square_ref = refs[-2:]
    weights = table_ref[...]
    low_ref[...] = bfloat(weights)
    squares = jnp.sum((weights * weights).reshape(-1, 8, weights.shape[1]), 0)
    square_ref[...] = jnp.where(pl.program_id(0) == 0, 0.0, square_ref[...]) + squares


def lowered(table, low, index, count):
    vocab_here, model = table.shape
    block = row_block(vocab_here, 1024)
    steps = vocab_here // block
    first, last = index * steps // count, (index + 1) * steps // count
    rows = pl.BlockSpec((block, model), lambda i: (i + first, 0))
    return pl.pallas_call(
        lower_kernel,
        grid=(last - first,),
        in_specs=[rows] + ([] if low is None else [pl.BlockSpec(memory_space=pl.ANY)]),
        out_specs=[rows, whole_block((8, model))],
        out_shape=[
            jax.ShapeDtypeStruct(table.shape, jnp.bfloat16),
            jax.ShapeDtypeStruct((8, model), jnp.float32),
        ],
        input_output_aliases={} if low is None else {1: 0},
        compiler_params=vmem(40),
        cost_estimate=small_cost(
            flops=2 * vocab_here * model // count,
            bytes_accessed=6 * vocab_here * model // count,
            transcendentals=0,
        ),
    )(*((table,) if low is None else (table, low)))


def head_stats_kernel(chosen_ref, target_ref, low_ref, stats_ref):
    step = pl.program_id(0)
    rows = low_ref.shape[0]

    @pl.when(step == 0)
    def _():
        stats_ref[...] = jnp.zeros_like(stats_ref)
        stats_ref[0:1, :] = jnp.full((1, stats_ref.shape[1]), MASKED, jnp.float32)

    logits = matmul(low_ref[...], chosen_ref[...])
    places = lax.broadcasted_iota(jnp.int32, logits.shape, 0)
    matches = places == target_ref[...] - step * rows
    before, totals = stats_ref[0:1, :], stats_ref[1:2, :]
    highest = jnp.maximum(before, jnp.max(logits, 0, keepdims=True))
    stats_ref[1:2, :] = totals * jnp.exp(before - highest) + jnp.sum(
        jnp.exp(logits - highest), 0, keepdims=True
    )
    stats_ref[0:1, :] = highest
    stats_ref[2:3, :] = stats_ref[2:3, :] + jnp.sum(
        jnp.where(matches, logits, 0.0), 0, keepdims=True
    )


def head_stats(chosen_across, target_row, low):
    vocab_here, model = low.shape
    slots = chosen_across.shape[1]
    block = row_block(vocab_here, 1024)
    return pl.pallas_call(
        head_stats_kernel,
        grid=(vocab_here // block,),
        in_specs=[
            whole_block(chosen_across.shape),
            whole_block((1, slots)),
            pl.BlockSpec((block, model), lambda i: (i, 0)),
        ],
        out_specs=whole_block((8, slots)),
        out_shape=jax.ShapeDtypeStruct((8, slots), jnp.float32),
        compiler_params=vmem(40),
        cost_estimate=small_cost(
            flops=2 * slots * vocab_here * model,
            bytes_accessed=2 * vocab_here * model,
            transcendentals=slots * vocab_here,
        ),
    )(chosen_across, target_row, low)


def head_rows_kernel(chosen_ref, target_ref, logsum_ref, low_ref, grad_ref):
    step = pl.program_id(0)
    rows = low_ref.shape[0]
    low = low_ref[...]
    logits = matmul_right(chosen_ref[...], low)
    places = lax.broadcasted_iota(jnp.int32, logits.shape, 1) + step * rows
    target = target_ref[...]
    matches = jnp.where(places == target, 1.0, 0.0)
    grads = jnp.where(target != DEAD, jnp.exp(logits - logsum_ref[...]) - matches, 0.0)
    before = jnp.where(step == 0, 0.0, grad_ref[...])
    grad_ref[...] = before + matmul(bfloat(grads), low)


def head_rows(chosen, target_column, logsum_column, low):
    vocab_here, model = low.shape
    slots = chosen.shape[0]
    block = row_block(vocab_here, 1024)
    return pl.pallas_call(
        head_rows_kernel,
        grid=(vocab_here // block,),
        in_specs=[
            whole_block(chosen.shape),
            whole_block((slots, 1)),
            whole_block((slots, 1)),
            pl.BlockSpec((block, model), lambda i: (i, 0)),
        ],
        out_specs=whole_block((slots, model)),
        out_shape=jax.ShapeDtypeStruct((slots, model), jnp.float32),
        compiler_params=vmem(40),
        cost_estimate=small_cost(
            flops=4 * slots * vocab_here * model,
            bytes_accessed=2 * vocab_here * model,
            transcendentals=slots * vocab_here,
        ),
    )(chosen, target_column, logsum_column, low)


def head_table_kernel(first, chosen_ref, across_ref, target_ref, logsum_ref, low_ref, *refs):
    step = pl.program_id(0) + first
    grad_ref = refs[-1]
    rows = low_ref.shape[0]
    logits = matmul(low_ref[...], across_ref[...])
    places = lax.broadcasted_iota(jnp.int32, logits.shape, 0) + step * rows
    target = target_ref[...]
    matches = jnp.where(places == target, 1.0, 0.0)
    grads = jnp.where(target != DEAD, jnp.exp(logits - logsum_ref[...]) - matches, 0.0)
    grad_ref[...] = matmul(bfloat(grads), chosen_ref[...])


def head_table(chosen, chosen_across, target_row, logsum_row, low, grads, index, count):
    vocab_here, model = low.shape
    slots = chosen.shape[0]
    block = row_block(vocab_here, 1024)
    steps = vocab_here // block
    first, last = index * steps // count, (index + 1) * steps // count
    rows = pl.BlockSpec((block, model), lambda i: (i + first, 0))
    return pl.pallas_call(
        functools.partial(head_table_kernel, first),
        grid=(last - first,),
        in_specs=[
            whole_block(chosen.shape),
            whole_block(chosen_across.shape),
            whole_block((1, slots)),
            whole_block((1, slots)),
            rows,
        ]
        + ([] if grads is None else [pl.BlockSpec(memory_space=pl.ANY)]),
        out_specs=rows,
        out_shape=jax.ShapeDtypeStruct(low.shape, jnp.float32),
        input_output_aliases={} if grads is None else {5: 0},
        compiler_params=vmem(48),
        cost_estimate=small_cost(
            flops=4 * slots * vocab_here * model // count,
            bytes_accessed=6 * vocab_here * model // count,
            transcendentals=slots * vocab_here // count,
        ),
    )(*((chosen, chosen_across, target_row, logsum_row, low) + (() if grads is None else (grads,))))


def table_sums_kernel(first, place_ref, starts_ref, ids_ref, order_ref, head_ref, stat_ref, *refs):
    pieces = refs[:8]
    grad_ref, rows_ref, sums_ref, wide_ref = refs[-4:]
    step = pl.program_id(0) + first
    rows, model = head_ref.shape
    room = pieces[0].shape[1]

    @pl.when(pl.program_id(0) == 0)
    def _():
        for side in range(2):
            section = place_ref[1] if side == 0 else 1 - place_ref[1]
            for k in range(4):
                for z in range(4):
                    block = (4 * section + z) * 4 + (place_ref[0] ^ k)
                    row = pl.multiple_of(block * room, 16)
                    wide_ref[pl.ds(row, room), :] = single(pieces[4 * side + k][z])
        sums_ref[...] = jnp.zeros_like(sums_ref)

    grad_ref[...] = head_ref[...]
    start, end = starts_ref[step], starts_ref[step + 1]

    @pl.loop(0, (end - start + 3) // 4)
    def _(i):
        places, values = [], []
        for k in range(4):
            j = jnp.minimum(start + 4 * i + k, end - 1)
            row = wide_ref[pl.ds(order_ref[j], 1), :]
            values.append(jnp.where(start + 4 * i + k < end, row, 0.0))
            places.append(pl.ds(ids_ref[j] - step * rows, 1))
        for place, row in zip(places, values):
            grad_ref[place, :] = grad_ref[place, :] + row

    stats = stat_ref[...]
    columns = jnp.zeros((8, model), jnp.float32)
    scaled = jnp.zeros((8, model), jnp.float32)
    for k in range(rows // LANES):
        part = grad_ref[k * LANES : (k + 1) * LANES, :]
        square = part * part
        mean = jnp.sum(square + SQUARE_EPS, -1, keepdims=True) * (1.0 / model)
        stat = jnp.transpose(jnp.broadcast_to(stats[k : k + 1, :], (LANES, LANES)))
        new = DECAY * stat + (1.0 - DECAY) * mean
        rows_ref[k : k + 1, :] = jnp.transpose(new)[0:1, :]
        columns = columns + jnp.sum((square + SQUARE_EPS).reshape(LANES // 8, 8, model), 0)
        ratio = square * (1.0 / new[:, 0:1])
        scaled = scaled + jnp.sum(ratio.reshape(LANES // 8, 8, model), 0)
    sums_ref[0:8, :] = sums_ref[0:8, :] + columns
    sums_ref[8:16, :] = sums_ref[8:16, :] + scaled


def table_sums(starts, ids, order, pieces, head, row_stat, block, earlier, index, count):
    vocab_here, model = head.shape
    steps = vocab_here // block
    first, last = index * steps // count, (index + 1) * steps // count
    rows = pl.BlockSpec((block, model), lambda i, *_: (i + first, 0))
    stats = pl.BlockSpec((block // LANES, LANES), lambda i, *_: (i + first, 0))
    kept = [] if earlier is None else [pl.BlockSpec(memory_space=pl.ANY)] * 2
    return pl.pallas_call(
        functools.partial(table_sums_kernel, first),
        grid_spec=pltpu.PrefetchScalarGridSpec(
            num_scalar_prefetch=4,
            grid=(last - first,),
            in_specs=[rows, stats]
            + [
                pl.BlockSpec(piece.shape, lambda *_: (0, 0, 0), pipeline_mode=pl.Buffered(1))
                for piece in pieces
            ]
            + kept,
            out_specs=[rows, stats, pl.BlockSpec((16, model), lambda *_: (0, 0))],
            scratch_shapes=[pltpu.VMEM((32 * pieces[0].shape[1], model), jnp.float32)],
        ),
        out_shape=[
            jax.ShapeDtypeStruct(head.shape, jnp.float32),
            jax.ShapeDtypeStruct((vocab_here // LANES, LANES), jnp.float32),
            jax.ShapeDtypeStruct((16, model), jnp.float32),
        ],
        input_output_aliases={} if earlier is None else {14: 0, 15: 1},
        compiler_params=vmem(56),
        cost_estimate=small_cost(
            flops=8 * vocab_here * model // count,
            bytes_accessed=8 * vocab_here * model // count,
            transcendentals=0,
        ),
    )(
        jnp.stack([lax.axis_index("ctx"), lax.axis_index("section")]),
        starts,
        ids,
        order,
        head,
        row_stat.reshape(-1, LANES),
        *pieces,
        *(earlier or ()),
    )


def gelu_slope(values):
    factor = (2.0 / jnp.pi) ** 0.5
    inner = jnp.tanh(factor * (values + 0.044715 * values * values * values))
    slope = factor * (1.0 + 3.0 * 0.044715 * values * values)
    return 0.5 * (1.0 + inner) + 0.5 * values * (1.0 - inner * inner) * slope


def put_together(c, step, pieces, up_ref, down_ref):
    model = up_ref.shape[0]
    columns, packed = pieces[0].shape[:2]
    part, half = model // (8 * columns), packed // 2
    for k in range(4):
        for z in range(2 * columns):
            piece = pieces[2 * k + z // columns]
            rows = pl.ds(pl.multiple_of((4 * z + (c ^ k)) * part, 16), part)
            place = pl.ds(pl.multiple_of(step * part, 16), part)
            up_ref[rows, :] = piece[z % columns, place, :]
    for side in range(2):

        @pl.when(step == side)
        def _():
            for k in range(4):
                for z in range(columns):
                    rows = pl.ds(pl.multiple_of((4 * z + (c ^ k)) * half, 16), half)
                    down_ref[rows, :] = pieces[2 * k + side][z, half : 2 * half, :]


def half_specs(hidden):
    if not isinstance(hidden, tuple):
        grid = hidden.reshape((4, 4) + hidden.shape[1:])
        shape = (2, None) + hidden.shape[1:]
        specs = [
            pl.BlockSpec(shape, lambda *_, k=k, side=side: (side, k, 0, 0))
            for k in range(4)
            for side in range(2)
        ]
        return jnp.zeros(1, jnp.int32), [grid] * 8, specs
    arrays, specs = [], []
    for piece in hidden:
        for side in range(2):
            array = piece[side] if isinstance(piece, tuple) else piece
            shape = (2,) + array.shape[1:]
            place = 0 if isinstance(piece, tuple) else side
            arrays.append(array)
            specs.append(pl.BlockSpec(shape, lambda *_, place=place: (place, 0, 0)))
    return lax.axis_index("ctx").reshape(1), arrays, specs


def hidden_kernel(place_ref, both_ref, *refs):
    *pieces, upper_ref, partial_ref, up_ref, down_ref = refs
    step = pl.program_id(0)
    put_together(place_ref[0], step, pieces, up_ref, down_ref)
    upper = matmul(both_ref[...], up_ref[...])
    upper_ref[...] = upper
    before = jnp.where(step == 0, 0.0, partial_ref[...])
    partial_ref[...] = before + matmul(bfloat(gelu_tanh(upper)), down_ref[...])


def hidden_forward(both, hidden):
    rows, model = both.shape
    blocks = lax.axis_size("dp") * lax.axis_size("ctx")
    if not by_fours():
        up, down = hidden_weights(hidden)
        upper = matmul(both, up)
        return upper, matmul(bfloat(gelu_tanh(upper)), down)
    packed = (hidden[0] if isinstance(hidden, tuple) else hidden).shape[1]
    size = blocks * packed * model
    steps = size // (2 * model * model)
    square = pltpu.VMEM((model, model), jnp.bfloat16)
    place, arrays, specs = half_specs(hidden)
    return pl.pallas_call(
        hidden_kernel,
        grid_spec=pltpu.PrefetchScalarGridSpec(
            num_scalar_prefetch=1,
            grid=(steps,),
            in_specs=[whole_block(both.shape)] + specs,
            out_specs=[pl.BlockSpec((rows, model), lambda j, _: (0, j)), whole_block(both.shape)],
            scratch_shapes=[square, square],
        ),
        out_shape=[
            jax.ShapeDtypeStruct((rows, steps * model), jnp.float32),
            jax.ShapeDtypeStruct((rows, model), jnp.float32),
        ],
        compiler_params=vmem(48),
        cost_estimate=small_cost(
            flops=2 * rows * size,
            bytes_accessed=2 * size + 8 * rows * steps * model,
            transcendentals=rows * steps * model,
        ),
    )(place, both, *arrays)


def hidden_back_kernel(place_ref, both_ref, upper_ref, grad_ref, *refs):
    *pieces, partial_ref, grads_ref, up_ref, down_ref = refs
    step = pl.program_id(0)
    model = both_ref.shape[1]
    blocks, half = grads_ref.shape[0], grads_ref.shape[1] // 2
    rows, per_step = model // blocks, model // half
    put_together(place_ref[0], step, pieces, up_ref, down_ref)
    both, upper, grad = both_ref[...], upper_ref[...], grad_ref[...]
    active = bfloat(gelu_tanh(upper))
    grad_upper = bfloat(matmul_right(grad, down_ref[...]) * gelu_slope(upper))
    before = jnp.where(step == 0, 0.0, partial_ref[...])
    partial_ref[...] = before + matmul_right(grad_upper, up_ref[...])
    grad_up = bfloat(matmul_left(both, grad_upper)).reshape(blocks, rows, model)
    grads_ref[:, pl.ds(pl.multiple_of(step * rows, 16), rows), :] = grad_up
    grad_down = bfloat(matmul_left(active, grad)).reshape(per_step, half, model)
    grads_ref[pl.ds(step * per_step, per_step), half : 2 * half, :] = grad_down


def hidden_backward(both, upper, grad_both, hidden):
    rows, model = both.shape
    blocks = lax.axis_size("dp") * lax.axis_size("ctx")
    if not by_fours():
        up, down = hidden_weights(hidden)
        active = bfloat(gelu_tanh(upper))
        grad_upper = bfloat(matmul_right(grad_both, down) * gelu_slope(upper))
        grad_up, grad_down = matmul_left(both, grad_upper), matmul_left(active, grad_both)
        parts = [
            grad_up[:, k : k + model].reshape(blocks, -1, model)
            for k in range(0, grad_up.shape[1], model)
        ]
        packed = jnp.concatenate(parts + [grad_down.reshape(blocks, -1, model)], 1)
        return matmul_right(grad_upper, up), bfloat(packed)
    packed = (hidden[0] if isinstance(hidden, tuple) else hidden).shape[1]
    size = blocks * packed * model
    steps = size // (2 * model * model)
    square = pltpu.VMEM((model, model), jnp.bfloat16)
    grads = (blocks, packed, model)
    place, arrays, specs = half_specs(hidden)
    return pl.pallas_call(
        hidden_back_kernel,
        grid_spec=pltpu.PrefetchScalarGridSpec(
            num_scalar_prefetch=1,
            grid=(steps,),
            in_specs=[
                whole_block(both.shape),
                pl.BlockSpec((rows, model), lambda j, _: (0, j)),
                whole_block(both.shape),
            ]
            + specs,
            out_specs=[whole_block(both.shape), whole_block(grads)],
            scratch_shapes=[square, square],
        ),
        out_shape=[
            jax.ShapeDtypeStruct((rows, model), jnp.float32),
            jax.ShapeDtypeStruct(grads, jnp.bfloat16),
        ],
        compiler_params=vmem(56),
        cost_estimate=small_cost(
            flops=4 * rows * size,
            bytes_accessed=4 * size + 4 * rows * steps * model,
            transcendentals=2 * rows * steps * model,
        ),
    )(place, both, upper, grad_both, *arrays)


def hidden_weights(hidden):
    blocks, packed, model = hidden.shape
    part = model // blocks
    parts = [hidden[:, k : k + part].reshape(model, model) for k in range(0, packed // 2, part)]
    return jnp.concatenate(parts, 1), hidden[:, packed // 2 :].reshape(-1, model)


def both_rows(values):
    return jnp.concatenate([values, swap(values)])


def own_rows(partial, pieces=1):
    rows = partial.shape[0] // 2
    return partial[:rows] + swap(partial[rows:])


def factored_sums(weight, gradient, row_stat):
    square = gradient * gradient + SQUARE_EPS
    rows_new = DECAY * row_stat + (1.0 - DECAY) * jnp.mean(square, -1)
    columns = jnp.sum(square, 0)
    scaled = jnp.sum(gradient * gradient / rows_new[:, None], 0)
    return rows_new, columns, scaled, jnp.sum(rows_new), jnp.sum(weight * weight)


def factored_new(weight, gradient, rows_new, col_stat, sums, row_count):
    columns, scaled, rows_sum, weight_sum = sums
    entries = row_count * weight.shape[1]
    cols_new = DECAY * col_stat + (1.0 - DECAY) * columns / row_count
    mean_rows = rows_sum / row_count
    update_sum = mean_rows * jnp.sum(scaled / cols_new)
    clipping = jnp.maximum(1.0, jnp.sqrt(update_sum / entries))
    size = jnp.maximum(SCALE_FLOOR, jnp.sqrt(weight_sum / entries))
    update = gradient * lax.rsqrt(rows_new[:, None] * cols_new[None, :] / mean_rows)
    return cols_new, weight - RELATIVE_RATE * size * (update / clipping)


def distinct_slots(ids, vocab_here):
    count = ids.shape[1]
    shard = ids // vocab_here
    earlier = jnp.arange(count)[None, :] < jnp.arange(count)[:, None]
    same = ids[:, :, None] == ids[:, None, :]
    first = ~jnp.any(same & earlier, -1)
    mates = (shard[:, :, None] == shard[:, None, :]) & first[:, None, :] & earlier
    rank = jnp.sum(mates.astype(jnp.int32), -1)
    slot = jnp.sum(jnp.where(same & first[:, None, :], rank[:, None, :], 0), -1)
    return slot, shard


def asked_ids(local, slot, here, room):
    places = jnp.arange(room, dtype=jnp.int32)[None, :, None]
    matches = (slot[:, None, :] == places) & here[:, None, :]
    return jnp.min(jnp.where(matches, local[:, None, :], 1 << 30), -1)


def attention_sum_kernel(kept0_ref, sent0_ref, kept1_ref, sent1_ref, out_ref):
    part = kept0_ref.shape[1]
    out_ref[:, :part] = bfloat(single(kept0_ref[...]) + single(sent0_ref[...]))
    out_ref[:, part:] = bfloat(single(kept1_ref[...]) + single(sent1_ref[...]))


def attention_sums(grads, blocks):
    wide = grads[0].shape[1]
    grads = [grad.reshape(blocks, -1, wide) for grad in grads]
    part = grads[0].shape[1]
    if part % 16:
        total = [bfloat(single(grads[k]) + single(grads[k + 1])) for k in (0, 2)]
        return jnp.concatenate(total, 1)
    step = row_block(blocks, 4)
    return pl.pallas_call(
        attention_sum_kernel,
        grid=(blocks // step,),
        in_specs=[pl.BlockSpec((step, part, wide), lambda i: (i, 0, 0))] * 4,
        out_specs=pl.BlockSpec((step, 2 * part, wide), lambda i: (i, 0, 0)),
        out_shape=jax.ShapeDtypeStruct((blocks, 2 * part, wide), jnp.bfloat16),
        compiler_params=vmem(24),
        cost_estimate=small_cost(
            flops=0, bytes_accessed=8 * grads[0].size, transcendentals=0
        ),
    )(*grads)


def picked_kernel(ids_ref, table_ref, out_ref, rows_ref, sem):
    count = rows_ref.shape[0]

    @pl.loop(0, count // 8)
    def _(i):
        for k in range(8):
            row = table_ref.at[pl.ds(ids_ref[8 * i + k], 1), :]
            pltpu.make_async_copy(row, rows_ref.at[pl.ds(8 * i + k, 1), :], sem).start()

    pltpu.make_async_copy(table_ref.at[pl.ds(0, count), :], rows_ref, sem).wait()
    out_ref[...] = bfloat(rows_ref[...])


def picked_rows(ids, table):
    shape = (ids.shape[0], table.shape[1])
    return pl.pallas_call(
        picked_kernel,
        grid_spec=pltpu.PrefetchScalarGridSpec(
            num_scalar_prefetch=1,
            grid=(1,),
            in_specs=[pl.BlockSpec(memory_space=pl.ANY)],
            out_specs=whole_block(shape),
            scratch_shapes=[pltpu.VMEM(shape, jnp.float32), pltpu.SemaphoreType.DMA],
        ),
        out_shape=jax.ShapeDtypeStruct(shape, jnp.bfloat16),
        compiler_params=vmem(24),
        cost_estimate=small_cost(
            flops=0, bytes_accessed=4 * shape[0] * shape[1], transcendentals=0
        ),
    )(ids, table)


def spilled_inside(ids, slot, room, vocab_here):
    local = ids - lax.axis_index("dp") * vocab_here
    return local, (local >= 0) & (local < vocab_here) & (slot >= room)


def spilled_rows(token_ids, slot, room, table):
    ids = at(token_ids, lax.axis_index("section"), 0)
    local, inside = spilled_inside(ids, slot, room, table.shape[0])
    rows = jnp.take(table, jnp.clip(local, 0, table.shape[0] - 1), axis=0)
    rows = jnp.where(inside[..., None], bfloat(rows), 0)
    return single(lax.psum_scatter(rows, "dp", scatter_dimension=0))


def spilled_grads(token_ids, slot, room, grad_start, vocab_here):
    ids = at(token_ids, lax.axis_index("section"), 0)
    local, inside = spilled_inside(ids, slot, room, vocab_here)
    column = lax.all_gather(grad_start, "dp")
    total = jax.ops.segment_sum(
        single(column.reshape(-1, column.shape[-1])),
        jnp.where(inside, local, vocab_here).reshape(-1),
        num_segments=vocab_here,
    )
    return single(lax.psum(bfloat(total), ("section", "ctx")))


def put_rows(ref, row, vector):
    for k in range(vector.shape[1] // LANES):
        ref[row + k : row + k + 1, :] = vector[:, k * LANES : (k + 1) * LANES]


def got_rows(ref, row, width):
    count = width // LANES
    return jnp.concatenate([ref[row + k : row + k + 1, :] for k in range(count)], 1)


def total(values):
    return jnp.sum(jnp.sum(values, 0, keepdims=True), 1, keepdims=True)


def pair(first, second):
    lanes = lax.broadcasted_iota(jnp.int32, (first.shape[0], LANES), 1)
    return jnp.where(lanes == 0, first, jnp.where(lanes == 1, second, 0.0))


def sum_rows(widths):
    starts = [0]
    for width in widths:
        starts.append(starts[-1] + 2 * width // LANES)
    scalars = -(-starts[-1] // 8) * 8
    return starts, scalars, scalars + 8


def layer_sums_kernel(*refs):
    grads, weights, stats = refs[:5], refs[5:10], refs[10:15]
    first_ref, second_ref, table_rows_ref, square_ref = refs[15:19]
    packed_ref, *new_refs = refs[19:]
    model = first_ref.shape[1]
    starts, scalars, table = sum_rows([ref.shape[1] for ref in grads[:4]])
    packed_ref[...] = jnp.zeros_like(packed_ref)
    for k in range(4):
        grad, weight = grads[k][...], weights[k][...]
        square = grad * grad
        full = square + SQUARE_EPS
        mean = jnp.sum(full, -1, keepdims=True) * (1.0 / grad.shape[1])
        new = DECAY * stats[k][...] + (1.0 - DECAY) * mean
        new_refs[k][...] = new
        count = grad.shape[1] // LANES
        put_rows(packed_ref, starts[k], jnp.sum(full, 0, keepdims=True))
        scaled = jnp.sum(square * (1.0 / new), 0, keepdims=True)
        put_rows(packed_ref, starts[k] + count, scaled)
        packed_ref[scalars + k : scalars + k + 1, :] = pair(total(new), total(weight * weight))
    grad, weight = grads[4][...], weights[4][...]
    new = DECAY * stats[4][...] + (1.0 - DECAY) * (grad * grad + SQUARE_EPS)
    new_refs[4][...] = new
    update = grad * lax.rsqrt(new)
    packed_ref[scalars + 4 : scalars + 8, :] = pair(
        jnp.sum(weight * weight, 1, keepdims=True), jnp.sum(update * update, 1, keepdims=True)
    )
    sums = first_ref[...] + second_ref[...]
    put_rows(packed_ref, table, jnp.sum(sums[0:8], 0, keepdims=True))
    put_rows(packed_ref, table + model // LANES, jnp.sum(sums[8:16], 0, keepdims=True))
    place = table + 2 * model // LANES
    packed_ref[place : place + 1, :] = pair(total(table_rows_ref[...]), total(square_ref[...]))


def layer_sums(grads, weights, stats, sums_first, sums_second, table_rows_new, squares):
    shapes = [stat.shape for stat in stats]
    _, _, table = sum_rows([grad.shape[1] for grad in grads[:4]])
    height = table + -(-(2 * sums_first.shape[1] // LANES + 1) // 8) * 8
    return pl.pallas_call(
        layer_sums_kernel,
        out_shape=[jax.ShapeDtypeStruct((height, LANES), jnp.float32)]
        + [jax.ShapeDtypeStruct(shape, jnp.float32) for shape in shapes],
        compiler_params=vmem(40),
        cost_estimate=small_cost(flops=0, bytes_accessed=1 << 22, transcendentals=0),
    )(*grads, *weights, *stats, sums_first, sums_second, table_rows_new, squares)


def factored_sizes(ref, start, scalar, col_stat, row_count):
    width = col_stat.shape[1]
    columns = got_rows(ref, start, width)
    scaled = got_rows(ref, start + width // LANES, width)
    rows_sum, weight_sum = ref[scalar : scalar + 1, 0:1], ref[scalar : scalar + 1, 1:2]
    new = DECAY * col_stat + (1.0 - DECAY) * columns * (1.0 / row_count)
    mean_rows = rows_sum * (1.0 / row_count)
    entries = row_count * width
    update_sum = mean_rows * jnp.sum(scaled / new, 1, keepdims=True)
    clipping = jnp.maximum(1.0, jnp.sqrt(update_sum * (1.0 / entries)))
    size = jnp.maximum(SCALE_FLOOR, jnp.sqrt(weight_sum * (1.0 / entries)))
    return new, mean_rows, RELATIVE_RATE * size / clipping


def layer_new_kernel(counts, totals_ref, *refs):
    grads, weights, rows, cols = refs[:5], refs[5:10], refs[10:15], refs[15:19]
    new_refs, col_refs = refs[19:24], refs[24:28]
    starts, scalars, _ = sum_rows([ref.shape[1] for ref in grads[:4]])
    for k in range(4):
        cols_new, mean_rows, rate = factored_sizes(
            totals_ref, starts[k], scalars + k, cols[k][...], counts[k]
        )
        col_refs[k][...] = cols_new
        scale = lax.rsqrt(rows[k][...] * cols_new / mean_rows)
        new_refs[k][...] = weights[k][...] - rate * (grads[k][...] * scale)
    model = counts[4]
    squares = totals_ref[scalars + 4 : scalars + 8, 0:1]
    updates = totals_ref[scalars + 4 : scalars + 8, 1:2]
    clipping = jnp.maximum(1.0, jnp.sqrt(updates * (1.0 / model)))
    size = jnp.maximum(SCALE_FLOOR, jnp.sqrt(squares * (1.0 / model)))
    update = grads[4][...] * lax.rsqrt(rows[4][...])
    new_refs[4][...] = weights[4][...] - RELATIVE_RATE * size / clipping * update


def layer_new(totals, grads, weights, rows, cols, counts):
    outs = [grad.shape for grad in grads] + [col.shape for col in cols]
    return pl.pallas_call(
        functools.partial(layer_new_kernel, counts),
        out_shape=[jax.ShapeDtypeStruct(shape, jnp.float32) for shape in outs],
        compiler_params=vmem(40),
        cost_estimate=small_cost(flops=0, bytes_accessed=1 << 22, transcendentals=0),
    )(totals, *grads, *weights, *rows, *cols)


def table_new_kernel(start, row_count, totals_ref, table_ref, grad_ref, rows_ref, cols_ref, *refs):
    new_ref, col_ref = refs
    scalar = start + 2 * cols_ref.shape[1] // LANES
    cols_new, mean_rows, rate = factored_sizes(totals_ref, start, scalar, cols_ref[...], row_count)
    col_ref[...] = cols_new
    across = rate * lax.rsqrt(cols_new)
    down = lax.rsqrt(rows_ref[...] / mean_rows)
    for k in range(rows_ref.shape[0]):
        place = slice(k * LANES, (k + 1) * LANES)
        scale = jnp.transpose(jnp.broadcast_to(down[k : k + 1, :], (LANES, LANES)))[:, 0:1]
        new_ref[place, :] = table_ref[place, :] - grad_ref[place, :] * scale * across


def table_new(totals, start, table, grad, rows_new, cols, row_count):
    vocab_here, model = table.shape
    block = row_block(vocab_here, 1024)
    rows = pl.BlockSpec((block, model), lambda i: (i, 0))
    return pl.pallas_call(
        functools.partial(table_new_kernel, start, row_count),
        grid=(vocab_here // block,),
        in_specs=[
            whole_block(totals.shape),
            rows,
            rows,
            pl.BlockSpec((block // LANES, LANES), lambda i: (i, 0)),
            whole_block(cols.shape),
        ],
        out_specs=[rows, whole_block(cols.shape)],
        out_shape=[
            jax.ShapeDtypeStruct(table.shape, jnp.float32),
            jax.ShapeDtypeStruct(cols.shape, jnp.float32),
        ],
        compiler_params=vmem(48),
        cost_estimate=small_cost(
            flops=4 * vocab_here * model,
            bytes_accessed=12 * vocab_here * model,
            transcendentals=0,
        ),
    )(totals, table, grad, rows_new, cols)


def body(
    token_ids,
    doc_lengths,
    picks,
    targets,
    table,
    table_rows,
    table_cols,
    attention_in,
    attention_in_rows,
    attention_in_cols,
    attention_out,
    attention_out_rows,
    attention_out_cols,
    hidden_in,
    hidden_in_rows,
    hidden_in_cols,
    hidden_out,
    hidden_out_rows,
    hidden_out_cols,
    gains,
    gains_stat,
):
    section = lax.axis_index("section")
    first = section == 0
    z, c = lax.axis_index("dp"), lax.axis_index("ctx")
    z_count, c_count = lax.axis_size("dp"), lax.axis_size("ctx")
    blocks = z_count * c_count
    model = table.shape[1]
    part = attention_in.shape[1]
    units = hidden_in.shape[2]
    half = units // (2 * blocks)
    wide = attention_in.shape[2]
    local_len = token_ids.shape[2]
    slots = picks.shape[2]
    vocab_here = table.shape[0]
    vocab_base = z * vocab_here

    low_in = bfloat(attention_in[0])
    low_out = jnp.concatenate(
        [bfloat(attention_out[0]), bfloat(gains[0]).T, jnp.zeros((part, wide - model - 4), jnp.bfloat16)], 1
    )
    barrier = lax.optimization_barrier
    at_p = jnp.concatenate(
        mine_first(
            jnp.where(first, low_in, low_out), swap(jnp.where(first, low_out, low_in))
        )
    )
    at_p, hidden_in_now, hidden_out_now = barrier((at_p, hidden_in, hidden_out))
    at_z = column_pieces(at_p)
    low_up = bfloat(hidden_in_now[0]).reshape(part, blocks, 2, half)
    low_down = bfloat(hidden_out_now[0])

    def unit_half(index):
        up = at(low_up, index, 2).reshape(part, -1, model)
        down = lax.dynamic_slice_in_dim(low_down, index * half, half, 0)
        return jnp.concatenate([up[:, k] for k in range(up.shape[1])] + [down])

    hid_p0, hid_p1 = mine_first(unit_half(section), swap(unit_half(1 - section)))

    room = local_len * 3 // 128 * 16

    hidden_w0 = lax.all_gather(hid_p0, BLOCKS, axis=0)

    if by_fours():
        slot, shard = distinct_slots(at(token_ids, section, 0), vocab_here)
        asked = asked_ids(at(token_ids, section, 0) - vocab_base, slot, shard == z, room)
        spilled = jnp.max(slot) >= room
        wanted = jnp.minimum(asked, vocab_here - 1).reshape(-1)
        place = at(jnp.where(slot < room, shard * room + slot, -1), z, 0)
        placed = bfloat(
            single(place[:, None] == jnp.arange(z_count * room, dtype=jnp.int32)[None, :])
        )
        notes = [asked.reshape(-1), spilled.astype(jnp.int32)[None], targets.reshape(-1)]
        notes = jnp.concatenate(notes)
        notes = jnp.stack(mine_first(notes, swap(notes)))
        x, y = plane_bits()
        beside = cross(notes, "ctx", 1)
        notes = jnp.stack([jnp.where(x == 0, notes, beside), jnp.where(x == 0, beside, notes)])
        above = cross(notes, "ctx", 2)
        notes = jnp.concatenate([jnp.where(y == 0, notes, above), jnp.where(y == 0, above, notes)])
        looked = picked_rows(after(wanted, at_p), table).reshape(z_count, room, model)
    else:
        my_ids = at(token_ids, section, 0) - vocab_base
        inside = (my_ids >= 0) & (my_ids < vocab_here)
        looked = jnp.take(table, jnp.clip(my_ids, 0, vocab_here - 1), axis=0)
        looked = jnp.where(inside[..., None], bfloat(looked), 0)
        notes = []

    at_z, hid_p1, looked, notes, table_now = barrier((at_z, hid_p1, looked, notes, table))
    at_c = column_join(at_p, at_z)
    at_n = plane_near(at_c)
    start_pieces = row_pieces(looked)
    low_first, square_first = lowered(table_now, None, 0, 3)
    at_n, start_pieces, low_first, hid_p1 = barrier((at_n, start_pieces, low_first, hid_p1))
    at_f = plane_far(at_n)
    hid_z1 = column_pieces(hid_p1)
    table_low, square_second = lowered(table, low_first, 1, 3)
    at_f, table_low, at_c = barrier((at_f, table_low, at_c))
    at_w = plane_list(at_c, at_n, at_f)
    if by_fours():
        at_w = jnp.concatenate(at_w)
    at_o = swap(at_w)
    table_low, square_third = lowered(table, table_low, 2, 3)
    at_o, table_low = barrier((at_o, table_low))
    if by_fours():
        target_notes = notes[:, 0, asked.size + 1 :]
        asked_all = notes[..., : asked.size].reshape(c_count, 2, z_count, room)
        local = jnp.minimum(asked_all.transpose(1, 2, 0, 3).reshape(-1), vocab_here)
        order = jnp.arange(local.shape[0], dtype=jnp.int32)
        local, order = lax.sort((local, order), num_keys=1)
        block = row_block(vocab_here, 1024)
        edges = jnp.arange(vocab_here // block + 1, dtype=jnp.int32) * block
        starts = jnp.sum((local[None, :] < edges[:, None]).astype(jnp.int32), 1)
    else:
        local = order = starts = notes
    in0, out0, gains0 = attention_weights(at_w, at_o, model, 0)
    if by_fours():
        spilled = jnp.max(notes[..., asked.size]) > 0
        found = column_join(at(looked, z, 0), start_pieces)
        start = matmul(placed, found.reshape(-1, model))
        start = start + lax.cond(
            spilled,
            lambda: spilled_rows(token_ids, slot, room, table),
            lambda: jnp.zeros_like(start),
        )
    else:
        target_notes = lax.all_gather(targets, "ctx")
        start = row_sum(looked, start_pieces)
    lengths = at(doc_lengths, section, 0)[0]
    my_picks = at(picks, section, 0)[0]

    places = c * local_len + jnp.arange(local_len, dtype=jnp.int32)
    reach = earlier_count(local_len)
    key_places = (c - reach) * local_len + jnp.arange((reach + 1) * local_len, dtype=jnp.int32)
    bias = pair_bias(lengths, places, key_places)
    pick_bias = pair_bias(lengths, c * local_len + jnp.maximum(my_picks, 0), key_places)
    onehot = (my_picks[:, None] == jnp.arange(local_len, dtype=jnp.int32)[None, :]).astype(
        jnp.bfloat16
    )

    normed0 = bfloat(layer_norm(start, gains0[0], gains0[1]))
    mixed_in = matmul(normed0, in0)
    query0 = bfloat(mixed_in[:, :model] * HD ** (-0.5))
    keyval0, query0, local, order, starts = barrier(
        (bfloat(mixed_in[:, model:]), query0, local, order, starts)
    )
    keyval0, query0, hid_z1 = barrier((key_rows(keyval0), query0, hid_z1))
    hid_c1 = column_join(hid_p1, hid_z1)
    hid_n1 = plane_near_half(hid_c1, 0)
    attended0 = attend(query0, keyval0, bias)
    mixed0 = start + matmul(attended0, out0)
    normed_two0 = bfloat(layer_norm(mixed0, gains0[2], gains0[3]))
    hid_n1, mixed0, normed_two0 = barrier((hid_n1, mixed0, normed_two0))
    both0, hid_c1 = barrier((both_rows(normed_two0), hid_c1))
    hid_m1 = plane_near_half(hid_c1, 1)
    upper0, partial = hidden_forward(both0, hidden_w0)
    in1, out1, gains1 = attention_weights(at_w, at_o, model, 1)
    hid_m1, partial, in1, out1 = barrier((hid_m1, partial, in1, out1))
    hid_f1 = plane_far_half(hid_n1, hid_m1)
    result0 = mixed0 + own_rows(partial)

    inputs1_low = bfloat(result0)
    inputs1 = single(inputs1_low)
    normed1 = bfloat(layer_norm(inputs1, gains1[0], gains1[1]))
    keyval1 = bfloat(matmul(normed1, in1[:, model:]))
    picked_normed = bfloat(matmul(onehot, normed1))
    picked = matmul(onehot, inputs1_low)
    query1 = bfloat(matmul(picked_normed, in1[:, :model]) * HD ** (-0.5))
    keyval1, query1, hid_f1 = barrier((keyval1, query1, hid_f1))
    keyval1 = key_rows(keyval1)
    hidden_w1 = plane_halves(hid_c1, (hid_n1, hid_m1), hid_f1)
    all_targets = target_notes.reshape((c_count,) + targets.shape).transpose(1, 2, 0, 3).reshape(-1)
    heads1 = query1.reshape(slots, -1, HD).transpose(1, 0, 2).reshape(-1, HD)
    heads1 = jnp.concatenate([heads1, jnp.zeros_like(heads1)], 1)
    pick_bias = jnp.tile(pick_bias, (model // HD, 1))

    def side_by_side(heads):
        return heads.reshape(-1, slots, HD).transpose(1, 0, 2).reshape(slots, model)

    attended1 = side_by_side(attend(heads1, keyval1, pick_bias)[:, :HD])
    mixed1 = picked + matmul(attended1, out1)
    normed_two1 = bfloat(layer_norm(mixed1, gains1[2], gains1[3]))
    both1 = both_rows(normed_two1)
    upper1, partial = hidden_forward(both1, hidden_w1)
    result1 = mixed1 + own_rows(partial)

    chosen_mine = gather_blocks(bfloat(result1)).reshape(-1, model)
    chosen = jnp.concatenate(mine_first(chosen_mine, swap(chosen_mine)))
    live = all_targets >= 0
    local_target = jnp.where(live, all_targets - vocab_base, DEAD)
    across = chosen.T
    stats = head_stats(across, local_target[None], table_low)

    def combine(one, two):
        top = jnp.maximum(one[0], two[0])
        both = one[1] * jnp.exp(one[0] - top) + two[1] * jnp.exp(two[0] - top)
        return jnp.stack([top, both, one[2] + two[2]])

    if by_fours():
        stats = stats[:3]
        one, two, three = (cross(stats, "dp", k) for k in (1, 2, 3))
        stats = combine(combine(stats, one), combine(two, three))
    else:
        stats = lax.scan(
            lambda total, share: (combine(total, share), None),
            jnp.stack([jnp.full_like(stats[0], MASKED), 0 * stats[0], 0 * stats[0]]),
            lax.all_gather(stats, "dp"),
        )[0]
    logsum = stats[0] + jnp.log(stats[1])
    loss_sum = jnp.sum(jnp.where(live, logsum - stats[2], 0.0))
    loss_count = jnp.sum(single(live))

    def own_slots(values):
        shape = (2, z_count, c_count, slots) + values.shape[1:]
        return at(at(values.reshape(shape), section, 0), c, 1).reshape((-1,) + values.shape[1:])

    grad_chosen = head_rows(
        own_slots(chosen), own_slots(local_target)[:, None], own_slots(logsum)[:, None], table_low
    )
    grad_result1 = scatter_rows(grad_chosen.reshape(z_count, slots, model))

    def attention_grads(grad_in, grad_out, grad_gains):
        grad_out = jnp.concatenate(
            [
                bfloat(grad_out),
                bfloat(grad_gains).T,
                jnp.zeros((model, wide - model - 4), jnp.bfloat16),
            ],
            1,
        )
        grad_in = bfloat(grad_in)
        return jnp.where(first, grad_in, grad_out), jnp.where(first, grad_out, grad_in)

    low = bfloat(grad_result1)
    partial, hidden_grads1 = hidden_backward(both1, upper1, both_rows(low), hidden_w1)
    hidden1 = scattered(hidden_grads1)
    _, pull = jax.vjp(layer_norm, mixed1, gains1[2], gains1[3])
    grad_mixed1, grad_gain2, grad_shift2 = pull(own_rows(partial))
    grad_mixed1 = grad_mixed1 + grad_result1
    grad_low = bfloat(grad_mixed1)
    grad_out1 = matmul_left(attended1, grad_low)
    grad_heads = bfloat(matmul_right(grad_low, out1)).reshape(slots, -1, HD)
    grad_heads = grad_heads.transpose(1, 0, 2).reshape(-1, HD)
    grad_heads = jnp.concatenate([grad_heads, jnp.zeros_like(grad_heads)], 1)
    grad_query, grad_keyval = attend_back(heads1, keyval1, pick_bias, grad_heads)
    grad_query = side_by_side(grad_query[:, :HD])
    grad_keyval = key_rows_sum(grad_keyval, key_rows_back(grad_keyval, local_len), local_len)
    grad_in1 = jnp.concatenate(
        [matmul_left(picked_normed, grad_query), matmul_left(normed1, grad_keyval)], 1
    )
    spread = jnp.dot(
        single(onehot).T,
        jnp.concatenate([matmul_right(grad_query, in1[:, :model]), grad_mixed1], 1),
        precision=lax.Precision.HIGHEST,
    )
    grad_normed = matmul_right(grad_keyval, in1[:, model:]) + spread[:, :model]
    _, pull = jax.vjp(layer_norm, inputs1, gains1[0], gains1[1])
    grad_inputs1, grad_gain1, grad_shift1 = pull(grad_normed)
    grad_result0 = single(bfloat(grad_inputs1 + spread[:, model:]))
    grad_gains1 = jnp.stack([grad_gain1, grad_shift1, grad_gain2, grad_shift2])
    kept1, sent1 = attention_grads(grad_in1, grad_out1, grad_gains1)

    low = bfloat(grad_result0)
    partial, hidden_grads0 = hidden_backward(both0, upper0, both_rows(low), hidden_w0)
    every, wide_rows = (0, 2 * part + half), (0, 2 * part)
    partial, hidden_grads0, sent1 = barrier((own_rows(partial), hidden_grads0, swap(sent1)))
    hid_s = half_first(hidden_grads0, every) if by_fours() else ()
    _, pull = jax.vjp(layer_norm, mixed0, gains0[2], gains0[3])
    grad_mixed0, grad_gain2, grad_shift2 = pull(partial)
    grad_mixed0 = grad_mixed0 + grad_result0
    grad_low = bfloat(grad_mixed0)
    grad_out0 = matmul_left(attended0, grad_low)
    grad_query, grad_keyval = attend_back(
        query0, keyval0, bias, bfloat(matmul_right(grad_low, out0))
    )
    grad_query, grad_keyval = barrier((grad_query, grad_keyval))
    returned, hid_s = barrier((key_rows_back(grad_keyval, local_len), hid_s))
    if by_fours():
        hid_k, hid_h = half_kept(hidden_grads0, every, hid_s)
    grad_keyval = key_rows_sum(grad_keyval, returned, local_len)
    grad_mixed_in = jnp.concatenate([grad_query, grad_keyval], 1)
    grad_in0 = matmul_left(normed0, grad_mixed_in)
    _, pull = jax.vjp(layer_norm, start, gains0[0], gains0[1])
    grad_start, grad_gain1, grad_shift1 = pull(matmul_right(grad_mixed_in, in0))
    grad_start = bfloat(grad_start + grad_mixed0)
    grad_gains0 = jnp.stack([grad_gain1, grad_shift1, grad_gain2, grad_shift2])
    kept0, sent0 = attention_grads(grad_in0, grad_out0, grad_gains0)
    def owned(one, two):
        return mine_first(jnp.where(first, one, two), swap(jnp.where(first, two, one)))

    def hidden_shards(one, two):
        halves = jnp.stack(owned(one, two))
        ups = units // 2 // model
        up = halves[:, : ups * part].reshape(2, ups, part, model).transpose(2, 0, 1, 3)
        up = up.reshape(part, 2, blocks, half).transpose(0, 2, 1, 3).reshape(part, units)
        return up, halves[:, ups * part :].reshape(2 * half, model)

    def head_part(grads, index, count):
        return head_table(
            chosen, across, local_target[None], logsum[None], table_low, grads, index, count
        )

    table_square = square_first + square_second + square_third
    if by_fours():
        sent = bfloat(matmul_left(placed, grad_start)).reshape(z_count, room, model)
        sent, hid_h = barrier((sent, hid_h))
        row_z = row_pieces(sent)
        hid_t = half_send(hid_h)
        chosen = after(chosen, sent)
        grad_head = head_part(None, 0, 3)
        row_z, grad_head, hid_t, kept0, sent0 = barrier((row_z, grad_head, hid_t, kept0, sent0))
        column = column_join(at(sent, z, 0), row_z)
        near = plane_near(column)
        other, sent0 = swap((column, sent0))
        hid_v = half_column(hid_k, hid_t)
        grad_head = head_part(grad_head, 1, 3)
        near, grad_head, other, sent0, hid_v = barrier((near, grad_head, other, sent0, hid_v))
        far = plane_far(near)
        attention_both = attention_sums((kept0, sent0, kept1, sent1), blocks)
        at_s = half_first(attention_both, wide_rows)
        grad_head = head_part(grad_head, 2, 3)
        grad_head = lax.while_loop(
            lambda carry: carry[0] < spilled.astype(jnp.int32),
            lambda carry: (
                carry[0] + 1,
                carry[1] + spilled_grads(token_ids, slot, room, grad_start, vocab_here),
            ),
            (jnp.zeros((), jnp.int32), grad_head),
        )[1]
        far, grad_head, hidden1 = barrier((far, grad_head, hidden1))
        far = jnp.concatenate(far)
        others, hid_v = barrier((swap((*near, far)), hid_v))
        hid_q = row_pieces(hid_v)
        pieces = (column, *near, far, other, *others)
        parts = (starts, local, order, pieces, grad_head, table_rows, block)
        grad_table, rows_new, sums_first = table_sums(*parts, None, 0, 3)
        at_s, hid_q, grad_table, rows_new = barrier((at_s, hid_q, grad_table, rows_new))
        at_k, at_h = half_kept(attention_both, wide_rows, at_s)
        at_t = half_send(at_h)
        grad_table, rows_new, sums_second = table_sums(*parts, (grad_table, rows_new), 1, 3)
        at_t, grad_table, rows_new = barrier((at_t, grad_table, rows_new))
        at_v = half_column(at_k, at_t)
        at_q = row_pieces(at_v)
        shard_up, shard_down = hidden_shards(row_sum(hid_v, hid_q), hidden1)
        grad_table, rows_new, sums_third = table_sums(*parts, (grad_table, rows_new), 2, 3)
        sums_second = sums_second + sums_third
        at_q, grad_table, rows_new, shard_up, shard_down = barrier(
            (at_q, grad_table, rows_new, shard_up, shard_down)
        )
        attention = row_sum(at_v, at_q)
    else:
        hidden0 = scattered(hidden_grads0)
        attention_both = attention_sums((kept0, swap(sent0), kept1, sent1), blocks)
        attention = scattered(attention_both)
        column = lax.all_gather(grad_start, "dp").reshape(-1, model)
        local = jnp.where(inside, my_ids, vocab_here).reshape(-1)
        lookup_grad = jax.ops.segment_sum(single(column), local, num_segments=vocab_here)
        lookup_grad = single(lax.psum(bfloat(lookup_grad), ("section", "ctx")))
        grad_table = head_part(None, 0, 1) + lookup_grad
        table_sum = (
            *factored_sums(table, grad_table, table_rows)[:4],
            jnp.sum(table_square),
        )

    if not by_fours():
        shard_up, shard_down = hidden_shards(hidden0, hidden1)
    shard_in, shard_out = owned(attention[:part], attention[part:])
    shard_gains = shard_out[:, model : model + 4].T
    shard_out = shard_out[:, :model]

    if by_fours():
        grads = (shard_in, shard_out, shard_up, shard_down, shard_gains)
        weights = (attention_in[0], attention_out[0], hidden_in[0], hidden_out[0], gains[0])
        rows = (attention_in_rows, attention_out_rows, hidden_in_rows, hidden_out_rows)
        rows = [stat.reshape(-1, 1) for stat in rows] + [gains_stat[0]]
        sums, *rows_news = layer_sums(
            grads, weights, rows, sums_first, sums_second, rows_new, table_square
        )
        sums = summed(sums, ("dp",))
        _, _, table_start = sum_rows([grad.shape[1] for grad in grads[:4]])
        layer_part = sums[:table_start]
        layer_pieces = [cross(layer_part, "ctx", k) for k in (1, 2, 3)]
        table_news, table_cols_new = table_new(
            sums, table_start, table, grad_table, rows_new, table_cols[None], vocab_here * z_count
        )
        (one, two, three), table_cols_new = barrier((layer_pieces, table_cols_new))
        layer_totals = (layer_part + one) + (two + three)
        cols = (attention_in_cols, attention_out_cols, hidden_in_cols, hidden_out_cols)
        *news, in_cols, out_cols, up_cols, down_cols = layer_new(
            layer_totals, grads, weights, rows_news, cols, (model, model, model, units, model)
        )
        layered = []
        for k, cols_new in enumerate((in_cols, out_cols, up_cols, down_cols)):
            layered += [grads[k][None], rows_news[k].reshape(1, -1), cols_new, news[k][None]]
        return (
            loss_sum,
            loss_count,
            grad_table,
            rows_new.reshape(-1),
            table_cols_new[0],
            table_news,
            *layered,
            shard_gains[None],
            rows_news[4][None],
            news[4][None],
        )
    entries = [
        (table, grad_table, table_rows, table_cols, vocab_here * z_count),
        (attention_in[0], shard_in, attention_in_rows[0], attention_in_cols[0], model),
        (attention_out[0], shard_out, attention_out_rows[0], attention_out_cols[0], model),
        (hidden_in[0], shard_up, hidden_in_rows[0], hidden_in_cols[0], model),
        (hidden_out[0], shard_down, hidden_out_rows[0], hidden_out_cols[0], units),
    ]
    sums = [table_sum] + [factored_sums(*entry[:3]) for entry in entries[1:]]
    gain_weight = gains[0]
    gain_stat_new = DECAY * gains_stat[0] + (1.0 - DECAY) * (shard_gains * shard_gains + SQUARE_EPS)
    gain_update = shard_gains * lax.rsqrt(gain_stat_new)

    def packed(group):
        rows = []
        for item in group:
            flat = item.reshape(-1)
            if flat.shape[0] % LANES:
                flat = jnp.pad(flat, (0, LANES - flat.shape[0]))
            rows.append(flat.reshape(-1, LANES))
        return jnp.concatenate(rows), [item.shape for item in group]

    def unpacked(rows, shapes):
        items, start = [], 0
        for shape in shapes:
            size = 1
            for length in shape:
                size *= length
            count = -(-size // LANES)
            items.append(rows[start : start + count].reshape(-1)[:size].reshape(shape))
            start += count
        return items

    table_group, table_shapes = packed(sums[0][1:])
    layer_group, layer_shapes = packed(
        [item for entry in sums[1:] for item in entry[1:]]
        + [jnp.sum(gain_weight * gain_weight, -1), jnp.sum(gain_update * gain_update, -1)]
    )
    everything = summed(jnp.concatenate([table_group, layer_group]), ("dp",))
    table_totals = unpacked(everything[: table_group.shape[0]], table_shapes)
    layer_parts = unpacked(summed(everything[table_group.shape[0] :], ("ctx",)), layer_shapes)
    groups = [table_totals] + [layer_parts[4 * k : 4 * k + 4] for k in range(4)]
    gain_squares, gain_update_sums = layer_parts[16:]
    outs = []
    for (weight, gradient, _, col_stat, row_count), own, group in zip(entries, sums, groups):
        cols_new, new = factored_new(weight, gradient, own[0], col_stat, group, row_count)
        outs.append((gradient, own[0], cols_new, new))
    gain_clipping = jnp.maximum(1.0, jnp.sqrt(gain_update_sums / model))
    gain_size = jnp.maximum(SCALE_FLOOR, jnp.sqrt(gain_squares / model))
    gain_new = gain_weight - RELATIVE_RATE * gain_size[:, None] * (
        gain_update / gain_clipping[:, None]
    )
    layered = [item[None] for out in outs[1:] for item in out]
    return (
        loss_sum,
        loss_count,
        *outs[0],
        *layered,
        shard_gains[None],
        gain_stat_new[None],
        gain_new[None],
    )


def solution(mesh):
    rows = P("section", BLOCKS, None)
    row = P("section", BLOCKS)
    shared = P("section", None)
    side = P("section", None, BLOCKS)
    matrix_in = (rows, row, shared)
    matrix_out = (rows, row, shared, rows)
    placed = (
        P(None, None, "ctx"),
        P(None, "dp", None),
        P(None, "dp", "ctx"),
        P(None, None, "ctx"),
        P("dp", None),
        P("dp"),
        P(),
        *(matrix_in * 4),
        side,
        side,
    )
    return jax.shard_map(
        body,
        mesh=mesh,
        in_specs=placed,
        out_specs=(
            P(),
            P(),
            P("dp", None),
            P("dp"),
            P(),
            P("dp", None),
            *(matrix_out * 4),
            side,
            side,
            side,
        ),
        check_vma=False,
    )
```
